32 devices in a mesh: groups: 2 (over x), inputs: 16 (over z, y, core).
Axes of the slice: x: 2, y: 2, z: 4, core: 2. Of those that a mesh axis runs over, the one named last changes fastest.
Arguments:
- samples: bfloat16 [128, 548864], P(('groups', 'inputs')), parts along dimension 0, may hold values from -6 to 6
- filter_coefs: float32 [4, 8192], replicated, may hold values from -0.09375 to 0.09375
Outputs:
- visibilities: bfloat16 [4096, 64, 64], P(('groups', 'inputs')), parts along dimension 0
The draws below stay inside these ranges and needn't reach their ends.
There are 2 independent parts, one for each index of `groups`. The reference program is written for one: setup_inputs(seed, part) draws one part's arguments, and reference() takes and returns one part's arrays. A program takes and returns all parts, laid end to end along the dimension named above; an argument that names none is the same for every part. Nothing has to cross between parts.
All inputs are finite; a program needn't handle non-finite values.
Results may differ from the reference program's by a relative error of at most 0.0085.
Values may be sent and summed in bfloat16 or wider, within the bound.
A program may use at most 128 MiB of HBM per device.

```python
import math
import jax
import jax.numpy as jnp
from jax import lax

NFFT = 8192
TAPS = 4
NSPEC = 64
NCH = 2048
NIN = 64
SAMPLES = 548864


def levels(stream_key, extent, shards, least, top_value):
    factor_of = 1.0
    for axis_at, parts in shards:
        heights = jax.random.uniform(jax.random.fold_in(jax.random.fold_in(stream_key, 6), axis_at), (parts,), jnp.float32, least / len(shards), top_value / len(shards))
        factor_of = factor_of * jnp.repeat(jnp.exp(heights), extent[axis_at] // parts).reshape((-1,) + (1,) * (len(extent) - 1 - axis_at))
    return factor_of


def noise(key, shape, scale, most, cuts=(), held_as=jnp.bfloat16):
    values = scale * jax.random.normal(key, shape, jnp.float32)
    if cuts:
        values = values * levels(key, shape, cuts, -0.22, 0.18)
    return jnp.clip(values, -most, most).astype(held_as)


def setup_inputs(seed: int = 0, part: int = 0) -> dict:
    seeds = jax.random.split(jax.random.key(seed), 3)
    own_keys = jax.random.split(jax.random.fold_in(seeds[2], part), 3)
    samples = noise(own_keys[0], (NIN, SAMPLES), 1.0, 6.0, ((0, 16),))
    filter_coefs = noise(seeds[1], (TAPS, NFFT), (TAPS * NFFT // 8) ** -0.5, 0.09375, (), jnp.float32)
    return dict(samples=samples, filter_coefs=filter_coefs)


HIGH = lax.Precision.HIGHEST


def phase_table(first, second, period):
    rows = lax.broadcasted_iota(jnp.int32, (first, second), 0)
    cols = lax.broadcasted_iota(jnp.int32, (first, second), 1)
    angle = (2.0 * math.pi / period) * ((rows * cols) % period).astype(jnp.float32)
    return jnp.cos(angle), -jnp.sin(angle)


def as_rounded(values):
    return lax.optimization_barrier(values.astype(jnp.bfloat16)).astype(jnp.float32)


def channelise(series, filter_coefs):
    width_b = 128
    width_a = NFFT // width_b
    kept_width = width_b // 4
    frames = series.astype(jnp.float32).reshape(NSPEC + TAPS - 1, NFFT)
    filtered = filter_coefs[0] * frames[0:NSPEC]
    for tap_index in range(1, TAPS):
        filtered = filtered + filter_coefs[tap_index] * frames[tap_index:tap_index + NSPEC]
    grid_view = as_rounded(filtered).reshape(NSPEC, width_a, width_b)
    first_cos, first_sin = phase_table(width_a, width_a, width_a)
    first_cos = as_rounded(first_cos)
    first_sin = as_rounded(first_sin)
    real_one = jnp.einsum("tab,ak->tkb", grid_view, first_cos, precision=HIGH)
    imag_one = jnp.einsum("tab,ak->tkb", grid_view, first_sin, precision=HIGH)
    twist_cos, twist_sin = phase_table(width_a, width_b, NFFT)
    real_two = as_rounded(real_one * twist_cos - imag_one * twist_sin)
    imag_two = as_rounded(real_one * twist_sin + imag_one * twist_cos)
    second_cos, second_sin = phase_table(width_b, width_b, width_b)
    second_cos = as_rounded(second_cos[:, :kept_width])
    second_sin = as_rounded(second_sin[:, :kept_width])
    real_out = (jnp.einsum("tkn,nq->tqk", real_two, second_cos, precision=HIGH)
                - jnp.einsum("tkn,nq->tqk", imag_two, second_sin, precision=HIGH))
    imag_out = (jnp.einsum("tkn,nq->tqk", real_two, second_sin, precision=HIGH)
                + jnp.einsum("tkn,nq->tqk", imag_two, second_cos, precision=HIGH))
    real_part = real_out.reshape(NSPEC, NCH).astype(jnp.bfloat16)
    imag_part = imag_out.reshape(NSPEC, NCH).astype(jnp.bfloat16)
    return jnp.concatenate([real_part.T, imag_part.T], axis=1)


def correlate_block(block):
    values = block.astype(jnp.float32)
    rotated = jnp.concatenate([-values[..., NSPEC:], values[..., :NSPEC]], axis=-1)
    real_sum = jnp.einsum("ikt,jkt->kij", values, values, precision=HIGH)
    imag_sum = jnp.einsum("ikt,jkt->kij", values, rotated, precision=HIGH)
    rows = lax.broadcasted_iota(jnp.int32, (NIN, NIN), 0)
    cols = lax.broadcasted_iota(jnp.int32, (NIN, NIN), 1)
    return (jnp.where(rows >= cols, real_sum, imag_sum) / NSPEC).astype(jnp.bfloat16)


def reference(samples, filter_coefs):
    spectra = lax.map(lambda series: channelise(series, filter_coefs), samples)
    block_size = 32
    blocks = spectra.reshape(NIN, NCH // block_size, block_size, 2 * NSPEC).transpose(1, 0, 2, 3)
    result = lax.map(correlate_block, blocks)
    return result.reshape(NCH, NIN, NIN)
```

```python
import functools
import math

import jax
import jax.numpy as jnp
import numpy as np
from jax import lax
from jax.experimental import pallas as pl
from jax.experimental.pallas import tpu as pltpu
from jax.sharding import PartitionSpec as P


def phase_table(first, second, period):
    rows = lax.broadcasted_iota(jnp.int32, (first, second), 0)
    cols = lax.broadcasted_iota(jnp.int32, (first, second), 1)
    angle = 2.0 * math.pi / period * (rows * cols % period).astype(jnp.float32)
    return (jnp.cos(angle), -jnp.sin(angle))


def correlate_items(block):
    count = block.shape[0]
    nspec_local = block.shape[2] // 2
    rotated = jnp.concatenate([-block[..., nspec_local:], block[..., :nspec_local]], axis=-1)
    real_sum = jnp.einsum("ikt,jkt->kij", block, block, preferred_element_type=jnp.float32)
    imag_sum = jnp.einsum("ikt,jkt->kij", block, rotated, preferred_element_type=jnp.float32)
    rows = lax.broadcasted_iota(jnp.int32, (count, count), 0)
    cols = lax.broadcasted_iota(jnp.int32, (count, count), 1)
    return (jnp.where(rows >= cols, real_sum, imag_sum) / nspec_local).astype(jnp.bfloat16)


def correlate_turned(block):
    flat_block = block.reshape(block.shape[0], block.shape[2], block.shape[3])
    return correlate_items(flat_block)


def plain_body(samples, filter_coefs):
    in_local, total = samples.shape
    taps_count, nfft_local = filter_coefs.shape
    frame_count = total // nfft_local
    nspec_local = frame_count - taps_count + 1
    width_b = 128
    width_a = nfft_local // width_b
    kept_width = width_b // 4
    frames = samples.reshape(in_local, frame_count, nfft_local).astype(jnp.float32)
    filtered = filter_coefs[0] * frames[:, 0:nspec_local]
    for tap_index in range(1, taps_count):
        filtered = (
            filtered + filter_coefs[tap_index] * frames[:, tap_index : tap_index + nspec_local]
        )
    grid_view = filtered.astype(jnp.bfloat16).reshape(in_local, nspec_local, width_a, width_b)
    first_cos, first_sin = phase_table(width_a, width_a, width_a)
    first_table = jnp.concatenate([first_cos, first_sin], axis=1).astype(jnp.bfloat16)
    first_out = jnp.einsum(
        "itab,ak->itkb", grid_view, first_table, preferred_element_type=jnp.float32
    )
    real_one = first_out[:, :, :width_a]
    imag_one = first_out[:, :, width_a:]
    twist_cos, twist_sin = phase_table(width_a, width_b, nfft_local)
    real_two = real_one * twist_cos - imag_one * twist_sin
    imag_two = real_one * twist_sin + imag_one * twist_cos
    stacked = jnp.concatenate(
        [real_two.astype(jnp.bfloat16), imag_two.astype(jnp.bfloat16)], axis=3
    )
    second_cos, second_sin = phase_table(width_b, width_b, width_b)
    second_cos = second_cos[:, :kept_width]
    second_sin = second_sin[:, :kept_width]
    upper_rows = jnp.concatenate([second_cos, second_sin], axis=1)
    lower_rows = jnp.concatenate([-second_sin, second_cos], axis=1)
    second_table = jnp.concatenate([upper_rows, lower_rows], axis=0).astype(jnp.bfloat16)
    second_out = jnp.einsum(
        "itkn,nq->iqkt", stacked, second_table, preferred_element_type=jnp.float32
    )
    real_out = second_out[:, :kept_width]
    imag_out = second_out[:, kept_width:]
    channels = width_a * kept_width
    spectra = jnp.concatenate(
        [real_out.astype(jnp.bfloat16), imag_out.astype(jnp.bfloat16)], axis=3
    )
    spectra = spectra.reshape(in_local, channels, 2 * nspec_local)
    peers = lax.axis_size("inputs")
    per_peer = channels // peers
    owner_view = spectra.reshape(in_local, peers, per_peer, 2 * nspec_local)
    result = correlate_turned(
        lax.all_to_all(owner_view, "inputs", split_axis=1, concat_axis=0, tiled=True)
    )
    return result


WIDTH_B = 128
BF16 = jnp.bfloat16
F32 = jnp.float32
NT = (((1,), (1,)), ((), ()))


def np_phase(first, second, period):
    turns = np.outer(np.arange(first), np.arange(second)) % period
    angle = np.float32(2.0 * math.pi / period) * turns.astype(np.float32)
    return np.cos(angle), -np.sin(angle)


def make_tables(in_local, width_a, kept):
    nfft = width_a * WIDTH_B
    first = np.concatenate([t.T for t in np_phase(width_a, width_a, width_a)], axis=0)
    first = np.kron(first, np.eye(in_local, dtype=np.float32))
    twist = np.concatenate(
        [np.repeat(t, in_local, axis=0) for t in np_phase(width_a, WIDTH_B, nfft)], axis=0
    )
    cos_b, sin_b = (t[:, :kept].T for t in np_phase(WIDTH_B, WIDTH_B, WIDTH_B))
    second = np.concatenate(
        [np.concatenate([cos_b, -sin_b], axis=1), np.concatenate([sin_b, cos_b], axis=1)], axis=0
    )
    return jnp.asarray(first, BF16), jnp.asarray(twist, F32), jnp.asarray(second, BF16)


def correlator_kernel(
    dims, x_any, coef_any, first_any, twist_any, second_any, order_any, half_ref,
    x_ref, coef_in, first_ref, twist_ref, second_ref, order_ref, coef_ref,
    real_ref, imag_ref, turn_ref, send_ref, recv_ref, line_ref, quad_ref, vis_ref,
    load_sem, x_sem, send_sem, recv_sem, own_sem,
):
    peers, in_local, nspec, taps, kept, span, step, pad = dims
    rows = first_ref.shape[1]
    width_a = rows // in_local
    parts = nspec // span
    shared = WIDTH_B // (2 * span)
    wide = shared * span
    groups = width_a // (2 * shared)
    chunks = parts * groups // step
    per_part = groups // step
    slot = span + pad
    half = peers // 2
    me = lax.axis_index("inputs")
    side = me // half
    place = me % half

    def partner(n):
        near = n // half
        return ((side + 1 + near) % 2) * half + (place + n % half + near) % half

    barrier = pltpu.get_barrier_semaphore()

    def greet(n, carry):
        pl.semaphore_signal(
            barrier, inc=1, device_id={"inputs": partner(n)},
            device_id_type=pl.DeviceIdType.MESH,
        )
        return carry

    lax.fori_loop(0, peers - 1, greet, 0)

    def load_frames(start, count, n):
        at = pl.ds(start * rows, count * rows)
        return pltpu.make_async_copy(x_any.at[at], x_ref.at[at], x_sem.at[n])

    def load_part(h):
        return load_frames(h * span + taps - 1, span, h)

    small = [
        pltpu.make_async_copy(src, dst, load_sem.at[n])
        for n, (src, dst) in enumerate((
            (coef_any, coef_in), (first_any, first_ref), (twist_any, twist_ref),
            (second_any, second_ref), (order_any, order_ref),
        ))
    ]
    small[0].start()
    load_frames(0, taps - 1, parts).start()
    load_part(0).start()
    for copy in small[1:]:
        copy.start()
    for n in range(1, parts):
        load_part(n).start()

    small[0].wait()
    for m in range(taps):
        tap = coef_in[pl.ds(m, width_a, stride=taps), :]
        for i in range(in_local):
            coef_ref[pl.ds(m * rows + i, width_a, stride=in_local), :] = tap
    for copy in small[1:]:
        copy.wait()
    load_frames(0, taps - 1, parts).wait()

    lane_block = 64

    def two_spectra(h, tp):
        late_t = tp * 2
        t = h * span + late_t
        filtered = []
        for r in range(0, rows, lane_block):
            frames = [
                x_ref[pl.ds(pl.multiple_of((t + m) * rows + r, lane_block), lane_block), :].astype(F32)
                for m in range(taps + 1)
            ]
            pair = []
            for late in range(2):
                acc = None
                for m in range(taps):
                    at = m * rows + r
                    term = coef_ref[at:at + lane_block, :] * frames[m + late]
                    acc = term if acc is None else acc + term
                pair.append(acc.astype(BF16))
            filtered.append(jnp.concatenate(pair, axis=1))
        filtered = jnp.concatenate(filtered, axis=0)
        out = jnp.dot(first_ref[...], filtered, preferred_element_type=F32)
        w_re, w_im = twist_ref[:rows, :], twist_ref[rows:, :]
        for late in range(2):
            cols = slice(late * WIDTH_B, (late + 1) * WIDTH_B)
            re, im = out[:rows, cols], out[rows:, cols]
            real_ref[pl.ds(late_t + late, rows, stride=slot), :] = re * w_re - im * w_im
            imag_ref[pl.ds(late_t + late, rows, stride=slot), :] = re * w_im + im * w_re

    per_dest = kept // peers * in_local

    def channel_group(h, kp):
        parts_out = []
        for kk in range(2):
            both = []
            for i in range(in_local):
                for u in range(shared):
                    k = (kp * 2 + kk) * shared + u
                    at = pl.ds((k * in_local + i) * slot, span)
                    both.append(jnp.concatenate(
                        [real_ref[at, :].astype(BF16), imag_ref[at, :].astype(BF16)], axis=1
                    ))
            both = jnp.concatenate(both, axis=0)
            res = lax.dot_general(second_ref[...], both, NT, preferred_element_type=F32)
            for i in range(in_local):
                cols = slice(i * wide, (i + 1) * wide)
                turn_ref[pl.ds(kk * kept * in_local + i, kept, stride=in_local), :] = (
                    jnp.concatenate([res[:kept, cols], res[kept:, cols]], axis=1)
                )
            part = turn_ref[kk * kept * in_local:(kk + 1) * kept * in_local, :]
            parts_out.append(part.reshape(peers, per_dest, WIDTH_B))
        send_ref[:, h * groups + kp] = jnp.concatenate(parts_out, axis=1).astype(BF16)

    def remote(c, n):
        dest = partner(n)
        at = pl.ds(c * step, step)
        return pltpu.make_async_remote_copy(
            src_ref=send_ref.at[dest, at], dst_ref=recv_ref.at[me, at],
            send_sem=send_sem.at[c, n], recv_sem=recv_sem.at[c, n],
            device_id={"inputs": dest}, device_id_type=pl.DeviceIdType.MESH,
        )

    def forward(h, carry):
        load_part(h).wait()

        def spectra(tp, u):
            two_spectra(h, tp)
            return u

        lax.fori_loop(0, span // 2, spectra, 0, unroll=4)

        @pl.when(h == 0)
        def _():
            pl.semaphore_wait(barrier, peers - 1)

        def send_chunk(c, u):
            def one(n, v):
                channel_group(h, c * step + n)
                return v

            lax.fori_loop(0, step, one, 0, unroll=2)

            def push(n, v):
                remote(h * per_part + c, n).start()
                return v

            lax.fori_loop(0, peers - 1, push, 0)
            return u

        lax.fori_loop(0, per_part, send_chunk, 0)
        return carry

    lax.fori_loop(0, parts, forward, 0)
    own = pltpu.make_async_copy(send_ref.at[me], recv_ref.at[me], own_sem)
    own.start()
    own.wait()

    count = peers * in_local
    per = 2 * (kept // peers)
    halves = per // 2
    channels = width_a * halves
    low = count // 2
    i_at = lax.broadcasted_iota(jnp.int32, (low, WIDTH_B), 0)
    lane = lax.broadcasted_iota(jnp.int32, (low, WIDTH_B), 1)
    first_half = lane < count
    top_real = i_at >= lane
    low_real = i_at + low >= lane - count
    lane_row = lax.broadcasted_iota(jnp.int32, (count, WIDTH_B), 1)
    masks = [
        jnp.where((lane_row % wide) // span == u, 1.0, 0.0).astype(BF16) for u in range(shared)
    ]

    def swap(v):
        return jnp.concatenate([v[:, wide:], v[:, :wide]], axis=1)

    def line_up(g):
        lined = jnp.dot(
            order_ref[...], recv_ref[:, g].reshape(per * count, WIDTH_B),
            preferred_element_type=F32,
        )
        line_ref[g] = lined.astype(BF16)
        quad_ref[g] = jnp.concatenate([-lined[:, wide:], lined[:, :wide]], axis=1).astype(BF16)

    def correlate(kp):
        for s in range(per):
            at = slice(s * count, (s + 1) * count)
            tiles = [line_ref[h * groups + kp, at, :] for h in range(parts)]
            turned = [quad_ref[h * groups + kp, at, :] for h in range(parts)]
            right = jnp.concatenate(
                [jnp.concatenate(tiles, axis=1), jnp.concatenate(turned, axis=1)], axis=0
            )
            left = jnp.concatenate(
                [jnp.concatenate([t * m for t in tiles], axis=1) for m in masks], axis=0
            )
            res = lax.dot_general(left, right, NT, preferred_element_type=F32)
            for u in range(shared):
                top = res[u * count:u * count + low]
                bottom = res[u * count + low:(u + 1) * count]
                vis = jnp.where(
                    first_half,
                    jnp.where(top_real, top, swap(top)),
                    jnp.where(low_real, swap(bottom), bottom),
                )
                c = (s % halves) * width_a + (kp * 2 + s // halves) * shared + u
                vis_ref[pl.ds(c, low, stride=channels), :] = vis * (1.0 / nspec)

    def receive(c, carry):
        def arrive(n, u):
            remote(c, n).wait()
            return u

        lax.fori_loop(0, peers - 1, arrive, 0)

        def one(n, u):
            line_up(c * step + n)
            return u

        lax.fori_loop(0, step, one, 0, unroll=2)
        return carry

    def finish(c, carry):
        receive((parts - 1) * per_part + c, 0)

        def one(n, u):
            correlate(c * step + n)
            return u

        lax.fori_loop(0, step, one, 0)
        return carry

    lax.fori_loop(0, (parts - 1) * per_part, receive, 0)
    lax.fori_loop(0, per_part, finish, 0)
    half_ref[...] = vis_ref[...].astype(BF16)


def turn_kernel(channels, vis_ref, out_ref):
    half = out_ref.shape[0] // 2
    width = out_ref.shape[1]

    def one_row(i, carry):
        block = vis_ref[pl.ds(pl.multiple_of(i * channels, channels), channels), :]
        block = block.astype(F32).T.astype(BF16)
        out_ref[i] = block[:width]
        out_ref[i + half] = block[width:]
        return carry

    lax.fori_loop(0, half, one_row, 0, unroll=4)


def kernel_body(peers, kept, samples, filter_coefs):
    in_local, total = samples.shape
    taps, nfft = filter_coefs.shape
    width_a = nfft // WIDTH_B
    nspec = total // nfft - taps + 1
    rows = width_a * in_local
    span = 16
    step = 4
    pad = 1
    parts = nspec // span
    groups = width_a * span // WIDTH_B
    chunks = parts * groups // step
    per = 2 * (kept // peers)
    count = peers * in_local
    channels = width_a * per // 2
    x = samples.reshape(in_local, total // WIDTH_B, WIDTH_B).transpose(1, 0, 2)
    x = x.reshape(total // WIDTH_B * in_local, WIDTH_B)
    coefs = filter_coefs.reshape(taps, width_a, WIDTH_B).transpose(1, 0, 2)
    coefs = coefs.reshape(width_a * taps, WIDTH_B)
    first, twist, second = make_tables(in_local, width_a, kept)
    order = np.zeros((per, peers, in_local, peers, per, in_local), np.float32)
    for s in range(per):
        for p in range(peers):
            order[s, p, range(in_local), p, s, range(in_local)] = 1
    order = jnp.asarray(order.reshape(per * count, per * count), BF16)
    blocks = (peers, parts * groups, per * in_local, WIDTH_B)
    lines = (parts * groups, per * count, WIDTH_B)
    inputs = (x, coefs, first, twist, second, order)
    vis = pl.pallas_call(
        functools.partial(
            correlator_kernel, (peers, in_local, nspec, taps, kept, span, step, pad)
        ),
        out_shape=jax.ShapeDtypeStruct((count // 2 * channels, 2 * count), BF16),
        in_specs=[pl.BlockSpec(memory_space=pl.ANY)] * len(inputs),
        out_specs=pl.BlockSpec(memory_space=pltpu.VMEM),
        scratch_shapes=[pltpu.VMEM(a.shape, a.dtype) for a in inputs] + [
            pltpu.VMEM((taps * rows, WIDTH_B), F32),
            pltpu.VMEM((rows * (span + pad), WIDTH_B), F32),
            pltpu.VMEM((rows * (span + pad), WIDTH_B), F32),
            pltpu.VMEM((2 * kept * in_local, WIDTH_B), F32),
            pltpu.VMEM(blocks, BF16),
            pltpu.VMEM(blocks, BF16),
            pltpu.VMEM(lines, BF16),
            pltpu.VMEM(lines, BF16),
            pltpu.VMEM((count // 2 * channels, 2 * count), F32),
            pltpu.SemaphoreType.DMA((len(inputs) - 1,)),
            pltpu.SemaphoreType.DMA((parts + 1,)),
            pltpu.SemaphoreType.DMA((chunks, peers)),
            pltpu.SemaphoreType.DMA((chunks, peers)),
            pltpu.SemaphoreType.DMA,
        ],
        compiler_params=pltpu.CompilerParams(
            collective_id=0, has_side_effects=True, vmem_limit_bytes=56 * 2**20
        ),
        name="correlator",
    )(*inputs)
    out = pl.pallas_call(
        functools.partial(turn_kernel, channels),
        out_shape=jax.ShapeDtypeStruct((count, count, channels), BF16),
        in_specs=[pl.BlockSpec(memory_space=pltpu.VMEM)],
        out_specs=pl.BlockSpec(memory_space=pltpu.VMEM),
        compiler_params=pltpu.CompilerParams(vmem_limit_bytes=32 * 2**20),
        name="turn",
    )(vis)
    return out.transpose(2, 0, 1)


def solution(mesh):
    peers = mesh.shape["inputs"]

    def body(samples, filter_coefs):
        in_local = samples.shape[0]
        kept = WIDTH_B // 4
        nfft = filter_coefs.shape[1]
        nspec = samples.shape[1] // nfft - filter_coefs.shape[0] + 1
        fits = kept % peers == 0 and peers % 2 == 0 and 2 * peers * in_local == WIDTH_B
        fits = fits and nspec % 16 == 0 and nfft % (32 * WIDTH_B) == 0
        if fits and (2 * in_local * (kept // peers)) % 16 == 0:
            return kernel_body(peers, kept, samples, filter_coefs)
        return plain_body(samples, filter_coefs)

    return jax.shard_map(
        body,
        mesh=mesh,
        in_specs=(P(("groups", "inputs"), None), P()),
        out_specs=P(("groups", "inputs"), None, None),
        check_vma=False,
    )
```

```python
import functools
import math

import jax
import jax.numpy as jnp
import numpy as np
from jax import lax
from jax.experimental import pallas as pl
from jax.experimental.pallas import tpu as pltpu
from jax.sharding import PartitionSpec as P


def phase_table(first, second, period):
    rows = lax.broadcasted_iota(jnp.int32, (first, second), 0)
    cols = lax.broadcasted_iota(jnp.int32, (first, second), 1)
    angle = 2.0 * math.pi / period * (rows * cols % period).astype(jnp.float32)
    return (jnp.cos(angle), -jnp.sin(angle))


def correlate_items(block):
    count = block.shape[0]
    nspec_local = block.shape[2] // 2
    rotated = jnp.concatenate([-block[..., nspec_local:], block[..., :nspec_local]], axis=-1)
    real_sum = jnp.einsum("ikt,jkt->kij", block, block, preferred_element_type=jnp.float32)
    imag_sum = jnp.einsum("ikt,jkt->kij", block, rotated, preferred_element_type=jnp.float32)
    rows = lax.broadcasted_iota(jnp.int32, (count, count), 0)
    cols = lax.broadcasted_iota(jnp.int32, (count, count), 1)
    return (jnp.where(rows >= cols, real_sum, imag_sum) / nspec_local).astype(jnp.bfloat16)


def correlate_turned(block):
    flat_block = block.reshape(block.shape[0], block.shape[2], block.shape[3])
    return correlate_items(flat_block)


def plain_body(samples, filter_coefs):
    in_local, total = samples.shape
    taps_count, nfft_local = filter_coefs.shape
    frame_count = total // nfft_local
    nspec_local = frame_count - taps_count + 1
    width_b = 128
    width_a = nfft_local // width_b
    kept_width = width_b // 4
    frames = samples.reshape(in_local, frame_count, nfft_local).astype(jnp.float32)
    filtered = filter_coefs[0] * frames[:, 0:nspec_local]
    for tap_index in range(1, taps_count):
        filtered = (
            filtered + filter_coefs[tap_index] * frames[:, tap_index : tap_index + nspec_local]
        )
    grid_view = filtered.astype(jnp.bfloat16).reshape(in_local, nspec_local, width_a, width_b)
    first_cos, first_sin = phase_table(width_a, width_a, width_a)
    first_table = jnp.concatenate([first_cos, first_sin], axis=1).astype(jnp.bfloat16)
    first_out = jnp.einsum(
        "itab,ak->itkb", grid_view, first_table, preferred_element_type=jnp.float32
    )
    real_one = first_out[:, :, :width_a]
    imag_one = first_out[:, :, width_a:]
    twist_cos, twist_sin = phase_table(width_a, width_b, nfft_local)
    real_two = real_one * twist_cos - imag_one * twist_sin
    imag_two = real_one * twist_sin + imag_one * twist_cos
    stacked = jnp.concatenate(
        [real_two.astype(jnp.bfloat16), imag_two.astype(jnp.bfloat16)], axis=3
    )
    second_cos, second_sin = phase_table(width_b, width_b, width_b)
    second_cos = second_cos[:, :kept_width]
    second_sin = second_sin[:, :kept_width]
    upper_rows = jnp.concatenate([second_cos, second_sin], axis=1)
    lower_rows = jnp.concatenate([-second_sin, second_cos], axis=1)
    second_table = jnp.concatenate([upper_rows, lower_rows], axis=0).astype(jnp.bfloat16)
    second_out = jnp.einsum(
        "itkn,nq->iqkt", stacked, second_table, preferred_element_type=jnp.float32
    )
    real_out = second_out[:, :kept_width]
    imag_out = second_out[:, kept_width:]
    channels = width_a * kept_width
    spectra = jnp.concatenate(
        [real_out.astype(jnp.bfloat16), imag_out.astype(jnp.bfloat16)], axis=3
    )
    spectra = spectra.reshape(in_local, channels, 2 * nspec_local)
    peers = lax.axis_size("inputs")
    per_peer = channels // peers
    owner_view = spectra.reshape(in_local, peers, per_peer, 2 * nspec_local)
    result = correlate_turned(
        lax.all_to_all(owner_view, "inputs", split_axis=1, concat_axis=0, tiled=True)
    )
    return result


WIDTH_B = 128
BF16 = jnp.bfloat16
F32 = jnp.float32
NT = (((1,), (1,)), ((), ()))


def np_phase(first, second, period):
    turns = np.outer(np.arange(first), np.arange(second)) % period
    angle = np.float32(2.0 * math.pi / period) * turns.astype(np.float32)
    return np.cos(angle), -np.sin(angle)


def make_tables(in_local, width_a, kept):
    nfft = width_a * WIDTH_B
    first = np.concatenate([t.T for t in np_phase(width_a, width_a, width_a)], axis=0)
    first = np.kron(first, np.eye(in_local, dtype=np.float32))
    twist = np.concatenate(
        [np.repeat(t, in_local, axis=0) for t in np_phase(width_a, WIDTH_B, nfft)], axis=0
    )
    cos_b, sin_b = (t[:, :kept].T for t in np_phase(WIDTH_B, WIDTH_B, WIDTH_B))
    second = np.concatenate(
        [np.concatenate([cos_b, -sin_b], axis=1), np.concatenate([sin_b, cos_b], axis=1)], axis=0
    )
    return jnp.asarray(first, BF16), jnp.asarray(twist, F32), jnp.asarray(second, BF16)


def correlator_kernel(
    dims, x_any, coef_any, first_any, twist_any, second_any, order_any, half_ref,
    x_ref, coef_in, first_ref, twist_ref, second_ref, order_ref, coef_ref,
    real_ref, imag_ref, turn_ref, send_ref, recv_ref, line_ref, quad_ref, sum_ref, vis_ref,
    load_sem, x_sem, send_sem, recv_sem, own_sem,
):
    peers, in_local, nspec, taps, kept, span, step, pad = dims
    rows = first_ref.shape[1]
    width_a = rows // in_local
    parts = nspec // span
    shared = WIDTH_B // (2 * span)
    wide = shared * span
    groups = width_a // (2 * shared)
    slot = span + pad
    me = lax.axis_index("inputs")

    def partner(n):
        return lax.rem(me + n + 1, peers)

    barrier = pltpu.get_barrier_semaphore()

    def greet(n, carry):
        pl.semaphore_signal(
            barrier, inc=1, device_id={"inputs": partner(n)},
            device_id_type=pl.DeviceIdType.MESH,
        )
        return carry

    lax.fori_loop(0, peers - 1, greet, 0)

    def load_frames(start, count, n):
        at = pl.ds(start * rows, count * rows)
        return pltpu.make_async_copy(x_any.at[at], x_ref.at[at], x_sem.at[n])

    def load_part(h):
        return load_frames(h * span + taps - 1, span, h)

    small = [
        pltpu.make_async_copy(src, dst, load_sem.at[n])
        for n, (src, dst) in enumerate((
            (coef_any, coef_in), (first_any, first_ref), (twist_any, twist_ref),
            (second_any, second_ref), (order_any, order_ref),
        ))
    ]
    small[0].start()
    load_frames(0, taps - 1, parts).start()
    load_part(0).start()
    for copy in small[1:]:
        copy.start()
    for n in range(1, parts):
        load_part(n).start()

    small[0].wait()
    for m in range(taps):
        tap = coef_in[pl.ds(m, width_a, stride=taps), :]
        for i in range(in_local):
            coef_ref[pl.ds(m * rows + i, width_a, stride=in_local), :] = tap
    for copy in small[1:]:
        copy.wait()
    load_frames(0, taps - 1, parts).wait()

    lane_block = 64

    def two_spectra(h, tp):
        late_t = tp * 2
        t = h * span + late_t
        filtered = []
        for r in range(0, rows, lane_block):
            frames = [
                x_ref[pl.ds(pl.multiple_of((t + m) * rows + r, lane_block), lane_block), :].astype(F32)
                for m in range(taps + 1)
            ]
            pair = []
            for late in range(2):
                acc = None
                for m in range(taps):
                    at = m * rows + r
                    term = coef_ref[at:at + lane_block, :] * frames[m + late]
                    acc = term if acc is None else acc + term
                pair.append(acc.astype(BF16))
            filtered.append(jnp.concatenate(pair, axis=1))
        filtered = jnp.concatenate(filtered, axis=0)
        out = jnp.dot(first_ref[...], filtered, preferred_element_type=F32)
        w_re, w_im = twist_ref[:rows, :], twist_ref[rows:, :]
        for late in range(2):
            cols = slice(late * WIDTH_B, (late + 1) * WIDTH_B)
            re, im = out[:rows, cols], out[rows:, cols]
            real_ref[pl.ds(late_t + late, rows, stride=slot), :] = re * w_re - im * w_im
            imag_ref[pl.ds(late_t + late, rows, stride=slot), :] = re * w_im + im * w_re

    per_dest = kept // peers * in_local

    def channel_group(h, kp):
        parts_out = []
        for kk in range(2):
            both = []
            for i in range(in_local):
                for u in range(shared):
                    k = (kp * 2 + kk) * shared + u
                    at = pl.ds((k * in_local + i) * slot, span)
                    both.append(jnp.concatenate(
                        [real_ref[at, :].astype(BF16), imag_ref[at, :].astype(BF16)], axis=1
                    ))
            both = jnp.concatenate(both, axis=0)
            res = lax.dot_general(second_ref[...], both, NT, preferred_element_type=F32)
            for i in range(in_local):
                cols = slice(i * wide, (i + 1) * wide)
                turn_ref[pl.ds(kk * kept * in_local + i, kept, stride=in_local), :] = (
                    jnp.concatenate([res[:kept, cols], res[kept:, cols]], axis=1)
                )
            part = turn_ref[kk * kept * in_local:(kk + 1) * kept * in_local, :]
            parts_out.append(part.reshape(peers, per_dest, WIDTH_B))
        send_ref[:, h * groups + kp] = jnp.concatenate(parts_out, axis=1).astype(BF16)

    def remote(c, size, n):
        dest = partner(n)
        at = pl.ds((c + 1) * step - size, size)
        return pltpu.make_async_remote_copy(
            src_ref=send_ref.at[dest, at], dst_ref=recv_ref.at[me, at],
            send_sem=send_sem.at[c, n], recv_sem=recv_sem.at[c, n],
            device_id={"inputs": dest}, device_id_type=pl.DeviceIdType.MESH,
        )

    def push(c, size):
        def one(n, u):
            remote(c, size, n).start()
            return u

        lax.fori_loop(0, peers - 1, one, 0)

    def forward(h, carry):
        load_part(h).wait()

        def spectra(tp, u):
            two_spectra(h, tp)
            return u

        lax.fori_loop(0, span // 2, spectra, 0, unroll=4)

        @pl.when(h == 0)
        def _():
            pl.semaphore_wait(barrier, peers - 1)

        def send_chunk(c, u):
            def one(n, v):
                channel_group(h, c * step + n)
                return v

            lax.fori_loop(0, step, one, 0, unroll=2)
            split = (h == 0) | (h == parts - 1)

            @pl.when(split)
            def _():
                push(2 * h + c, step)

            @pl.when(jnp.logical_not(split) & (c == 1))
            def _():
                push(2 * h + c, groups)

            return u

        lax.fori_loop(0, 2, send_chunk, 0)
        return carry

    lax.fori_loop(0, parts, forward, 0)
    own = pltpu.make_async_copy(send_ref.at[me], recv_ref.at[me], own_sem)
    own.start()
    own.wait()

    count = peers * in_local
    per = 2 * (kept // peers)
    halves = per // 2
    channels = width_a * halves
    low = count // 2
    i_at = lax.broadcasted_iota(jnp.int32, (low, WIDTH_B), 0)
    lane = lax.broadcasted_iota(jnp.int32, (low, WIDTH_B), 1)
    first_half = lane < count
    top_real = i_at >= lane
    low_real = i_at + low >= lane - count
    lane_row = lax.broadcasted_iota(jnp.int32, (count, WIDTH_B), 1)
    masks = [
        jnp.where((lane_row % wide) // span == u, 1.0, 0.0).astype(BF16) for u in range(shared)
    ]

    signs = jnp.where(
        lax.broadcasted_iota(jnp.int32, (per * count, WIDTH_B), 1) < wide, -1.0, 1.0
    )

    def swap(v):
        return pltpu.roll(v, wide, 1)

    def line_up(g):
        lined = jnp.dot(
            order_ref[...], recv_ref[:, g].reshape(per * count, WIDTH_B),
            preferred_element_type=F32,
        )
        line_ref[g] = lined.astype(BF16)
        quad_ref[g] = (swap(lined) * signs).astype(BF16)

    def gram(kp, s, first, last):
        at = slice(s * count, (s + 1) * count)
        tiles = [line_ref[h * groups + kp, at, :] for h in range(first, last)]
        turned = [quad_ref[h * groups + kp, at, :] for h in range(first, last)]
        right = jnp.concatenate(
            [jnp.concatenate(tiles, axis=1), jnp.concatenate(turned, axis=1)], axis=0
        )
        left = jnp.concatenate(
            [jnp.concatenate([t * m for t in tiles], axis=1) for m in masks], axis=0
        )
        return lax.dot_general(left, right, NT, preferred_element_type=F32)

    def correlate_early(kp, u):
        for s in range(per):
            sum_ref[kp * per + s] = gram(kp, s, 0, parts - 2)
        return u

    def correlate(kp):
        for s in range(per):
            res = sum_ref[kp * per + s] + gram(kp, s, parts - 2, parts)
            for u in range(shared):
                top = res[u * count:u * count + low]
                bottom = res[u * count + low:(u + 1) * count]
                vis = jnp.where(
                    first_half,
                    jnp.where(top_real, top, swap(top)),
                    jnp.where(low_real, swap(bottom), bottom),
                )
                c = (s % halves) * width_a + (kp * 2 + s // halves) * shared + u
                vis_ref[pl.ds(c, low, stride=channels), :] = vis * (1.0 / nspec)

    def arrive(c, size):
        def one(n, u):
            remote(c, size, n).wait()
            return u

        lax.fori_loop(0, peers - 1, one, 0)

    def lines(h):
        def one(n, u):
            line_up(h * groups + n)
            return u

        lax.fori_loop(0, groups, one, 0, unroll=2)

    def middle(h, carry):
        arrive(2 * h + 1, groups)
        lines(h)

        @pl.when(h == parts - 3)
        def _():
            lax.fori_loop(0, groups, correlate_early, 0)

        return carry

    def finish(c, carry):
        arrive(2 * (parts - 1) + c, step)

        def one(n, u):
            kp = c * step + n
            line_up((parts - 1) * groups + kp)
            correlate(kp)
            return u

        lax.fori_loop(0, step, one, 0)
        return carry

    arrive(0, step)
    arrive(1, step)
    lines(0)
    lax.fori_loop(1, parts - 1, middle, 0)
    lax.fori_loop(0, 2, finish, 0)
    half_ref[...] = vis_ref[...].astype(BF16)


def turn_kernel(channels, pieces, vis_any, out_any, vis_ref, out_ref, in_sem, out_sem):
    half = out_ref.shape[0] // 2
    width = out_ref.shape[1]
    each = half // pieces

    def fetch(p):
        at = pl.ds(p * each * channels, each * channels)
        return pltpu.make_async_copy(vis_any.at[at], vis_ref.at[at], in_sem.at[p])

    def put(p, upper):
        at = pl.ds(p * each + upper * half, each)
        return pltpu.make_async_copy(out_ref.at[at], out_any.at[at], out_sem.at[upper, p])

    for p in range(pieces):
        fetch(p).start()

    for p in range(pieces):
        fetch(p).wait()

        def one_row(n, carry):
            i = p * each + n
            block = vis_ref[pl.ds(pl.multiple_of(i * channels, channels), channels), :]
            block = block.astype(F32).T.astype(BF16)
            out_ref[i] = block[:width]
            out_ref[i + half] = block[width:]
            return carry

        lax.fori_loop(0, each, one_row, 0, unroll=4)
        put(p, 0).start()
        put(p, 1).start()
    for p in range(pieces):
        put(p, 0).wait()
        put(p, 1).wait()


def kernel_body(peers, kept, samples, filter_coefs):
    in_local, total = samples.shape
    taps, nfft = filter_coefs.shape
    width_a = nfft // WIDTH_B
    nspec = total // nfft - taps + 1
    rows = width_a * in_local
    span = 16
    pieces = 4
    pad = 1
    parts = nspec // span
    groups = width_a * span // WIDTH_B
    step = groups // 2
    chunks = 2 * parts
    per = 2 * (kept // peers)
    count = peers * in_local
    channels = width_a * per // 2
    x = samples.reshape(in_local, total // WIDTH_B, WIDTH_B).transpose(1, 0, 2)
    x = x.reshape(total // WIDTH_B * in_local, WIDTH_B)
    coefs = filter_coefs.reshape(taps, width_a, WIDTH_B).transpose(1, 0, 2)
    coefs = coefs.reshape(width_a * taps, WIDTH_B)
    first, twist, second = make_tables(in_local, width_a, kept)
    order = np.zeros((per, peers, in_local, peers, per, in_local), np.float32)
    for s in range(per):
        for p in range(peers):
            order[s, p, range(in_local), p, s, range(in_local)] = 1
    order = jnp.asarray(order.reshape(per * count, per * count), BF16)
    blocks = (peers, parts * groups, per * in_local, WIDTH_B)
    lines = (parts * groups, per * count, WIDTH_B)
    inputs = (x, coefs, first, twist, second, order)
    vis = pl.pallas_call(
        functools.partial(
            correlator_kernel, (peers, in_local, nspec, taps, kept, span, step, pad)
        ),
        out_shape=jax.ShapeDtypeStruct((count // 2 * channels, 2 * count), BF16),
        in_specs=[pl.BlockSpec(memory_space=pl.ANY)] * len(inputs),
        out_specs=pl.BlockSpec(memory_space=pltpu.VMEM),
        scratch_shapes=[pltpu.VMEM(a.shape, a.dtype) for a in inputs] + [
            pltpu.VMEM((taps * rows, WIDTH_B), F32),
            pltpu.VMEM((rows * (span + pad), WIDTH_B), F32),
            pltpu.VMEM((rows * (span + pad), WIDTH_B), F32),
            pltpu.VMEM((2 * kept * in_local, WIDTH_B), F32),
            pltpu.VMEM(blocks, BF16),
            pltpu.VMEM(blocks, BF16),
            pltpu.VMEM(lines, BF16),
            pltpu.VMEM(lines, BF16),
            pltpu.VMEM((groups * per, per * count, WIDTH_B), F32),
            pltpu.VMEM((count // 2 * channels, 2 * count), F32),
            pltpu.SemaphoreType.DMA((len(inputs) - 1,)),
            pltpu.SemaphoreType.DMA((parts + 1,)),
            pltpu.SemaphoreType.DMA((chunks, peers)),
            pltpu.SemaphoreType.DMA((chunks, peers)),
            pltpu.SemaphoreType.DMA,
        ],
        compiler_params=pltpu.CompilerParams(
            collective_id=0, has_side_effects=True, vmem_limit_bytes=56 * 2**20
        ),
        name="correlator",
    )(*inputs)
    out = pl.pallas_call(
        functools.partial(turn_kernel, channels, pieces),
        out_shape=jax.ShapeDtypeStruct((count, count, channels), BF16),
        in_specs=[pl.BlockSpec(memory_space=pltpu.HBM)],
        out_specs=pl.BlockSpec(memory_space=pl.ANY),
        scratch_shapes=[
            pltpu.VMEM((count // 2 * channels, 2 * count), BF16),
            pltpu.VMEM((count, count, channels), BF16),
            pltpu.SemaphoreType.DMA((pieces,)),
            pltpu.SemaphoreType.DMA((2, pieces)),
        ],
        compiler_params=pltpu.CompilerParams(vmem_limit_bytes=32 * 2**20),
        name="turn",
    )(vis)
    return out.transpose(2, 0, 1)


def solution(mesh):
    peers = mesh.shape["inputs"]

    def body(samples, filter_coefs):
        in_local = samples.shape[0]
        kept = WIDTH_B // 4
        nfft = filter_coefs.shape[1]
        nspec = samples.shape[1] // nfft - filter_coefs.shape[0] + 1
        fits = kept % peers == 0 and 2 * peers * in_local == WIDTH_B
        fits = fits and nspec % 16 == 0 and nspec >= 64 and nfft % (32 * WIDTH_B) == 0
        if fits and (2 * in_local * (kept // peers)) % 16 == 0:
            return kernel_body(peers, kept, samples, filter_coefs)
        return plain_body(samples, filter_coefs)

    return jax.shard_map(
        body,
        mesh=mesh,
        in_specs=(P(("groups", "inputs"), None), P()),
        out_specs=P(("groups", "inputs"), None, None),
        check_vma=False,
    )
```

```python
import functools
import math

import jax
import jax.numpy as jnp
import numpy as np
from jax import lax
from jax.experimental import pallas as pl
from jax.experimental.pallas import tpu as pltpu
from jax.sharding import PartitionSpec as P


def phase_table(first, second, period):
    rows = lax.broadcasted_iota(jnp.int32, (first, second), 0)
    cols = lax.broadcasted_iota(jnp.int32, (first, second), 1)
    angle = 2.0 * math.pi / period * (rows * cols % period).astype(jnp.float32)
    return (jnp.cos(angle), -jnp.sin(angle))


def correlate_items(block):
    count = block.shape[0]
    nspec_local = block.shape[2] // 2
    rotated = jnp.concatenate([-block[..., nspec_local:], block[..., :nspec_local]], axis=-1)
    real_sum = jnp.einsum("ikt,jkt->kij", block, block, preferred_element_type=jnp.float32)
    imag_sum = jnp.einsum("ikt,jkt->kij", block, rotated, preferred_element_type=jnp.float32)
    rows = lax.broadcasted_iota(jnp.int32, (count, count), 0)
    cols = lax.broadcasted_iota(jnp.int32, (count, count), 1)
    return (jnp.where(rows >= cols, real_sum, imag_sum) / nspec_local).astype(jnp.bfloat16)


def correlate_turned(block):
    flat_block = block.reshape(block.shape[0], block.shape[2], block.shape[3])
    return correlate_items(flat_block)


def plain_body(samples, filter_coefs):
    in_local, total = samples.shape
    taps_count, nfft_local = filter_coefs.shape
    frame_count = total // nfft_local
    nspec_local = frame_count - taps_count + 1
    width_b = 128
    width_a = nfft_local // width_b
    kept_width = width_b // 4
    frames = samples.reshape(in_local, frame_count, nfft_local).astype(jnp.float32)
    filtered = filter_coefs[0] * frames[:, 0:nspec_local]
    for tap_index in range(1, taps_count):
        filtered = (
            filtered + filter_coefs[tap_index] * frames[:, tap_index : tap_index + nspec_local]
        )
    grid_view = filtered.astype(jnp.bfloat16).reshape(in_local, nspec_local, width_a, width_b)
    first_cos, first_sin = phase_table(width_a, width_a, width_a)
    first_table = jnp.concatenate([first_cos, first_sin], axis=1).astype(jnp.bfloat16)
    first_out = jnp.einsum(
        "itab,ak->itkb", grid_view, first_table, preferred_element_type=jnp.float32
    )
    real_one = first_out[:, :, :width_a]
    imag_one = first_out[:, :, width_a:]
    twist_cos, twist_sin = phase_table(width_a, width_b, nfft_local)
    real_two = real_one * twist_cos - imag_one * twist_sin
    imag_two = real_one * twist_sin + imag_one * twist_cos
    stacked = jnp.concatenate(
        [real_two.astype(jnp.bfloat16), imag_two.astype(jnp.bfloat16)], axis=3
    )
    second_cos, second_sin = phase_table(width_b, width_b, width_b)
    second_cos = second_cos[:, :kept_width]
    second_sin = second_sin[:, :kept_width]
    upper_rows = jnp.concatenate([second_cos, second_sin], axis=1)
    lower_rows = jnp.concatenate([-second_sin, second_cos], axis=1)
    second_table = jnp.concatenate([upper_rows, lower_rows], axis=0).astype(jnp.bfloat16)
    second_out = jnp.einsum(
        "itkn,nq->iqkt", stacked, second_table, preferred_element_type=jnp.float32
    )
    real_out = second_out[:, :kept_width]
    imag_out = second_out[:, kept_width:]
    channels = width_a * kept_width
    spectra = jnp.concatenate(
        [real_out.astype(jnp.bfloat16), imag_out.astype(jnp.bfloat16)], axis=3
    )
    spectra = spectra.reshape(in_local, channels, 2 * nspec_local)
    peers = lax.axis_size("inputs")
    per_peer = channels // peers
    owner_view = spectra.reshape(in_local, peers, per_peer, 2 * nspec_local)
    result = correlate_turned(
        lax.all_to_all(owner_view, "inputs", split_axis=1, concat_axis=0, tiled=True)
    )
    return result


WIDTH_B = 128
BF16 = jnp.bfloat16
F32 = jnp.float32
NT = (((1,), (1,)), ((), ()))


def np_phase(first, second, period):
    turns = np.outer(np.arange(first), np.arange(second)) % period
    angle = np.float32(2.0 * math.pi / period) * turns.astype(np.float32)
    return np.cos(angle), -np.sin(angle)


def make_tables(in_local, width_a, kept):
    nfft = width_a * WIDTH_B
    first = np.concatenate([t.T for t in np_phase(width_a, width_a, width_a)], axis=0)
    first = np.kron(first, np.eye(in_local, dtype=np.float32))
    twist = np.concatenate(
        [np.repeat(t, in_local, axis=0) for t in np_phase(width_a, WIDTH_B, nfft)], axis=0
    )
    cos_b, sin_b = (t[:, :kept].T for t in np_phase(WIDTH_B, WIDTH_B, WIDTH_B))
    second = np.concatenate(
        [np.concatenate([cos_b, -sin_b], axis=1), np.concatenate([sin_b, cos_b], axis=1)], axis=0
    )
    return jnp.asarray(first, BF16), jnp.asarray(twist, F32), jnp.asarray(second, BF16)


def correlator_kernel(
    dims, x_any, coef_any, first_any, twist_any, second_any, order_any, out_any,
    x_ref, coef_in, first_ref, twist_ref, second_ref, order_ref, coef_ref,
    real_ref, imag_ref, turn_ref, send_ref, recv_ref, line_ref, quad_ref, sum_ref, vis_ref, half_ref,
    load_sem, x_sem, send_sem, recv_sem, own_sem,
):
    peers, in_local, nspec, taps, kept, span, head, tail, pieces, pad = dims
    rows = first_ref.shape[1]
    width_a = rows // in_local
    parts = nspec // span
    shared = WIDTH_B // (2 * span)
    wide = shared * span
    groups = width_a // (2 * shared)
    slot = span + pad
    me = lax.axis_index("inputs")

    def partner(n):
        return lax.rem(me + n + 1, peers)

    barrier = pltpu.get_barrier_semaphore()

    def greet(n, carry):
        pl.semaphore_signal(
            barrier, inc=1, device_id={"inputs": partner(n)},
            device_id_type=pl.DeviceIdType.MESH,
        )
        return carry


    def load_frames(start, count, n):
        at = pl.ds(start * rows, count * rows)
        return pltpu.make_async_copy(x_any.at[at], x_ref.at[at], x_sem.at[n])

    def load_part(h):
        return load_frames(h * span + taps - 1, span, h)

    small = [
        pltpu.make_async_copy(src, dst, load_sem.at[n])
        for n, (src, dst) in enumerate((
            (coef_any, coef_in), (first_any, first_ref), (twist_any, twist_ref),
            (second_any, second_ref), (order_any, order_ref),
        ))
    ]
    small[0].start()
    load_frames(0, taps - 1, parts).start()
    load_part(0).start()
    for copy in small[1:]:
        copy.start()
    for n in range(1, parts):
        load_part(n).start()
    lax.fori_loop(0, peers - 1, greet, 0)

    small[0].wait()
    for m in range(taps):
        tap = coef_in[pl.ds(m, width_a, stride=taps), :]
        for i in range(in_local):
            coef_ref[pl.ds(m * rows + i, width_a, stride=in_local), :] = tap
    for copy in small[1:]:
        copy.wait()
    load_frames(0, taps - 1, parts).wait()

    lane_block = 64

    def two_spectra(h, tp):
        late_t = tp * 2
        t = h * span + late_t
        filtered = []
        for r in range(0, rows, lane_block):
            frames = [
                x_ref[pl.ds(pl.multiple_of((t + m) * rows + r, lane_block), lane_block), :].astype(F32)
                for m in range(taps + 1)
            ]
            pair = []
            for late in range(2):
                acc = None
                for m in range(taps):
                    at = m * rows + r
                    term = coef_ref[at:at + lane_block, :] * frames[m + late]
                    acc = term if acc is None else acc + term
                pair.append(acc.astype(BF16))
            filtered.append(jnp.concatenate(pair, axis=1))
        filtered = jnp.concatenate(filtered, axis=0)
        out = jnp.dot(first_ref[...], filtered, preferred_element_type=F32)
        w_re, w_im = twist_ref[:rows, :], twist_ref[rows:, :]
        for late in range(2):
            cols = slice(late * WIDTH_B, (late + 1) * WIDTH_B)
            re, im = out[:rows, cols], out[rows:, cols]
            real_ref[pl.ds(late_t + late, rows, stride=slot), :] = re * w_re - im * w_im
            imag_ref[pl.ds(late_t + late, rows, stride=slot), :] = re * w_im + im * w_re

    per_dest = kept // peers * in_local

    def channel_group(h, kp):
        parts_out = []
        for kk in range(2):
            both = []
            for i in range(in_local):
                for u in range(shared):
                    k = (kp * 2 + kk) * shared + u
                    at = pl.ds((k * in_local + i) * slot, span)
                    both.append(jnp.concatenate(
                        [real_ref[at, :].astype(BF16), imag_ref[at, :].astype(BF16)], axis=1
                    ))
            both = jnp.concatenate(both, axis=0)
            res = lax.dot_general(second_ref[...], both, NT, preferred_element_type=F32)
            for i in range(in_local):
                cols = slice(i * wide, (i + 1) * wide)
                turn_ref[pl.ds(kk * kept * in_local + i, kept, stride=in_local), :] = (
                    jnp.concatenate([res[:kept, cols], res[kept:, cols]], axis=1)
                )
            part = turn_ref[kk * kept * in_local:(kk + 1) * kept * in_local, :]
            parts_out.append(part.reshape(peers, per_dest, WIDTH_B))
        send_ref[:, h * groups + kp] = jnp.concatenate(parts_out, axis=1).astype(BF16)

    def remote(c, h, start, size, n):
        dest = partner(n)
        at = pl.ds(h * groups + start, size)
        return pltpu.make_async_remote_copy(
            src_ref=send_ref.at[dest, at], dst_ref=recv_ref.at[me, at],
            send_sem=send_sem.at[c, n], recv_sem=recv_sem.at[c, n],
            device_id={"inputs": dest}, device_id_type=pl.DeviceIdType.MESH,
        )

    def push(c, h, start, size):
        def one(n, u):
            remote(c, h, start, size, n).start()
            return u

        lax.fori_loop(0, peers - 1, one, 0)

    def arrive(c, h, start, size):
        def one(n, u):
            remote(c, h, start, size, n).wait()
            return u

        lax.fori_loop(0, peers - 1, one, 0)

    def forward(h, carry):
        load_part(h).wait()

        def spectra(tp, u):
            two_spectra(h, tp)
            return u

        lax.fori_loop(0, span // 2, spectra, 0, unroll=4)

        def two_groups(n, u):
            channel_group(h, 2 * n)
            channel_group(h, 2 * n + 1)
            return u

        is_first = h == 0
        is_last = h == parts - 1
        cut = jnp.where(is_first, head // 2, jnp.where(is_last, tail // 2, 0))
        lax.fori_loop(0, cut, two_groups, 0)

        @pl.when(is_first)
        def _():
            pl.semaphore_wait(barrier, peers - 1)
            push(0, h, 0, head)

        @pl.when(is_last)
        def _():
            push(2 * h, h, 0, tail)

        lax.fori_loop(cut, groups // 2, two_groups, 0)

        @pl.when(is_first)
        def _():
            push(1, h, head, groups - head)

        @pl.when(is_last)
        def _():
            push(2 * h + 1, h, tail, groups - tail)

        @pl.when(jnp.logical_not(is_first | is_last))
        def _():
            push(2 * h + 1, h, 0, groups)

        return carry

    lax.fori_loop(0, parts, forward, 0)
    own = pltpu.make_async_copy(send_ref.at[me], recv_ref.at[me], own_sem)
    own.start()
    own.wait()

    count = peers * in_local
    per = 2 * (kept // peers)
    halves = per // 2
    channels = width_a * halves
    low = count // 2
    i_at = lax.broadcasted_iota(jnp.int32, (low, WIDTH_B), 0)
    lane = lax.broadcasted_iota(jnp.int32, (low, WIDTH_B), 1)
    first_half = lane < count
    top_real = i_at >= lane
    low_real = i_at + low >= lane - count
    lane_row = lax.broadcasted_iota(jnp.int32, (count, WIDTH_B), 1)
    masks = [
        jnp.where((lane_row % wide) // span == u, 1.0, 0.0).astype(BF16) for u in range(shared)
    ]

    signs = jnp.where(
        lax.broadcasted_iota(jnp.int32, (per * count, WIDTH_B), 1) < wide, -1.0, 1.0
    )

    def swap(v):
        return pltpu.roll(v, wide, 1)

    def line_up(g):
        lined = jnp.dot(
            order_ref[...], recv_ref[:, g].reshape(per * count, WIDTH_B),
            preferred_element_type=F32,
        )
        line_ref[g] = lined.astype(BF16)
        quad_ref[g] = (swap(lined) * signs).astype(BF16)

    def gram(kp, s, first, last):
        at = slice(s * count, (s + 1) * count)
        tiles = [line_ref[h * groups + kp, at, :] for h in range(first, last)]
        turned = [quad_ref[h * groups + kp, at, :] for h in range(first, last)]
        right = jnp.concatenate(
            [jnp.concatenate(tiles, axis=1), jnp.concatenate(turned, axis=1)], axis=0
        )
        left = jnp.concatenate(
            [jnp.concatenate([t * m for t in tiles], axis=1) for m in masks], axis=0
        )
        return lax.dot_general(left, right, NT, preferred_element_type=F32)

    def correlate_early(kp, u):
        for s in range(per):
            sum_ref[kp * per + s] = gram(kp, s, 0, parts - 2)
        return u

    def correlate(kp):
        for s in range(per):
            res = sum_ref[kp * per + s] + gram(kp, s, parts - 2, parts)
            for u in range(shared):
                top = res[u * count:u * count + low]
                bottom = res[u * count + low:(u + 1) * count]
                vis = jnp.where(
                    first_half,
                    jnp.where(top_real, top, swap(top)),
                    jnp.where(low_real, swap(bottom), bottom),
                )
                c = (s % halves) * width_a + (kp * 2 + s // halves) * shared + u
                vis_ref[pl.ds(c, low, stride=channels), :] = vis * (1.0 / nspec)

    def lines(h):
        def one(n, u):
            line_up(h * groups + n)
            return u

        lax.fori_loop(0, groups, one, 0, unroll=2)

    def middle(h, carry):
        arrive(2 * h + 1, h, 0, groups)
        lines(h)

        @pl.when(h == parts - 3)
        def _():
            lax.fori_loop(0, groups, correlate_early, 0)

        return carry

    def finish(n, u):
        line_up((parts - 1) * groups + n)
        correlate(n)
        return u

    arrive(0, 0, 0, head)
    arrive(1, 0, head, groups - head)
    lines(0)
    lax.fori_loop(1, parts - 1, middle, 0)
    arrive(2 * parts - 2, parts - 1, 0, tail)
    lax.fori_loop(0, tail, finish, 0, unroll=2)
    arrive(2 * parts - 1, parts - 1, tail, groups - tail)
    lax.fori_loop(tail, groups, finish, 0, unroll=2)

    piece = vis_ref.shape[0] // pieces

    def put(p):
        at = pl.ds(p * piece, piece)
        return pltpu.make_async_copy(half_ref.at[at], out_any.at[at], load_sem.at[p])

    for p in range(pieces):
        at = slice(p * piece, (p + 1) * piece)
        half_ref[at, :] = vis_ref[at, :].astype(BF16)
        put(p).start()
    for p in range(pieces):
        put(p).wait()


def turn_kernel(channels, pieces, vis_any, out_any, vis_ref, out_ref, in_sem, out_sem):
    half = out_ref.shape[0] // 2
    width = out_ref.shape[1]
    each = half // pieces

    def fetch(p):
        at = pl.ds(p * each * channels, each * channels)
        return pltpu.make_async_copy(vis_any.at[at], vis_ref.at[at], in_sem.at[p])

    def put(p, upper):
        at = pl.ds(p * each + upper * half, each)
        return pltpu.make_async_copy(out_ref.at[at], out_any.at[at], out_sem.at[upper, p])

    for p in range(pieces):
        fetch(p).start()

    for p in range(pieces):
        fetch(p).wait()

        def one_row(n, carry):
            i = p * each + n
            block = vis_ref[pl.ds(pl.multiple_of(i * channels, channels), channels), :]
            block = block.astype(F32).T.astype(BF16)
            out_ref[i] = block[:width]
            out_ref[i + half] = block[width:]
            return carry

        lax.fori_loop(0, each, one_row, 0, unroll=4)
        put(p, 0).start()
        put(p, 1).start()
    for p in range(pieces):
        put(p, 0).wait()
        put(p, 1).wait()


def kernel_body(peers, kept, samples, filter_coefs):
    in_local, total = samples.shape
    taps, nfft = filter_coefs.shape
    width_a = nfft // WIDTH_B
    nspec = total // nfft - taps + 1
    rows = width_a * in_local
    span = 16
    pieces = 4
    pad = 1
    parts = nspec // span
    groups = width_a * span // WIDTH_B
    head = 2
    tail = groups // 2
    chunks = 2 * parts
    per = 2 * (kept // peers)
    count = peers * in_local
    channels = width_a * per // 2
    x = samples.reshape(in_local, total // WIDTH_B, WIDTH_B).transpose(1, 0, 2)
    x = x.reshape(total // WIDTH_B * in_local, WIDTH_B)
    coefs = filter_coefs.reshape(taps, width_a, WIDTH_B).transpose(1, 0, 2)
    coefs = coefs.reshape(width_a * taps, WIDTH_B)
    first, twist, second = make_tables(in_local, width_a, kept)
    order = np.zeros((per, peers, in_local, peers, per, in_local), np.float32)
    for s in range(per):
        for p in range(peers):
            order[s, p, range(in_local), p, s, range(in_local)] = 1
    order = jnp.asarray(order.reshape(per * count, per * count), BF16)
    blocks = (peers, parts * groups, per * in_local, WIDTH_B)
    lines = (parts * groups, per * count, WIDTH_B)
    inputs = (x, coefs, first, twist, second, order)
    vis = pl.pallas_call(
        functools.partial(
            correlator_kernel, (peers, in_local, nspec, taps, kept, span, head, tail, pieces, pad)
        ),
        out_shape=jax.ShapeDtypeStruct((count // 2 * channels, 2 * count), BF16),
        in_specs=[pl.BlockSpec(memory_space=pl.ANY)] * len(inputs),
        out_specs=pl.BlockSpec(memory_space=pl.ANY),
        scratch_shapes=[pltpu.VMEM(a.shape, a.dtype) for a in inputs] + [
            pltpu.VMEM((taps * rows, WIDTH_B), F32),
            pltpu.VMEM((rows * (span + pad), WIDTH_B), F32),
            pltpu.VMEM((rows * (span + pad), WIDTH_B), F32),
            pltpu.VMEM((2 * kept * in_local, WIDTH_B), F32),
            pltpu.VMEM(blocks, BF16),
            pltpu.VMEM(blocks, BF16),
            pltpu.VMEM(lines, BF16),
            pltpu.VMEM(lines, BF16),
            pltpu.VMEM((groups * per, per * count, WIDTH_B), F32),
            pltpu.VMEM((count // 2 * channels, 2 * count), F32),
            pltpu.VMEM((count // 2 * channels, 2 * count), BF16),
            pltpu.SemaphoreType.DMA((len(inputs) - 1,)),
            pltpu.SemaphoreType.DMA((parts + 1,)),
            pltpu.SemaphoreType.DMA((chunks, peers)),
            pltpu.SemaphoreType.DMA((chunks, peers)),
            pltpu.SemaphoreType.DMA,
        ],
        compiler_params=pltpu.CompilerParams(
            collective_id=0, has_side_effects=True, vmem_limit_bytes=56 * 2**20
        ),
        name="correlator",
    )(*inputs)
    out = pl.pallas_call(
        functools.partial(turn_kernel, channels, pieces),
        out_shape=jax.ShapeDtypeStruct((count, count, channels), BF16),
        in_specs=[pl.BlockSpec(memory_space=pltpu.HBM)],
        out_specs=pl.BlockSpec(memory_space=pl.ANY),
        scratch_shapes=[
            pltpu.VMEM((count // 2 * channels, 2 * count), BF16),
            pltpu.VMEM((count, count, channels), BF16),
            pltpu.SemaphoreType.DMA((pieces,)),
            pltpu.SemaphoreType.DMA((2, pieces)),
        ],
        compiler_params=pltpu.CompilerParams(vmem_limit_bytes=60 * 2**20),
        name="turn",
    )(vis)
    return out.transpose(2, 0, 1)


def solution(mesh):
    peers = mesh.shape["inputs"]

    def body(samples, filter_coefs):
        in_local = samples.shape[0]
        kept = WIDTH_B // 4
        nfft = filter_coefs.shape[1]
        nspec = samples.shape[1] // nfft - filter_coefs.shape[0] + 1
        fits = kept % peers == 0 and 2 * peers * in_local == WIDTH_B
        fits = fits and nspec % 16 == 0 and nspec >= 64 and nfft % (32 * WIDTH_B) == 0
        if fits and (2 * in_local * (kept // peers)) % 16 == 0:
            return kernel_body(peers, kept, samples, filter_coefs)
        return plain_body(samples, filter_coefs)

    return jax.shard_map(
        body,
        mesh=mesh,
        in_specs=(P(("groups", "inputs"), None), P()),
        out_specs=P(("groups", "inputs"), None, None),
        check_vma=False,
    )
```

```python
import functools
import math

import jax
import jax.numpy as jnp
import numpy as np
from jax import lax
from jax.experimental import pallas as pl
from jax.experimental.pallas import tpu as pltpu
from jax.sharding import PartitionSpec as P


def phase_table(first, second, period):
    rows = lax.broadcasted_iota(jnp.int32, (first, second), 0)
    cols = lax.broadcasted_iota(jnp.int32, (first, second), 1)
    angle = 2.0 * math.pi / period * (rows * cols % period).astype(jnp.float32)
    return (jnp.cos(angle), -jnp.sin(angle))


def correlate_items(block):
    count = block.shape[0]
    nspec_local = block.shape[2] // 2
    rotated = jnp.concatenate([-block[..., nspec_local:], block[..., :nspec_local]], axis=-1)
    real_sum = jnp.einsum("ikt,jkt->kij", block, block, preferred_element_type=jnp.float32)
    imag_sum = jnp.einsum("ikt,jkt->kij", block, rotated, preferred_element_type=jnp.float32)
    rows = lax.broadcasted_iota(jnp.int32, (count, count), 0)
    cols = lax.broadcasted_iota(jnp.int32, (count, count), 1)
    return (jnp.where(rows >= cols, real_sum, imag_sum) / nspec_local).astype(jnp.bfloat16)


def correlate_turned(block):
    flat_block = block.reshape(block.shape[0], block.shape[2], block.shape[3])
    return correlate_items(flat_block)


def plain_body(samples, filter_coefs):
    in_local, total = samples.shape
    taps_count, nfft_local = filter_coefs.shape
    frame_count = total // nfft_local
    nspec_local = frame_count - taps_count + 1
    width_b = 128
    width_a = nfft_local // width_b
    kept_width = width_b // 4
    frames = samples.reshape(in_local, frame_count, nfft_local).astype(jnp.float32)
    filtered = filter_coefs[0] * frames[:, 0:nspec_local]
    for tap_index in range(1, taps_count):
        filtered = (
            filtered + filter_coefs[tap_index] * frames[:, tap_index : tap_index + nspec_local]
        )
    grid_view = filtered.astype(jnp.bfloat16).reshape(in_local, nspec_local, width_a, width_b)
    first_cos, first_sin = phase_table(width_a, width_a, width_a)
    first_table = jnp.concatenate([first_cos, first_sin], axis=1).astype(jnp.bfloat16)
    first_out = jnp.einsum(
        "itab,ak->itkb", grid_view, first_table, preferred_element_type=jnp.float32
    )
    real_one = first_out[:, :, :width_a]
    imag_one = first_out[:, :, width_a:]
    twist_cos, twist_sin = phase_table(width_a, width_b, nfft_local)
    real_two = real_one * twist_cos - imag_one * twist_sin
    imag_two = real_one * twist_sin + imag_one * twist_cos
    stacked = jnp.concatenate(
        [real_two.astype(jnp.bfloat16), imag_two.astype(jnp.bfloat16)], axis=3
    )
    second_cos, second_sin = phase_table(width_b, width_b, width_b)
    second_cos = second_cos[:, :kept_width]
    second_sin = second_sin[:, :kept_width]
    upper_rows = jnp.concatenate([second_cos, second_sin], axis=1)
    lower_rows = jnp.concatenate([-second_sin, second_cos], axis=1)
    second_table = jnp.concatenate([upper_rows, lower_rows], axis=0).astype(jnp.bfloat16)
    second_out = jnp.einsum(
        "itkn,nq->iqkt", stacked, second_table, preferred_element_type=jnp.float32
    )
    real_out = second_out[:, :kept_width]
    imag_out = second_out[:, kept_width:]
    channels = width_a * kept_width
    spectra = jnp.concatenate(
        [real_out.astype(jnp.bfloat16), imag_out.astype(jnp.bfloat16)], axis=3
    )
    spectra = spectra.reshape(in_local, channels, 2 * nspec_local)
    peers = lax.axis_size("inputs")
    per_peer = channels // peers
    owner_view = spectra.reshape(in_local, peers, per_peer, 2 * nspec_local)
    result = correlate_turned(
        lax.all_to_all(owner_view, "inputs", split_axis=1, concat_axis=0, tiled=True)
    )
    return result


WIDTH_B = 128
BF16 = jnp.bfloat16
F32 = jnp.float32
NT = (((1,), (1,)), ((), ()))


def np_phase(first, second, period):
    turns = np.outer(np.arange(first), np.arange(second)) % period
    angle = np.float32(2.0 * math.pi / period) * turns.astype(np.float32)
    return np.cos(angle), -np.sin(angle)


def make_tables(in_local, width_a, kept):
    nfft = width_a * WIDTH_B
    first = np.concatenate([t.T for t in np_phase(width_a, width_a, width_a)], axis=0)
    first = np.kron(first, np.eye(in_local, dtype=np.float32))
    twist = np.concatenate(
        [np.repeat(t, in_local, axis=0) for t in np_phase(width_a, WIDTH_B, nfft)], axis=0
    )
    cos_b, sin_b = (t[:, :kept].T for t in np_phase(WIDTH_B, WIDTH_B, WIDTH_B))
    second = np.concatenate(
        [np.concatenate([cos_b, -sin_b], axis=1), np.concatenate([sin_b, cos_b], axis=1)], axis=0
    )
    return jnp.asarray(first, BF16), jnp.asarray(twist, F32), jnp.asarray(second, BF16)


def correlator_kernel(
    dims, x_any, coef_any, first_any, twist_any, second_any, order_any, out_any,
    x_ref, coef_in, first_ref, twist_ref, second_ref, order_ref, coef_ref,
    real_ref, imag_ref, turn_ref, send_ref, recv_ref, line_ref, quad_ref, sum_ref, vis_ref, half_ref,
    load_sem, x_sem, send_sem, recv_sem, own_sem,
):
    peers, in_local, nspec, taps, kept, span, head, tail, pieces, pad = dims
    rows = first_ref.shape[1]
    width_a = rows // in_local
    parts = nspec // span
    shared = WIDTH_B // (2 * span)
    wide = shared * span
    groups = width_a // (2 * shared)
    slot = span + pad
    me = lax.axis_index("inputs")

    def partner(n):
        return lax.rem(me + n + 1, peers)

    barrier = pltpu.get_barrier_semaphore()

    def greet(n, carry):
        pl.semaphore_signal(
            barrier, inc=1, device_id={"inputs": partner(n)},
            device_id_type=pl.DeviceIdType.MESH,
        )
        return carry


    def load_frames(start, count, n):
        at = pl.ds(start * rows, count * rows)
        return pltpu.make_async_copy(x_any.at[at], x_ref.at[at], x_sem.at[n])

    def load_part(h):
        return load_frames(h * span + taps - 1, span, h)

    small = [
        pltpu.make_async_copy(src, dst, load_sem.at[n])
        for n, (src, dst) in enumerate((
            (coef_any, coef_in), (first_any, first_ref), (twist_any, twist_ref),
            (second_any, second_ref), (order_any, order_ref),
        ))
    ]
    small[0].start()
    load_frames(0, taps - 1, parts).start()
    load_part(0).start()
    for copy in small[1:]:
        copy.start()
    for n in range(1, parts):
        load_part(n).start()
    lax.fori_loop(0, peers - 1, greet, 0)

    small[0].wait()
    for m in range(taps):
        tap = coef_in[pl.ds(m, width_a, stride=taps), :]
        for i in range(in_local):
            coef_ref[pl.ds(m * rows + i, width_a, stride=in_local), :] = tap
    for copy in small[1:]:
        copy.wait()
    load_frames(0, taps - 1, parts).wait()

    lane_block = 64

    def two_spectra(h, tp):
        late_t = tp * 2
        t = h * span + late_t
        filtered = []
        for r in range(0, rows, lane_block):
            frames = [
                x_ref[pl.ds(pl.multiple_of((t + m) * rows + r, lane_block), lane_block), :].astype(F32)
                for m in range(taps + 1)
            ]
            pair = []
            for late in range(2):
                acc = None
                for m in range(taps):
                    at = m * rows + r
                    term = coef_ref[at:at + lane_block, :] * frames[m + late]
                    acc = term if acc is None else acc + term
                pair.append(acc.astype(BF16))
            filtered.append(jnp.concatenate(pair, axis=1))
        filtered = jnp.concatenate(filtered, axis=0)
        out = jnp.dot(first_ref[...], filtered, preferred_element_type=F32)
        w_re, w_im = twist_ref[:rows, :], twist_ref[rows:, :]
        for late in range(2):
            cols = slice(late * WIDTH_B, (late + 1) * WIDTH_B)
            re, im = out[:rows, cols], out[rows:, cols]
            real_ref[pl.ds(late_t + late, rows, stride=slot), :] = re * w_re - im * w_im
            imag_ref[pl.ds(late_t + late, rows, stride=slot), :] = re * w_im + im * w_re

    per_dest = kept // peers * in_local

    def channel_group(h, kp):
        parts_out = []
        for kk in range(2):
            both = []
            for i in range(in_local):
                for u in range(shared):
                    k = (kp * 2 + kk) * shared + u
                    at = pl.ds((k * in_local + i) * slot, span)
                    both.append(jnp.concatenate(
                        [real_ref[at, :].astype(BF16), imag_ref[at, :].astype(BF16)], axis=1
                    ))
            both = jnp.concatenate(both, axis=0)
            res = lax.dot_general(second_ref[...], both, NT, preferred_element_type=F32)
            for i in range(in_local):
                cols = slice(i * wide, (i + 1) * wide)
                turn_ref[pl.ds(kk * kept * in_local + i, kept, stride=in_local), :] = (
                    jnp.concatenate([res[:kept, cols], res[kept:, cols]], axis=1)
                )
            part = turn_ref[kk * kept * in_local:(kk + 1) * kept * in_local, :]
            parts_out.append(part.reshape(peers, per_dest, WIDTH_B))
        send_ref[:, h * groups + kp] = jnp.concatenate(parts_out, axis=1).astype(BF16)

    def remote(c, h, start, size, n):
        dest = partner(n)
        at = pl.ds(h * groups + start, size)
        return pltpu.make_async_remote_copy(
            src_ref=send_ref.at[dest, at], dst_ref=recv_ref.at[me, at],
            send_sem=send_sem.at[c, n], recv_sem=recv_sem.at[c, n],
            device_id={"inputs": dest}, device_id_type=pl.DeviceIdType.MESH,
        )

    def push(c, h, start, size):
        def one(n, u):
            remote(c, h, start, size, n).start()
            return u

        lax.fori_loop(0, peers - 1, one, 0)

    def arrive(c, h, start, size):
        def one(n, u):
            remote(c, h, start, size, n).wait()
            return u

        lax.fori_loop(0, peers - 1, one, 0)

    def forward(h, carry):
        load_part(h).wait()

        def spectra(tp, u):
            two_spectra(h, tp)
            return u

        lax.fori_loop(0, span // 2, spectra, 0, unroll=4)

        def two_groups(n, u):
            channel_group(h, 2 * n)
            channel_group(h, 2 * n + 1)
            return u

        is_first = h == 0
        is_last = h == parts - 1
        cut = jnp.where(is_first, head // 2, jnp.where(is_last, tail // 2, 0))
        lax.fori_loop(0, cut, two_groups, 0)

        @pl.when(is_first)
        def _():
            pl.semaphore_wait(barrier, peers - 1)
            push(0, h, 0, head)

        @pl.when(is_last)
        def _():
            push(2 * h, h, 0, tail)

        lax.fori_loop(cut, groups // 2, two_groups, 0)

        @pl.when(is_first)
        def _():
            push(1, h, head, groups - head)

        @pl.when(is_last)
        def _():
            push(2 * h + 1, h, tail, groups - tail)

        @pl.when(jnp.logical_not(is_first | is_last))
        def _():
            push(2 * h + 1, h, 0, groups)

        return carry

    lax.fori_loop(0, parts, forward, 0)
    own = pltpu.make_async_copy(send_ref.at[me], recv_ref.at[me], own_sem)
    own.start()
    own.wait()

    count = peers * in_local
    per = 2 * (kept // peers)
    halves = per // 2
    channels = width_a * halves
    low = count // 2
    i_at = lax.broadcasted_iota(jnp.int32, (low, WIDTH_B), 0)
    lane = lax.broadcasted_iota(jnp.int32, (low, WIDTH_B), 1)
    first_half = lane < count
    top_real = i_at >= lane
    low_real = i_at + low >= lane - count
    lane_row = lax.broadcasted_iota(jnp.int32, (count, WIDTH_B), 1)
    masks = [
        jnp.where((lane_row % wide) // span == u, 1.0, 0.0).astype(BF16) for u in range(shared)
    ]

    signs = jnp.where(
        lax.broadcasted_iota(jnp.int32, (per * count, WIDTH_B), 1) < wide, -1.0, 1.0
    )

    def swap(v):
        return pltpu.roll(v, wide, 1)

    def line_up(g):
        lined = jnp.dot(
            order_ref[...], recv_ref[:, g].reshape(per * count, WIDTH_B),
            preferred_element_type=F32,
        )
        line_ref[g] = lined.astype(BF16)
        quad_ref[g] = (swap(lined) * signs).astype(BF16)

    def gram(kp, s, first, last):
        at = slice(s * count, (s + 1) * count)
        tiles = [line_ref[h * groups + kp, at, :] for h in range(first, last)]
        turned = [quad_ref[h * groups + kp, at, :] for h in range(first, last)]
        right = jnp.concatenate(
            [jnp.concatenate(tiles, axis=1), jnp.concatenate(turned, axis=1)], axis=0
        )
        left = jnp.concatenate(
            [jnp.concatenate([t * m for t in tiles], axis=1) for m in masks], axis=0
        )
        return lax.dot_general(left, right, NT, preferred_element_type=F32)

    def correlate_early(kp, u):
        for s in range(per):
            sum_ref[kp * per + s] = gram(kp, s, 0, parts - 2)
        return u

    def correlate(kp):
        for s in range(per):
            res = sum_ref[kp * per + s] + gram(kp, s, parts - 2, parts)
            for u in range(shared):
                top = res[u * count:u * count + low]
                bottom = res[u * count + low:(u + 1) * count]
                vis = jnp.where(
                    first_half,
                    jnp.where(top_real, top, swap(top)),
                    jnp.where(low_real, swap(bottom), bottom),
                )
                c = (s % halves) * width_a + (kp * 2 + s // halves) * shared + u
                vis_ref[pl.ds(c, low, stride=channels), :] = vis * (1.0 / nspec)

    def lines(h):
        def one(n, u):
            line_up(h * groups + n)
            return u

        lax.fori_loop(0, groups, one, 0, unroll=2)

    def middle(h, carry):
        arrive(2 * h + 1, h, 0, groups)
        lines(h)

        @pl.when(h == parts - 3)
        def _():
            lax.fori_loop(0, groups, correlate_early, 0)

        return carry

    def finish(n, u):
        line_up((parts - 1) * groups + n)
        correlate(n)
        return u

    arrive(0, 0, 0, head)
    arrive(1, 0, head, groups - head)
    lines(0)
    lax.fori_loop(1, parts - 1, middle, 0)
    arrive(2 * parts - 2, parts - 1, 0, tail)
    lax.fori_loop(0, tail, finish, 0, unroll=2)
    arrive(2 * parts - 1, parts - 1, tail, groups - tail)
    lax.fori_loop(tail, groups, finish, 0, unroll=2)

    piece = vis_ref.shape[0] // pieces

    def put(p):
        at = pl.ds(p * piece, piece)
        return pltpu.make_async_copy(half_ref.at[at], out_any.at[at], load_sem.at[p])

    for p in range(pieces):
        at = slice(p * piece, (p + 1) * piece)
        half_ref[at, :] = vis_ref[at, :].astype(BF16)
        put(p).start()
    for p in range(pieces):
        put(p).wait()


def turn_kernel(channels, pieces, vis_ref, out_any, out_ref, out_sem):
    half = out_ref.shape[0] // 2
    width = out_ref.shape[1]
    each = half // pieces

    def put(p, upper):
        at = pl.ds(p * each + upper * half, each)
        return pltpu.make_async_copy(out_ref.at[at], out_any.at[at], out_sem.at[upper, p])

    for p in range(pieces):
        def one_row(n, carry):
            i = p * each + n
            block = vis_ref[pl.ds(pl.multiple_of(i * channels, channels), channels), :]
            block = block.astype(F32).T.astype(BF16)
            out_ref[i] = block[:width]
            out_ref[i + half] = block[width:]
            return carry

        lax.fori_loop(0, each, one_row, 0, unroll=8)
        put(p, 0).start()
        put(p, 1).start()
    for p in range(pieces):
        put(p, 0).wait()
        put(p, 1).wait()


def kernel_body(peers, kept, samples, filter_coefs):
    in_local, total = samples.shape
    taps, nfft = filter_coefs.shape
    width_a = nfft // WIDTH_B
    nspec = total // nfft - taps + 1
    rows = width_a * in_local
    span = 16
    pieces = 4
    pad = 1
    parts = nspec // span
    groups = width_a * span // WIDTH_B
    head = 2
    tail = groups // 2
    chunks = 2 * parts
    per = 2 * (kept // peers)
    count = peers * in_local
    channels = width_a * per // 2
    x = samples.reshape(in_local, total // WIDTH_B, WIDTH_B).transpose(1, 0, 2)
    x = x.reshape(total // WIDTH_B * in_local, WIDTH_B)
    coefs = filter_coefs.reshape(taps, width_a, WIDTH_B).transpose(1, 0, 2)
    coefs = coefs.reshape(width_a * taps, WIDTH_B)
    first, twist, second = make_tables(in_local, width_a, kept)
    order = np.zeros((per, peers, in_local, peers, per, in_local), np.float32)
    for s in range(per):
        for p in range(peers):
            order[s, p, range(in_local), p, s, range(in_local)] = 1
    order = jnp.asarray(order.reshape(per * count, per * count), BF16)
    blocks = (peers, parts * groups, per * in_local, WIDTH_B)
    lines = (parts * groups, per * count, WIDTH_B)
    inputs = (x, coefs, first, twist, second, order)
    inputs = [pltpu.with_memory_space_constraint(a, pltpu.HBM) for a in inputs]
    vis = pl.pallas_call(
        functools.partial(
            correlator_kernel, (peers, in_local, nspec, taps, kept, span, head, tail, pieces, pad)
        ),
        out_shape=jax.ShapeDtypeStruct((count // 2 * channels, 2 * count), BF16),
        in_specs=[pl.BlockSpec(memory_space=pl.ANY)] * len(inputs),
        out_specs=pl.BlockSpec(memory_space=pl.ANY),
        scratch_shapes=[pltpu.VMEM(a.shape, a.dtype) for a in inputs] + [
            pltpu.VMEM((taps * rows, WIDTH_B), F32),
            pltpu.VMEM((rows * (span + pad), WIDTH_B), F32),
            pltpu.VMEM((rows * (span + pad), WIDTH_B), F32),
            pltpu.VMEM((2 * kept * in_local, WIDTH_B), F32),
            pltpu.VMEM(blocks, BF16),
            pltpu.VMEM(blocks, BF16),
            pltpu.VMEM(lines, BF16),
            pltpu.VMEM(lines, BF16),
            pltpu.VMEM((groups * per, per * count, WIDTH_B), F32),
            pltpu.VMEM((count // 2 * channels, 2 * count), F32),
            pltpu.VMEM((count // 2 * channels, 2 * count), BF16),
            pltpu.SemaphoreType.DMA((len(inputs) - 1,)),
            pltpu.SemaphoreType.DMA((parts + 1,)),
            pltpu.SemaphoreType.DMA((chunks, peers)),
            pltpu.SemaphoreType.DMA((chunks, peers)),
            pltpu.SemaphoreType.DMA,
        ],
        compiler_params=pltpu.CompilerParams(
            collective_id=0, has_side_effects=True, vmem_limit_bytes=48 * 2**20
        ),
        name="correlator",
    )(*inputs)
    out = pl.pallas_call(
        functools.partial(turn_kernel, channels, pieces),
        out_shape=jax.ShapeDtypeStruct((count, count, channels), BF16),
        in_specs=[pl.BlockSpec(memory_space=pltpu.VMEM)],
        out_specs=pl.BlockSpec(memory_space=pl.ANY),
        scratch_shapes=[
            pltpu.VMEM((count, count, channels), BF16),
            pltpu.SemaphoreType.DMA((2, pieces)),
        ],
        compiler_params=pltpu.CompilerParams(vmem_limit_bytes=16 * 2**20),
        name="turn",
    )(vis)
    return out.transpose(2, 0, 1)


def solution(mesh):
    peers = mesh.shape["inputs"]

    def body(samples, filter_coefs):
        in_local = samples.shape[0]
        kept = WIDTH_B // 4
        nfft = filter_coefs.shape[1]
        nspec = samples.shape[1] // nfft - filter_coefs.shape[0] + 1
        fits = kept % peers == 0 and 2 * peers * in_local == WIDTH_B
        fits = fits and nspec % 16 == 0 and nspec >= 64 and nfft % (32 * WIDTH_B) == 0
        if fits and (2 * in_local * (kept // peers)) % 16 == 0:
            return kernel_body(peers, kept, samples, filter_coefs)
        return plain_body(samples, filter_coefs)

    return jax.shard_map(
        body,
        mesh=mesh,
        in_specs=(P(("groups", "inputs"), None), P()),
        out_specs=P(("groups", "inputs"), None, None),
        check_vma=False,
    )
```

```python
import functools
import math

import jax
import jax.numpy as jnp
import numpy as np
from jax import lax
from jax.experimental import pallas as pl
from jax.experimental.pallas import tpu as pltpu
from jax.sharding import PartitionSpec as P


def phase_table(first, second, period):
    rows = lax.broadcasted_iota(jnp.int32, (first, second), 0)
    cols = lax.broadcasted_iota(jnp.int32, (first, second), 1)
    angle = 2.0 * math.pi / period * (rows * cols % period).astype(jnp.float32)
    return (jnp.cos(angle), -jnp.sin(angle))


def correlate_items(block):
    count = block.shape[0]
    nspec_local = block.shape[2] // 2
    rotated = jnp.concatenate([-block[..., nspec_local:], block[..., :nspec_local]], axis=-1)
    real_sum = jnp.einsum("ikt,jkt->kij", block, block, preferred_element_type=jnp.float32)
    imag_sum = jnp.einsum("ikt,jkt->kij", block, rotated, preferred_element_type=jnp.float32)
    rows = lax.broadcasted_iota(jnp.int32, (count, count), 0)
    cols = lax.broadcasted_iota(jnp.int32, (count, count), 1)
    return (jnp.where(rows >= cols, real_sum, imag_sum) / nspec_local).astype(jnp.bfloat16)


def correlate_turned(block):
    flat_block = block.reshape(block.shape[0], block.shape[2], block.shape[3])
    return correlate_items(flat_block)


def plain_body(samples, filter_coefs):
    in_local, total = samples.shape
    taps_count, nfft_local = filter_coefs.shape
    frame_count = total // nfft_local
    nspec_local = frame_count - taps_count + 1
    width_b = 128
    width_a = nfft_local // width_b
    kept_width = width_b // 4
    frames = samples.reshape(in_local, frame_count, nfft_local).astype(jnp.float32)
    filtered = filter_coefs[0] * frames[:, 0:nspec_local]
    for tap_index in range(1, taps_count):
        filtered = (
            filtered + filter_coefs[tap_index] * frames[:, tap_index : tap_index + nspec_local]
        )
    grid_view = filtered.astype(jnp.bfloat16).reshape(in_local, nspec_local, width_a, width_b)
    first_cos, first_sin = phase_table(width_a, width_a, width_a)
    first_table = jnp.concatenate([first_cos, first_sin], axis=1).astype(jnp.bfloat16)
    first_out = jnp.einsum(
        "itab,ak->itkb", grid_view, first_table, preferred_element_type=jnp.float32
    )
    real_one = first_out[:, :, :width_a]
    imag_one = first_out[:, :, width_a:]
    twist_cos, twist_sin = phase_table(width_a, width_b, nfft_local)
    real_two = real_one * twist_cos - imag_one * twist_sin
    imag_two = real_one * twist_sin + imag_one * twist_cos
    stacked = jnp.concatenate(
        [real_two.astype(jnp.bfloat16), imag_two.astype(jnp.bfloat16)], axis=3
    )
    second_cos, second_sin = phase_table(width_b, width_b, width_b)
    second_cos = second_cos[:, :kept_width]
    second_sin = second_sin[:, :kept_width]
    upper_rows = jnp.concatenate([second_cos, second_sin], axis=1)
    lower_rows = jnp.concatenate([-second_sin, second_cos], axis=1)
    second_table = jnp.concatenate([upper_rows, lower_rows], axis=0).astype(jnp.bfloat16)
    second_out = jnp.einsum(
        "itkn,nq->iqkt", stacked, second_table, preferred_element_type=jnp.float32
    )
    real_out = second_out[:, :kept_width]
    imag_out = second_out[:, kept_width:]
    channels = width_a * kept_width
    spectra = jnp.concatenate(
        [real_out.astype(jnp.bfloat16), imag_out.astype(jnp.bfloat16)], axis=3
    )
    spectra = spectra.reshape(in_local, channels, 2 * nspec_local)
    peers = lax.axis_size("inputs")
    per_peer = channels // peers
    owner_view = spectra.reshape(in_local, peers, per_peer, 2 * nspec_local)
    result = correlate_turned(
        lax.all_to_all(owner_view, "inputs", split_axis=1, concat_axis=0, tiled=True)
    )
    return result


WIDTH_B = 128
BF16 = jnp.bfloat16
F32 = jnp.float32
NT = (((1,), (1,)), ((), ()))


def np_phase(first, second, period):
    turns = np.outer(np.arange(first), np.arange(second)) % period
    angle = np.float32(2.0 * math.pi / period) * turns.astype(np.float32)
    return np.cos(angle), -np.sin(angle)


def make_tables(in_local, width_a, kept):
    nfft = width_a * WIDTH_B
    first = np.concatenate([t.T for t in np_phase(width_a, width_a, width_a)], axis=0)
    first = np.kron(first, np.eye(in_local, dtype=np.float32))
    twist = np.concatenate(
        [np.repeat(t, in_local, axis=0) for t in np_phase(width_a, WIDTH_B, nfft)], axis=0
    )
    cos_b, sin_b = (t[:, :kept].T for t in np_phase(WIDTH_B, WIDTH_B, WIDTH_B))
    second = np.concatenate(
        [np.concatenate([cos_b, -sin_b], axis=1), np.concatenate([sin_b, cos_b], axis=1)], axis=0
    )
    return jnp.asarray(first, BF16), jnp.asarray(twist, F32), jnp.asarray(second, BF16)


def correlator_kernel(
    dims, x_any, coef_any, first_any, twist_any, second_any, order_any, vis_ref,
    x_ref, coef_in, first_ref, twist_ref, second_ref, order_ref, coef_ref,
    real_ref, imag_ref, turn_ref, send_ref, recv_ref, line_ref, quad_ref, sum_ref,
    load_sem, x_sem, send_sem, recv_sem, own_sem,
):
    peers, in_local, nspec, taps, kept, span, head, tail, pieces, pad = dims
    rows = first_ref.shape[1]
    width_a = rows // in_local
    parts = nspec // span
    shared = WIDTH_B // (2 * span)
    wide = shared * span
    groups = width_a // (2 * shared)
    slot = span + pad
    me = lax.axis_index("inputs")

    def partner(n):
        return lax.rem(me + n + 1, peers)

    barrier = pltpu.get_barrier_semaphore()

    def greet(n, carry):
        pl.semaphore_signal(
            barrier, inc=1, device_id={"inputs": partner(n)},
            device_id_type=pl.DeviceIdType.MESH,
        )
        return carry


    def load_frames(start, count, n):
        at = pl.ds(start * rows, count * rows)
        return pltpu.make_async_copy(x_any.at[at], x_ref.at[at], x_sem.at[n])

    def load_part(h):
        return load_frames(h * span + taps - 1, span, h)

    small = [
        pltpu.make_async_copy(src, dst, load_sem.at[n])
        for n, (src, dst) in enumerate((
            (coef_any, coef_in), (first_any, first_ref), (twist_any, twist_ref),
            (second_any, second_ref), (order_any, order_ref),
        ))
    ]
    small[0].start()
    load_frames(0, taps - 1, parts).start()
    load_part(0).start()
    for copy in small[1:]:
        copy.start()
    for n in range(1, parts):
        load_part(n).start()
    lax.fori_loop(0, peers - 1, greet, 0)

    small[0].wait()
    for m in range(taps):
        tap = coef_in[pl.ds(m, width_a, stride=taps), :]
        for i in range(in_local):
            coef_ref[pl.ds(m * rows + i, width_a, stride=in_local), :] = tap
    for copy in small[1:]:
        copy.wait()
    load_frames(0, taps - 1, parts).wait()

    lane_block = 64

    def two_spectra(h, tp):
        late_t = tp * 2
        t = h * span + late_t
        filtered = []
        for r in range(0, rows, lane_block):
            frames = [
                x_ref[pl.ds(pl.multiple_of((t + m) * rows + r, lane_block), lane_block), :].astype(F32)
                for m in range(taps + 1)
            ]
            pair = []
            for late in range(2):
                acc = None
                for m in range(taps):
                    at = m * rows + r
                    term = coef_ref[at:at + lane_block, :] * frames[m + late]
                    acc = term if acc is None else acc + term
                pair.append(acc.astype(BF16))
            filtered.append(jnp.concatenate(pair, axis=1))
        filtered = jnp.concatenate(filtered, axis=0)
        out = jnp.dot(first_ref[...], filtered, preferred_element_type=F32)
        w_re, w_im = twist_ref[:rows, :], twist_ref[rows:, :]
        for late in range(2):
            cols = slice(late * WIDTH_B, (late + 1) * WIDTH_B)
            re, im = out[:rows, cols], out[rows:, cols]
            real_ref[pl.ds(late_t + late, rows, stride=slot), :] = re * w_re - im * w_im
            imag_ref[pl.ds(late_t + late, rows, stride=slot), :] = re * w_im + im * w_re

    per_dest = kept // peers * in_local

    def channel_group(h, kp):
        parts_out = []
        for kk in range(2):
            both = []
            for i in range(in_local):
                for u in range(shared):
                    k = (kp * 2 + kk) * shared + u
                    at = pl.ds((k * in_local + i) * slot, span)
                    both.append(jnp.concatenate(
                        [real_ref[at, :].astype(BF16), imag_ref[at, :].astype(BF16)], axis=1
                    ))
            both = jnp.concatenate(both, axis=0)
            res = lax.dot_general(second_ref[...], both, NT, preferred_element_type=F32)
            for i in range(in_local):
                cols = slice(i * wide, (i + 1) * wide)
                turn_ref[pl.ds(kk * kept * in_local + i, kept, stride=in_local), :] = (
                    jnp.concatenate([res[:kept, cols], res[kept:, cols]], axis=1)
                )
            part = turn_ref[kk * kept * in_local:(kk + 1) * kept * in_local, :]
            parts_out.append(part.reshape(peers, per_dest, WIDTH_B))
        send_ref[:, h * groups + kp] = jnp.concatenate(parts_out, axis=1).astype(BF16)

    def remote(c, h, start, size, n):
        dest = partner(n)
        at = pl.ds(h * groups + start, size)
        return pltpu.make_async_remote_copy(
            src_ref=send_ref.at[dest, at], dst_ref=recv_ref.at[me, at],
            send_sem=send_sem.at[c, n], recv_sem=recv_sem.at[c, n],
            device_id={"inputs": dest}, device_id_type=pl.DeviceIdType.MESH,
        )

    def push(c, h, start, size):
        def one(n, u):
            remote(c, h, start, size, n).start()
            return u

        lax.fori_loop(0, peers - 1, one, 0)

    def arrive(c, h, start, size):
        def one(n, u):
            remote(c, h, start, size, n).wait()
            return u

        lax.fori_loop(0, peers - 1, one, 0)

    def forward(h, carry):
        load_part(h).wait()

        def spectra(tp, u):
            two_spectra(h, tp)
            return u

        lax.fori_loop(0, span // 2, spectra, 0, unroll=4)

        def two_groups(n, u):
            channel_group(h, 2 * n)
            channel_group(h, 2 * n + 1)
            return u

        is_first = h == 0
        is_last = h == parts - 1
        cut = jnp.where(is_first, head // 2, 0)
        lax.fori_loop(0, cut, two_groups, 0)

        @pl.when(is_first)
        def _():
            pl.semaphore_wait(barrier, peers - 1)
            push(0, h, 0, head)

        def piece(j, u):
            lax.fori_loop(j * (tail // 2), (j + 1) * (tail // 2), two_groups, 0)
            push(2 * parts - 2 + j, h, j * tail, tail)
            return u

        lax.fori_loop(0, jnp.where(is_last, groups // tail, 0), piece, 0)
        lax.fori_loop(cut, jnp.where(is_last, 0, groups // 2), two_groups, 0)

        @pl.when(is_first)
        def _():
            push(1, h, head, groups - head)

        @pl.when(jnp.logical_not(is_first | is_last))
        def _():
            push(2 * h + 1, h, 0, groups)

        return carry

    lax.fori_loop(0, parts, forward, 0)
    own = pltpu.make_async_copy(send_ref.at[me], recv_ref.at[me], own_sem)
    own.start()
    own.wait()

    count = peers * in_local
    per = 2 * (kept // peers)
    halves = per // 2
    channels = width_a * halves
    low = count // 2
    i_at = lax.broadcasted_iota(jnp.int32, (low, WIDTH_B), 0)
    lane = lax.broadcasted_iota(jnp.int32, (low, WIDTH_B), 1)
    first_half = lane < count
    top_real = i_at >= lane
    low_real = i_at + low >= lane - count
    lane_row = lax.broadcasted_iota(jnp.int32, (count, WIDTH_B), 1)
    masks = [
        jnp.where((lane_row % wide) // span == u, 1.0, 0.0).astype(BF16) for u in range(shared)
    ]

    signs = jnp.where(
        lax.broadcasted_iota(jnp.int32, (per * count, WIDTH_B), 1) < wide, -1.0, 1.0
    )

    def swap(v):
        return pltpu.roll(v, wide, 1)

    def line_up(g):
        both = [recv_ref[:, g + n].reshape(per * count, WIDTH_B) for n in range(2)]
        lined = jnp.dot(
            order_ref[...], jnp.concatenate(both, axis=1), preferred_element_type=F32
        )
        for n in range(2):
            one = lined[:, n * WIDTH_B:(n + 1) * WIDTH_B]
            line_ref[g + n] = one.astype(BF16)
            quad_ref[g + n] = (swap(one) * signs).astype(BF16)

    def gram(kp, s, first, last):
        at = slice(s * count, (s + 1) * count)
        tiles = [line_ref[h * groups + kp, at, :] for h in range(first, last)]
        turned = [quad_ref[h * groups + kp, at, :] for h in range(first, last)]
        right = jnp.concatenate(
            [jnp.concatenate(tiles, axis=1), jnp.concatenate(turned, axis=1)], axis=0
        )
        left = jnp.concatenate(
            [jnp.concatenate([t * m for t in tiles], axis=1) for m in masks], axis=0
        )
        return lax.dot_general(left, right, NT, preferred_element_type=F32)

    def correlate_early(kp, u):
        for s in range(per):
            sum_ref[kp * per + s] = gram(kp, s, 0, parts - 2)
        return u

    def correlate(kp):
        for s in range(per):
            res = sum_ref[kp * per + s] + gram(kp, s, parts - 2, parts)
            for u in range(shared):
                top = res[u * count:u * count + low]
                bottom = res[u * count + low:(u + 1) * count]
                vis = jnp.where(
                    first_half,
                    jnp.where(top_real, top, swap(top)),
                    jnp.where(low_real, swap(bottom), bottom),
                )
                c = (s % halves) * width_a + (kp * 2 + s // halves) * shared + u
                vis_ref[pl.ds(c, low, stride=channels), :] = vis * (1.0 / nspec)

    def lines(h):
        def one(n, u):
            line_up(h * groups + 2 * n)
            return u

        lax.fori_loop(0, groups // 2, one, 0)

    def middle(h, carry):
        arrive(2 * h + 1, h, 0, groups)
        lines(h)

        @pl.when(h == parts - 3)
        def _():
            lax.fori_loop(0, groups, correlate_early, 0)

        return carry

    def finish(n, u):
        line_up((parts - 1) * groups + 2 * n)
        correlate(2 * n)
        correlate(2 * n + 1)
        return u

    def last_part(j, u):
        arrive(2 * parts - 2 + j, parts - 1, j * tail, tail)
        lax.fori_loop(j * (tail // 2), (j + 1) * (tail // 2), finish, 0)
        return u

    arrive(0, 0, 0, head)
    arrive(1, 0, head, groups - head)
    lines(0)
    lax.fori_loop(1, parts - 1, middle, 0)
    lax.fori_loop(0, groups // tail, last_part, 0)


def turn_kernel(channels, pieces, vis_ref, out_any, out_ref, out_sem):
    half = out_ref.shape[0] // 2
    width = out_ref.shape[1]
    each = half // pieces

    def put(p, upper):
        at = pl.ds(p * each + upper * half, each)
        return pltpu.make_async_copy(out_ref.at[at], out_any.at[at], out_sem.at[upper, p])

    for p in range(pieces):
        def one_row(n, carry):
            i = p * each + n
            block = vis_ref[pl.ds(pl.multiple_of(i * channels, channels), channels), :]
            block = block.T.astype(BF16)
            out_ref[i] = block[:width]
            out_ref[i + half] = block[width:]
            return carry

        lax.fori_loop(0, each, one_row, 0, unroll=8)
        put(p, 0).start()
        put(p, 1).start()
    for p in range(pieces):
        put(p, 0).wait()
        put(p, 1).wait()


def kernel_body(peers, kept, samples, filter_coefs):
    in_local, total = samples.shape
    taps, nfft = filter_coefs.shape
    width_a = nfft // WIDTH_B
    nspec = total // nfft - taps + 1
    rows = width_a * in_local
    span = 16
    pieces = 4
    pad = 1
    parts = nspec // span
    groups = width_a * span // WIDTH_B
    head = 2
    tail = 4
    chunks = 2 * parts - 2 + groups // tail
    per = 2 * (kept // peers)
    count = peers * in_local
    channels = width_a * per // 2
    x = samples.reshape(in_local, total // WIDTH_B, WIDTH_B).transpose(1, 0, 2)
    x = x.reshape(total // WIDTH_B * in_local, WIDTH_B)
    coefs = filter_coefs.reshape(taps, width_a, WIDTH_B).transpose(1, 0, 2)
    coefs = coefs.reshape(width_a * taps, WIDTH_B)
    first, twist, second = make_tables(in_local, width_a, kept)
    order = np.zeros((per, peers, in_local, peers, per, in_local), np.float32)
    for s in range(per):
        for p in range(peers):
            order[s, p, range(in_local), p, s, range(in_local)] = 1
    order = jnp.asarray(order.reshape(per * count, per * count), BF16)
    blocks = (peers, parts * groups, per * in_local, WIDTH_B)
    lines = (parts * groups, per * count, WIDTH_B)
    inputs = (x, coefs, first, twist, second, order)
    inputs = [pltpu.with_memory_space_constraint(a, pltpu.HBM) for a in inputs]
    vis = pl.pallas_call(
        functools.partial(
            correlator_kernel, (peers, in_local, nspec, taps, kept, span, head, tail, pieces, pad)
        ),
        out_shape=jax.ShapeDtypeStruct((count // 2 * channels, 2 * count), F32),
        in_specs=[pl.BlockSpec(memory_space=pl.ANY)] * len(inputs),
        out_specs=pl.BlockSpec(memory_space=pltpu.VMEM),
        scratch_shapes=[pltpu.VMEM(a.shape, a.dtype) for a in inputs] + [
            pltpu.VMEM((taps * rows, WIDTH_B), F32),
            pltpu.VMEM((rows * (span + pad), WIDTH_B), F32),
            pltpu.VMEM((rows * (span + pad), WIDTH_B), F32),
            pltpu.VMEM((2 * kept * in_local, WIDTH_B), F32),
            pltpu.VMEM(blocks, BF16),
            pltpu.VMEM(blocks, BF16),
            pltpu.VMEM(lines, BF16),
            pltpu.VMEM(lines, BF16),
            pltpu.VMEM((groups * per, per * count, WIDTH_B), F32),
            pltpu.SemaphoreType.DMA((len(inputs) - 1,)),
            pltpu.SemaphoreType.DMA((parts + 1,)),
            pltpu.SemaphoreType.DMA((chunks, peers)),
            pltpu.SemaphoreType.DMA((chunks, peers)),
            pltpu.SemaphoreType.DMA,
        ],
        compiler_params=pltpu.CompilerParams(
            collective_id=0, has_side_effects=True, vmem_limit_bytes=48 * 2**20
        ),
        name="correlator",
    )(*inputs)
    out = pl.pallas_call(
        functools.partial(turn_kernel, channels, pieces),
        out_shape=jax.ShapeDtypeStruct((count, count, channels), BF16),
        in_specs=[pl.BlockSpec(memory_space=pltpu.VMEM)],
        out_specs=pl.BlockSpec(memory_space=pl.ANY),
        scratch_shapes=[
            pltpu.VMEM((count, count, channels), BF16),
            pltpu.SemaphoreType.DMA((2, pieces)),
        ],
        compiler_params=pltpu.CompilerParams(vmem_limit_bytes=16 * 2**20),
        name="turn",
    )(vis)
    return out.transpose(2, 0, 1)


def solution(mesh):
    peers = mesh.shape["inputs"]

    def body(samples, filter_coefs):
        in_local = samples.shape[0]
        kept = WIDTH_B // 4
        nfft = filter_coefs.shape[1]
        nspec = samples.shape[1] // nfft - filter_coefs.shape[0] + 1
        fits = kept % peers == 0 and 2 * peers * in_local == WIDTH_B
        fits = fits and nspec % 16 == 0 and nspec >= 64 and nfft % (32 * WIDTH_B) == 0
        if fits and (2 * in_local * (kept // peers)) % 16 == 0:
            return kernel_body(peers, kept, samples, filter_coefs)
        return plain_body(samples, filter_coefs)

    return jax.shard_map(
        body,
        mesh=mesh,
        in_specs=(P(("groups", "inputs"), None), P()),
        out_specs=P(("groups", "inputs"), None, None),
        check_vma=False,
    )
```

```python
import functools
import math

import jax
import jax.numpy as jnp
import numpy as np
from jax import lax
from jax.experimental import pallas as pl
from jax.experimental.pallas import tpu as pltpu
from jax.sharding import PartitionSpec as P


def phase_table(first, second, period):
    rows = lax.broadcasted_iota(jnp.int32, (first, second), 0)
    cols = lax.broadcasted_iota(jnp.int32, (first, second), 1)
    angle = 2.0 * math.pi / period * (rows * cols % period).astype(jnp.float32)
    return (jnp.cos(angle), -jnp.sin(angle))


def correlate_items(block):
    count = block.shape[0]
    nspec_local = block.shape[2] // 2
    rotated = jnp.concatenate([-block[..., nspec_local:], block[..., :nspec_local]], axis=-1)
    real_sum = jnp.einsum("ikt,jkt->kij", block, block, preferred_element_type=jnp.float32)
    imag_sum = jnp.einsum("ikt,jkt->kij", block, rotated, preferred_element_type=jnp.float32)
    rows = lax.broadcasted_iota(jnp.int32, (count, count), 0)
    cols = lax.broadcasted_iota(jnp.int32, (count, count), 1)
    return (jnp.where(rows >= cols, real_sum, imag_sum) / nspec_local).astype(jnp.bfloat16)


def correlate_turned(block):
    flat_block = block.reshape(block.shape[0], block.shape[2], block.shape[3])
    return correlate_items(flat_block)


def plain_body(samples, filter_coefs):
    in_local, total = samples.shape
    taps_count, nfft_local = filter_coefs.shape
    frame_count = total // nfft_local
    nspec_local = frame_count - taps_count + 1
    width_b = 128
    width_a = nfft_local // width_b
    kept_width = width_b // 4
    frames = samples.reshape(in_local, frame_count, nfft_local).astype(jnp.float32)
    filtered = filter_coefs[0] * frames[:, 0:nspec_local]
    for tap_index in range(1, taps_count):
        filtered = (
            filtered + filter_coefs[tap_index] * frames[:, tap_index : tap_index + nspec_local]
        )
    grid_view = filtered.astype(jnp.bfloat16).reshape(in_local, nspec_local, width_a, width_b)
    first_cos, first_sin = phase_table(width_a, width_a, width_a)
    first_table = jnp.concatenate([first_cos, first_sin], axis=1).astype(jnp.bfloat16)
    first_out = jnp.einsum(
        "itab,ak->itkb", grid_view, first_table, preferred_element_type=jnp.float32
    )
    real_one = first_out[:, :, :width_a]
    imag_one = first_out[:, :, width_a:]
    twist_cos, twist_sin = phase_table(width_a, width_b, nfft_local)
    real_two = real_one * twist_cos - imag_one * twist_sin
    imag_two = real_one * twist_sin + imag_one * twist_cos
    stacked = jnp.concatenate(
        [real_two.astype(jnp.bfloat16), imag_two.astype(jnp.bfloat16)], axis=3
    )
    second_cos, second_sin = phase_table(width_b, width_b, width_b)
    second_cos = second_cos[:, :kept_width]
    second_sin = second_sin[:, :kept_width]
    upper_rows = jnp.concatenate([second_cos, second_sin], axis=1)
    lower_rows = jnp.concatenate([-second_sin, second_cos], axis=1)
    second_table = jnp.concatenate([upper_rows, lower_rows], axis=0).astype(jnp.bfloat16)
    second_out = jnp.einsum(
        "itkn,nq->iqkt", stacked, second_table, preferred_element_type=jnp.float32
    )
    real_out = second_out[:, :kept_width]
    imag_out = second_out[:, kept_width:]
    channels = width_a * kept_width
    spectra = jnp.concatenate(
        [real_out.astype(jnp.bfloat16), imag_out.astype(jnp.bfloat16)], axis=3
    )
    spectra = spectra.reshape(in_local, channels, 2 * nspec_local)
    peers = lax.axis_size("inputs")
    per_peer = channels // peers
    owner_view = spectra.reshape(in_local, peers, per_peer, 2 * nspec_local)
    result = correlate_turned(
        lax.all_to_all(owner_view, "inputs", split_axis=1, concat_axis=0, tiled=True)
    )
    return result


WIDTH_B = 128
BF16 = jnp.bfloat16
F32 = jnp.float32
NT = (((1,), (1,)), ((), ()))


def np_phase(first, second, period):
    turns = np.outer(np.arange(first), np.arange(second)) % period
    angle = np.float32(2.0 * math.pi / period) * turns.astype(np.float32)
    return np.cos(angle), -np.sin(angle)


def make_tables(in_local, width_a, kept):
    nfft = width_a * WIDTH_B
    first = np.concatenate([t.T for t in np_phase(width_a, width_a, width_a)], axis=0)
    first = np.kron(first, np.eye(in_local, dtype=np.float32))
    twist = np.concatenate(
        [np.repeat(t, in_local, axis=0) for t in np_phase(width_a, WIDTH_B, nfft)], axis=0
    )
    cos_b, sin_b = (t[:, :kept].T for t in np_phase(WIDTH_B, WIDTH_B, WIDTH_B))
    second = np.concatenate(
        [np.concatenate([cos_b, -sin_b], axis=1), np.concatenate([sin_b, cos_b], axis=1)], axis=0
    )
    return jnp.asarray(first, BF16), jnp.asarray(twist, F32), jnp.asarray(second, BF16)


def correlator_kernel(
    dims, x_any, coef_any, first_any, twist_any, second_any, order_any, vis_ref,
    x_ref, coef_in, first_ref, twist_ref, second_ref, order_ref, coef_ref,
    real_ref, imag_ref, turn_ref, send_ref, recv_ref, line_ref, quad_ref, sum_ref,
    load_sem, x_sem, send_sem, recv_sem, own_sem,
):
    peers, in_local, nspec, taps, kept, span, head, tail, pieces, pad = dims
    rows = first_ref.shape[1]
    width_a = rows // in_local
    parts = nspec // span
    shared = WIDTH_B // (2 * span)
    wide = shared * span
    groups = width_a // (2 * shared)
    slot = span + pad
    ahead = 2
    me = lax.axis_index("inputs")

    def partner(n):
        return lax.rem(me + n + 1, peers)

    barrier = pltpu.get_barrier_semaphore()

    def greet(n, carry):
        pl.semaphore_signal(
            barrier, inc=1, device_id={"inputs": partner(n)},
            device_id_type=pl.DeviceIdType.MESH,
        )
        return carry


    def load_frames(start, count, n):
        at = pl.ds(start * rows, count * rows)
        return pltpu.make_async_copy(x_any.at[at], x_ref.at[at], x_sem.at[n])

    def load_part(h):
        return load_frames(h * span + taps - 1, span, h)

    small = [
        pltpu.make_async_copy(src, dst, load_sem.at[n])
        for n, (src, dst) in enumerate((
            (coef_any, coef_in), (first_any, first_ref), (twist_any, twist_ref),
            (second_any, second_ref), (order_any, order_ref),
        ))
    ]
    small[0].start()
    load_frames(0, taps - 1, parts).start()
    load_part(0).start()
    for copy in small[1:-1]:
        copy.start()
    lax.fori_loop(0, peers - 1, greet, 0)

    small[0].wait()
    for m in range(taps):
        tap = coef_in[pl.ds(m, width_a, stride=taps), :]
        for i in range(in_local):
            coef_ref[pl.ds(m * rows + i, width_a, stride=in_local), :] = tap
    for copy in small[1:-1]:
        copy.wait()
    load_frames(0, taps - 1, parts).wait()

    lane_block = 64

    def two_spectra(h, tp):
        late_t = tp * 2
        t = h * span + late_t
        filtered = []
        for r in range(0, rows, lane_block):
            frames = [
                x_ref[pl.ds(pl.multiple_of((t + m) * rows + r, lane_block), lane_block), :].astype(F32)
                for m in range(taps + 1)
            ]
            pair = []
            for late in range(2):
                acc = None
                for m in range(taps):
                    at = m * rows + r
                    term = coef_ref[at:at + lane_block, :] * frames[m + late]
                    acc = term if acc is None else acc + term
                pair.append(acc.astype(BF16))
            filtered.append(jnp.concatenate(pair, axis=1))
        filtered = jnp.concatenate(filtered, axis=0)
        out = jnp.dot(first_ref[...], filtered, preferred_element_type=F32)
        w_re, w_im = twist_ref[:rows, :], twist_ref[rows:, :]
        for late in range(2):
            cols = slice(late * WIDTH_B, (late + 1) * WIDTH_B)
            re, im = out[:rows, cols], out[rows:, cols]
            real_ref[pl.ds(late_t + late, rows, stride=slot), :] = re * w_re - im * w_im
            imag_ref[pl.ds(late_t + late, rows, stride=slot), :] = re * w_im + im * w_re

    per_dest = kept // peers * in_local

    def channel_group(h, kp):
        parts_out = []
        for kk in range(2):
            both = []
            for i in range(in_local):
                for u in range(shared):
                    k = (kp * 2 + kk) * shared + u
                    at = pl.ds((k * in_local + i) * slot, span)
                    both.append(jnp.concatenate(
                        [real_ref[at, :].astype(BF16), imag_ref[at, :].astype(BF16)], axis=1
                    ))
            both = jnp.concatenate(both, axis=0)
            res = lax.dot_general(second_ref[...], both, NT, preferred_element_type=F32)
            for i in range(in_local):
                cols = slice(i * wide, (i + 1) * wide)
                turn_ref[pl.ds(kk * kept * in_local + i, kept, stride=in_local), :] = (
                    jnp.concatenate([res[:kept, cols], res[kept:, cols]], axis=1)
                )
            part = turn_ref[kk * kept * in_local:(kk + 1) * kept * in_local, :]
            parts_out.append(part.reshape(peers, per_dest, WIDTH_B))
        send_ref[:, h * groups + kp] = jnp.concatenate(parts_out, axis=1).astype(BF16)

    def remote(c, h, start, size, n):
        dest = partner(n)
        at = pl.ds(h * groups + start, size)
        return pltpu.make_async_remote_copy(
            src_ref=send_ref.at[dest, at], dst_ref=recv_ref.at[me, at],
            send_sem=send_sem.at[c, n], recv_sem=recv_sem.at[c, n],
            device_id={"inputs": dest}, device_id_type=pl.DeviceIdType.MESH,
        )

    def push(c, h, start, size):
        def one(n, u):
            remote(c, h, start, size, n).start()
            return u

        lax.fori_loop(0, peers - 1, one, 0)

    def arrive(c, h, start, size):
        def one(n, u):
            remote(c, h, start, size, n).wait()
            return u

        lax.fori_loop(0, peers - 1, one, 0)

    def forward(h, carry):
        load_part(h).wait()

        @pl.when(h < parts - 1)
        def _():
            load_part(h + 1).start()

        def spectra(tp, u):
            two_spectra(h, tp)
            return u

        lax.fori_loop(0, span // 2, spectra, 0, unroll=4)

        def two_groups(n, u):
            channel_group(h, 2 * n)
            channel_group(h, 2 * n + 1)
            return u

        is_first = h == 0
        is_last = h == parts - 1
        cut = jnp.where(is_first, head // 2, 0)
        lax.fori_loop(0, cut, two_groups, 0)

        @pl.when(is_first)
        def _():
            pl.semaphore_wait(barrier, peers - 1)
            push(0, h, 0, head)

        lax.fori_loop(cut, groups // 2, two_groups, 0)

        @pl.when(is_first)
        def _():
            push(1, h, head, groups - head)

        @pl.when(is_last)
        def _():
            def piece(q, u):
                later = q // (groups // tail)
                j = q % (groups // tail)

                def one(n, v):
                    @pl.when((partner(n) >= ahead) == (later == 1))
                    def _():
                        remote(2 * parts - 2 + j, h, j * tail, tail, n).start()

                    return v

                return lax.fori_loop(0, peers - 1, one, u)

            lax.fori_loop(0, 2 * (groups // tail), piece, 0)

        @pl.when(jnp.logical_not(is_first | is_last))
        def _():
            push(2 * h + 1, h, 0, groups)

        return carry

    lax.fori_loop(0, parts, forward, 0)
    small[-1].start()
    small[-1].wait()
    own = pltpu.make_async_copy(send_ref.at[me], recv_ref.at[me], own_sem)
    own.start()
    own.wait()

    count = peers * in_local
    per = 2 * (kept // peers)
    halves = per // 2
    channels = width_a * halves
    low = count // 2
    i_at = lax.broadcasted_iota(jnp.int32, (low, WIDTH_B), 0)
    lane = lax.broadcasted_iota(jnp.int32, (low, WIDTH_B), 1)
    first_half = lane < count
    top_real = i_at >= lane
    low_real = i_at + low >= lane - count
    lane_row = lax.broadcasted_iota(jnp.int32, (count, WIDTH_B), 1)
    masks = [
        jnp.where((lane_row % wide) // span == u, 1.0, 0.0).astype(BF16) for u in range(shared)
    ]

    signs = jnp.where(
        lax.broadcasted_iota(jnp.int32, (per * count, WIDTH_B), 1) < wide, -1.0, 1.0
    )

    def swap(v):
        return pltpu.roll(v, wide, 1)

    def line_up(g):
        both = [recv_ref[:, g + n].reshape(per * count, WIDTH_B) for n in range(2)]
        lined = jnp.dot(
            order_ref[...], jnp.concatenate(both, axis=1), preferred_element_type=F32
        )
        for n in range(2):
            one = lined[:, n * WIDTH_B:(n + 1) * WIDTH_B]
            line_ref[g + n] = one.astype(BF16)
            quad_ref[g + n] = (swap(one) * signs).astype(BF16)

    def gram(kp, s, first, last):
        at = slice(s * count, (s + 1) * count)
        tiles = [line_ref[h * groups + kp, at, :] for h in range(first, last)]
        turned = [quad_ref[h * groups + kp, at, :] for h in range(first, last)]
        right = jnp.concatenate(
            [jnp.concatenate(tiles, axis=1), jnp.concatenate(turned, axis=1)], axis=0
        )
        left = jnp.concatenate(
            [jnp.concatenate([t * m for t in tiles], axis=1) for m in masks], axis=0
        )
        return lax.dot_general(left, right, NT, preferred_element_type=F32)

    def correlate_early(kp, u):
        for s in range(per):
            sum_ref[kp * per + s] = gram(kp, s, 0, parts - 2)
        return u

    def correlate(kp):
        for s in range(per):
            res = sum_ref[kp * per + s] + gram(kp, s, parts - 2, parts)
            for u in range(shared):
                top = res[u * count:u * count + low]
                bottom = res[u * count + low:(u + 1) * count]
                vis = jnp.where(
                    first_half,
                    jnp.where(top_real, top, swap(top)),
                    jnp.where(low_real, swap(bottom), bottom),
                )
                c = (s % halves) * width_a + (kp * 2 + s // halves) * shared + u
                vis_ref[pl.ds(c, low, stride=channels), :] = vis * (1.0 / nspec)

    def lines(h):
        def one(n, u):
            line_up(h * groups + 2 * n)
            return u

        lax.fori_loop(0, groups // 2, one, 0)

    def middle(h, carry):
        arrive(2 * h + 1, h, 0, groups)
        lines(h)

        @pl.when(h == parts - 3)
        def _():
            lax.fori_loop(0, groups, correlate_early, 0, unroll=2)

        return carry

    def finish(n, u):
        line_up((parts - 1) * groups + 2 * n)
        correlate(2 * n)
        correlate(2 * n + 1)
        return u

    def last_part(j, u):
        arrive(2 * parts - 2 + j, parts - 1, j * tail, tail)
        for n in range(tail // 2):
            finish(j * (tail // 2) + n, 0)
        return u

    arrive(0, 0, 0, head)
    arrive(1, 0, head, groups - head)
    lines(0)
    lax.fori_loop(1, parts - 1, middle, 0)
    lax.fori_loop(0, groups // tail, last_part, 0)


def turn_kernel(channels, pieces, vis_ref, out_any, out_ref, out_sem):
    half = out_ref.shape[0] // 2
    width = out_ref.shape[1]
    each = half // pieces

    def put(p, upper):
        at = pl.ds(p * each + upper * half, each)
        return pltpu.make_async_copy(out_ref.at[at], out_any.at[at], out_sem.at[upper, p])

    for p in range(pieces):
        def one_row(n, carry):
            i = p * each + n
            block = vis_ref[pl.ds(pl.multiple_of(i * channels, channels), channels), :]
            block = block.T.astype(BF16)
            out_ref[i] = block[:width]
            out_ref[i + half] = block[width:]
            return carry

        lax.fori_loop(0, each, one_row, 0, unroll=8)
        put(p, 0).start()
        put(p, 1).start()
    for p in range(pieces):
        put(p, 0).wait()
        put(p, 1).wait()


def kernel_body(peers, kept, samples, filter_coefs):
    in_local, total = samples.shape
    taps, nfft = filter_coefs.shape
    width_a = nfft // WIDTH_B
    nspec = total // nfft - taps + 1
    rows = width_a * in_local
    span = 16
    pieces = 4
    pad = 1
    parts = nspec // span
    groups = width_a * span // WIDTH_B
    head = 2
    tail = 4
    chunks = 2 * parts - 2 + groups // tail
    per = 2 * (kept // peers)
    count = peers * in_local
    channels = width_a * per // 2
    x = samples.reshape(in_local, total // WIDTH_B, WIDTH_B).transpose(1, 0, 2)
    x = x.reshape(total // WIDTH_B * in_local, WIDTH_B)
    coefs = filter_coefs.reshape(taps, width_a, WIDTH_B).transpose(1, 0, 2)
    coefs = coefs.reshape(width_a * taps, WIDTH_B)
    first, twist, second = make_tables(in_local, width_a, kept)
    order = np.zeros((per, peers, in_local, peers, per, in_local), np.float32)
    for s in range(per):
        for p in range(peers):
            order[s, p, range(in_local), p, s, range(in_local)] = 1
    order = jnp.asarray(order.reshape(per * count, per * count), BF16)
    blocks = (peers, parts * groups, per * in_local, WIDTH_B)
    lines = (parts * groups, per * count, WIDTH_B)
    inputs = (x, coefs, first, twist, second, order)
    inputs = [pltpu.with_memory_space_constraint(a, pltpu.HBM) for a in inputs]
    vis = pl.pallas_call(
        functools.partial(
            correlator_kernel, (peers, in_local, nspec, taps, kept, span, head, tail, pieces, pad)
        ),
        out_shape=jax.ShapeDtypeStruct((count // 2 * channels, 2 * count), F32),
        in_specs=[pl.BlockSpec(memory_space=pl.ANY)] * len(inputs),
        out_specs=pl.BlockSpec(memory_space=pltpu.VMEM),
        scratch_shapes=[pltpu.VMEM(a.shape, a.dtype) for a in inputs] + [
            pltpu.VMEM((taps * rows, WIDTH_B), F32),
            pltpu.VMEM((rows * (span + pad), WIDTH_B), F32),
            pltpu.VMEM((rows * (span + pad), WIDTH_B), F32),
            pltpu.VMEM((2 * kept * in_local, WIDTH_B), F32),
            pltpu.VMEM(blocks, BF16),
            pltpu.VMEM(blocks, BF16),
            pltpu.VMEM(lines, BF16),
            pltpu.VMEM(lines, BF16),
            pltpu.VMEM((groups * per, per * count, WIDTH_B), F32),
            pltpu.SemaphoreType.DMA((len(inputs) - 1,)),
            pltpu.SemaphoreType.DMA((parts + 1,)),
            pltpu.SemaphoreType.DMA((chunks, peers)),
            pltpu.SemaphoreType.DMA((chunks, peers)),
            pltpu.SemaphoreType.DMA,
        ],
        compiler_params=pltpu.CompilerParams(
            collective_id=0, has_side_effects=True, vmem_limit_bytes=48 * 2**20
        ),
        name="correlator",
    )(*inputs)
    out = pl.pallas_call(
        functools.partial(turn_kernel, channels, pieces),
        out_shape=jax.ShapeDtypeStruct((count, count, channels), BF16),
        in_specs=[pl.BlockSpec(memory_space=pltpu.VMEM)],
        out_specs=pl.BlockSpec(memory_space=pl.ANY),
        scratch_shapes=[
            pltpu.VMEM((count, count, channels), BF16),
            pltpu.SemaphoreType.DMA((2, pieces)),
        ],
        compiler_params=pltpu.CompilerParams(vmem_limit_bytes=16 * 2**20),
        name="turn",
    )(vis)
    return out.transpose(2, 0, 1)


def solution(mesh):
    peers = mesh.shape["inputs"]

    def body(samples, filter_coefs):
        in_local = samples.shape[0]
        kept = WIDTH_B // 4
        nfft = filter_coefs.shape[1]
        nspec = samples.shape[1] // nfft - filter_coefs.shape[0] + 1
        fits = kept % peers == 0 and 2 * peers * in_local == WIDTH_B
        fits = fits and nspec % 16 == 0 and nspec >= 64 and nfft % (32 * WIDTH_B) == 0
        if fits and (2 * in_local * (kept // peers)) % 16 == 0:
            return kernel_body(peers, kept, samples, filter_coefs)
        return plain_body(samples, filter_coefs)

    return jax.shard_map(
        body,
        mesh=mesh,
        in_specs=(P(("groups", "inputs"), None), P()),
        out_specs=P(("groups", "inputs"), None, None),
        check_vma=False,
    )
```

```python
import functools
import math

import jax
import jax.numpy as jnp
import numpy as np
from jax import lax
from jax.experimental import pallas as pl
from jax.experimental.pallas import tpu as pltpu
from jax.sharding import PartitionSpec as P


def phase_table(first, second, period):
    rows = lax.broadcasted_iota(jnp.int32, (first, second), 0)
    cols = lax.broadcasted_iota(jnp.int32, (first, second), 1)
    angle = 2.0 * math.pi / period * (rows * cols % period).astype(jnp.float32)
    return (jnp.cos(angle), -jnp.sin(angle))


def correlate_items(block):
    count = block.shape[0]
    nspec_local = block.shape[2] // 2
    rotated = jnp.concatenate([-block[..., nspec_local:], block[..., :nspec_local]], axis=-1)
    real_sum = jnp.einsum("ikt,jkt->kij", block, block, preferred_element_type=jnp.float32)
    imag_sum = jnp.einsum("ikt,jkt->kij", block, rotated, preferred_element_type=jnp.float32)
    rows = lax.broadcasted_iota(jnp.int32, (count, count), 0)
    cols = lax.broadcasted_iota(jnp.int32, (count, count), 1)
    return (jnp.where(rows >= cols, real_sum, imag_sum) / nspec_local).astype(jnp.bfloat16)


def correlate_turned(block):
    flat_block = block.reshape(block.shape[0], block.shape[2], block.shape[3])
    return correlate_items(flat_block)


def plain_body(samples, filter_coefs):
    in_local, total = samples.shape
    taps_count, nfft_local = filter_coefs.shape
    frame_count = total // nfft_local
    nspec_local = frame_count - taps_count + 1
    width_b = 128
    width_a = nfft_local // width_b
    kept_width = width_b // 4
    frames = samples.reshape(in_local, frame_count, nfft_local).astype(jnp.float32)
    filtered = filter_coefs[0] * frames[:, 0:nspec_local]
    for tap_index in range(1, taps_count):
        filtered = (
            filtered + filter_coefs[tap_index] * frames[:, tap_index : tap_index + nspec_local]
        )
    grid_view = filtered.astype(jnp.bfloat16).reshape(in_local, nspec_local, width_a, width_b)
    first_cos, first_sin = phase_table(width_a, width_a, width_a)
    first_table = jnp.concatenate([first_cos, first_sin], axis=1).astype(jnp.bfloat16)
    first_out = jnp.einsum(
        "itab,ak->itkb", grid_view, first_table, preferred_element_type=jnp.float32
    )
    real_one = first_out[:, :, :width_a]
    imag_one = first_out[:, :, width_a:]
    twist_cos, twist_sin = phase_table(width_a, width_b, nfft_local)
    real_two = real_one * twist_cos - imag_one * twist_sin
    imag_two = real_one * twist_sin + imag_one * twist_cos
    stacked = jnp.concatenate(
        [real_two.astype(jnp.bfloat16), imag_two.astype(jnp.bfloat16)], axis=3
    )
    second_cos, second_sin = phase_table(width_b, width_b, width_b)
    second_cos = second_cos[:, :kept_width]
    second_sin = second_sin[:, :kept_width]
    upper_rows = jnp.concatenate([second_cos, second_sin], axis=1)
    lower_rows = jnp.concatenate([-second_sin, second_cos], axis=1)
    second_table = jnp.concatenate([upper_rows, lower_rows], axis=0).astype(jnp.bfloat16)
    second_out = jnp.einsum(
        "itkn,nq->iqkt", stacked, second_table, preferred_element_type=jnp.float32
    )
    real_out = second_out[:, :kept_width]
    imag_out = second_out[:, kept_width:]
    channels = width_a * kept_width
    spectra = jnp.concatenate(
        [real_out.astype(jnp.bfloat16), imag_out.astype(jnp.bfloat16)], axis=3
    )
    spectra = spectra.reshape(in_local, channels, 2 * nspec_local)
    peers = lax.axis_size("inputs")
    per_peer = channels // peers
    owner_view = spectra.reshape(in_local, peers, per_peer, 2 * nspec_local)
    result = correlate_turned(
        lax.all_to_all(owner_view, "inputs", split_axis=1, concat_axis=0, tiled=True)
    )
    return result


WIDTH_B = 128
BF16 = jnp.bfloat16
F32 = jnp.float32
NT = (((1,), (1,)), ((), ()))


def np_phase(first, second, period):
    turns = np.outer(np.arange(first), np.arange(second)) % period
    angle = np.float32(2.0 * math.pi / period) * turns.astype(np.float32)
    return np.cos(angle), -np.sin(angle)


def make_tables(in_local, width_a, kept):
    nfft = width_a * WIDTH_B
    half = width_a // 2
    cos_a, sin_a = (t.T for t in np_phase(width_a, width_a, width_a))
    first = np.concatenate([cos_a[:half + 1], sin_a[1:half]], axis=0)
    first = np.kron(first, np.eye(in_local, dtype=np.float32))
    mirrored = [*range(half + 1), *range(width_a - 1, half, -1)]
    twist = np.concatenate(
        [np.repeat(t[mirrored], in_local, axis=0) for t in np_phase(width_a, WIDTH_B, nfft)],
        axis=0,
    )
    cos_b, sin_b = (t[:, :kept].T for t in np_phase(WIDTH_B, WIDTH_B, WIDTH_B))
    second = np.concatenate(
        [np.concatenate([cos_b, -sin_b], axis=1), np.concatenate([sin_b, cos_b], axis=1)], axis=0
    )
    return jnp.asarray(first, BF16), jnp.asarray(twist, F32), jnp.asarray(second, BF16)


def correlator_kernel(
    dims, x_any, coef_any, first_any, twist_any, second_any, order_any, vis_ref,
    x_ref, coef_in, first_ref, twist_ref, second_ref, order_ref, coef_ref,
    real_ref, imag_ref, turn_ref, send_ref, recv_ref, line_ref, quad_ref, sum_ref,
    load_sem, x_sem, send_sem, recv_sem, own_sem,
):
    peers, in_local, nspec, taps, kept, span, head, tail, pieces, pad = dims
    rows = first_ref.shape[1]
    width_a = rows // in_local
    parts = nspec // span
    shared = WIDTH_B // (2 * span)
    wide = shared * span
    groups = width_a // (2 * shared)
    slot = rows + pad
    ahead = 2
    me = lax.axis_index("inputs")

    def partner(n):
        return lax.rem(me + n + 1, peers)

    barrier = pltpu.get_barrier_semaphore()

    def greet(n, carry):
        pl.semaphore_signal(
            barrier, inc=1, device_id={"inputs": partner(n)},
            device_id_type=pl.DeviceIdType.MESH,
        )
        return carry


    def load_frames(start, count, n):
        at = pl.ds(start * rows, count * rows)
        return pltpu.make_async_copy(x_any.at[at], x_ref.at[at], x_sem.at[n])

    def load_part(h):
        return load_frames(h * span + taps - 1, span, h)

    small = [
        pltpu.make_async_copy(src, dst, load_sem.at[n])
        for n, (src, dst) in enumerate((
            (coef_any, coef_in), (first_any, first_ref), (twist_any, twist_ref),
            (second_any, second_ref), (order_any, order_ref),
        ))
    ]
    small[0].start()
    load_frames(0, taps - 1, parts).start()
    load_part(0).start()
    for copy in small[1:-1]:
        copy.start()
    lax.fori_loop(0, peers - 1, greet, 0)

    small[0].wait()
    for m in range(taps):
        tap = coef_in[pl.ds(m, width_a, stride=taps), :]
        for i in range(in_local):
            coef_ref[pl.ds(m * rows + i, width_a, stride=in_local), :] = tap
    for copy in small[1:-1]:
        copy.wait()
    load_frames(0, taps - 1, parts).wait()

    lane_block = 64
    low_rows = rows // 2
    edge = lax.broadcasted_iota(jnp.int32, (8, WIDTH_B), 0) < in_local

    def two_spectra(h, tp):
        late_t = tp * 2
        t = h * span + late_t
        filtered = []
        for r in range(0, rows, lane_block):
            frames = [
                x_ref[pl.ds(pl.multiple_of((t + m) * rows + r, lane_block), lane_block), :].astype(F32)
                for m in range(taps + 1)
            ]
            pair = []
            for late in range(2):
                acc = None
                for m in range(taps):
                    at = m * rows + r
                    term = coef_ref[at:at + lane_block, :] * frames[m + late]
                    acc = term if acc is None else acc + term
                pair.append(acc.astype(BF16))
            filtered.append(jnp.concatenate(pair, axis=1))
        filtered = jnp.concatenate(filtered, axis=0)
        out = jnp.dot(first_ref[...], filtered, preferred_element_type=F32)
        w_re, w_im = twist_ref[:low_rows, :], twist_ref[rows:rows + low_rows, :]
        v_re, v_im = twist_ref[low_rows:rows, :], twist_ref[rows + low_rows:, :]
        for late in range(2):
            cols = slice(late * WIDTH_B, (late + 1) * WIDTH_B)
            re, im = out[:low_rows, cols], out[low_rows:, cols]
            mirror = jnp.concatenate([jnp.where(edge, im[:8], re[:8]), re[8:]], axis=0)
            im = jnp.concatenate([jnp.where(edge, 0.0, im[:8]), im[8:]], axis=0)
            at = pl.ds(pl.multiple_of((late_t + late) * slot, 8), low_rows)
            real_ref[at, :] = re * w_re - im * w_im
            imag_ref[at, :] = re * w_im + im * w_re
            at = pl.ds(pl.multiple_of((late_t + late) * slot + low_rows, 8), low_rows)
            real_ref[at, :] = mirror * v_re + im * v_im
            imag_ref[at, :] = mirror * v_im - im * v_re

    per_dest = kept // peers * in_local

    def channel_group(h, kp):
        parts_out = []
        for kk in range(2):
            both = []
            for i in range(in_local):
                for u in range(shared):
                    k = (kp * 2 + kk) * shared + u
                    k = jnp.where(k <= width_a // 2, k, width_a // 2 * 3 - k)
                    at = pl.ds(k * in_local + i, span, stride=slot)
                    both.append(jnp.concatenate(
                        [real_ref[at, :].astype(BF16), imag_ref[at, :].astype(BF16)], axis=1
                    ))
            both = jnp.concatenate(both, axis=0)
            res = lax.dot_general(second_ref[...], both, NT, preferred_element_type=F32)
            for i in range(in_local):
                cols = slice(i * wide, (i + 1) * wide)
                turn_ref[pl.ds(kk * kept * in_local + i, kept, stride=in_local), :] = (
                    jnp.concatenate([res[:kept, cols], res[kept:, cols]], axis=1)
                )
            part = turn_ref[kk * kept * in_local:(kk + 1) * kept * in_local, :]
            parts_out.append(part.reshape(peers, per_dest, WIDTH_B))
        send_ref[:, h * groups + kp] = jnp.concatenate(parts_out, axis=1).astype(BF16)

    def remote(c, h, start, size, n):
        dest = partner(n)
        at = pl.ds(h * groups + start, size)
        return pltpu.make_async_remote_copy(
            src_ref=send_ref.at[dest, at], dst_ref=recv_ref.at[me, at],
            send_sem=send_sem.at[c, n], recv_sem=recv_sem.at[c, n],
            device_id={"inputs": dest}, device_id_type=pl.DeviceIdType.MESH,
        )

    def push(c, h, start, size):
        def one(n, u):
            remote(c, h, start, size, n).start()
            return u

        lax.fori_loop(0, peers - 1, one, 0)

    def arrive(c, h, start, size):
        def one(n, u):
            remote(c, h, start, size, n).wait()
            return u

        lax.fori_loop(0, peers - 1, one, 0)

    def forward(h, carry):
        load_part(h).wait()

        @pl.when(h < parts - 1)
        def _():
            load_part(h + 1).start()

        def spectra(tp, u):
            two_spectra(h, tp)
            return u

        lax.fori_loop(0, span // 2, spectra, 0, unroll=8)

        def two_groups(n, u):
            channel_group(h, 2 * n)
            channel_group(h, 2 * n + 1)
            return u

        is_first = h == 0
        is_last = h == parts - 1
        cut = jnp.where(is_first, head // 2, 0)
        lax.fori_loop(0, cut, two_groups, 0)

        @pl.when(is_first)
        def _():
            pl.semaphore_wait(barrier, peers - 1)
            push(0, h, 0, head)

        lax.fori_loop(cut, groups // 2, two_groups, 0)

        @pl.when(is_first)
        def _():
            push(1, h, head, groups - head)

        @pl.when(is_last)
        def _():
            def piece(q, u):
                later = q // (groups // tail)
                j = q % (groups // tail)

                def one(n, v):
                    @pl.when((partner(n) >= ahead) == (later == 1))
                    def _():
                        remote(2 * parts - 2 + j, h, j * tail, tail, n).start()

                    return v

                return lax.fori_loop(0, peers - 1, one, u)

            lax.fori_loop(0, 2 * (groups // tail), piece, 0)

        @pl.when(jnp.logical_not(is_first | is_last))
        def _():
            push(2 * h + 1, h, 0, groups)

        return carry

    lax.fori_loop(0, parts, forward, 0)
    small[-1].start()
    small[-1].wait()
    own = pltpu.make_async_copy(send_ref.at[me], recv_ref.at[me], own_sem)
    own.start()
    own.wait()

    count = peers * in_local
    per = 2 * (kept // peers)
    halves = per // 2
    channels = width_a * halves
    low = count // 2
    i_at = lax.broadcasted_iota(jnp.int32, (low, WIDTH_B), 0)
    lane = lax.broadcasted_iota(jnp.int32, (low, WIDTH_B), 1)
    first_half = lane < count
    top_real = i_at >= lane
    low_real = i_at + low >= lane - count
    lane_row = lax.broadcasted_iota(jnp.int32, (count, WIDTH_B), 1)
    masks = [
        jnp.where((lane_row % wide) // span == u, 1.0, 0.0).astype(BF16) for u in range(shared)
    ]

    signs = jnp.where(
        lax.broadcasted_iota(jnp.int32, (per * count, WIDTH_B), 1) < wide, -1.0, 1.0
    )

    def swap(v):
        return pltpu.roll(v, wide, 1)

    def line_up(g):
        both = [recv_ref[:, g + n].reshape(per * count, WIDTH_B) for n in range(2)]
        lined = jnp.dot(
            order_ref[...], jnp.concatenate(both, axis=1), preferred_element_type=F32
        )
        for n in range(2):
            one = lined[:, n * WIDTH_B:(n + 1) * WIDTH_B]
            line_ref[g + n] = one.astype(BF16)
            quad_ref[g + n] = (swap(one) * signs).astype(BF16)

    def gram(kp, s, first, last):
        at = slice(s * count, (s + 1) * count)
        tiles = [line_ref[h * groups + kp, at, :] for h in range(first, last)]
        turned = [quad_ref[h * groups + kp, at, :] for h in range(first, last)]
        right = jnp.concatenate(
            [jnp.concatenate(tiles, axis=1), jnp.concatenate(turned, axis=1)], axis=0
        )
        left = jnp.concatenate(
            [jnp.concatenate([t * m for t in tiles], axis=1) for m in masks], axis=0
        )
        return lax.dot_general(left, right, NT, preferred_element_type=F32)

    def correlate_early(kp, u):
        for s in range(per):
            sum_ref[kp * per + s] = gram(kp, s, 0, parts - 2)
        return u

    def correlate(kp):
        for s in range(per):
            res = sum_ref[kp * per + s] + gram(kp, s, parts - 2, parts)
            for u in range(shared):
                top = res[u * count:u * count + low]
                bottom = res[u * count + low:(u + 1) * count]
                vis = jnp.where(
                    first_half,
                    jnp.where(top_real, top, swap(top)),
                    jnp.where(low_real, swap(bottom), bottom),
                )
                c = (s % halves) * width_a + (kp * 2 + s // halves) * shared + u
                vis_ref[pl.ds(c, low, stride=channels), :] = vis * (1.0 / nspec)

    def lines(h):
        def one(n, u):
            line_up(h * groups + 2 * n)
            return u

        lax.fori_loop(0, groups // 2, one, 0)

    def middle(h, carry):
        arrive(2 * h + 1, h, 0, groups)
        lines(h)

        @pl.when(h == parts - 3)
        def _():
            lax.fori_loop(0, groups, correlate_early, 0, unroll=2)

        return carry

    def finish(n, u):
        line_up((parts - 1) * groups + 2 * n)
        correlate(2 * n)
        correlate(2 * n + 1)
        return u

    def last_part(j, u):
        arrive(2 * parts - 2 + j, parts - 1, j * tail, tail)
        for n in range(tail // 2):
            finish(j * (tail // 2) + n, 0)
        return u

    arrive(0, 0, 0, head)
    arrive(1, 0, head, groups - head)
    lines(0)
    lax.fori_loop(1, parts - 1, middle, 0)
    lax.fori_loop(0, groups // tail, last_part, 0)


def turn_kernel(channels, pieces, vis_ref, out_any, out_ref, out_sem):
    half = out_ref.shape[0] // 2
    width = out_ref.shape[1]
    each = half // pieces

    def put(p, upper):
        at = pl.ds(p * each + upper * half, each)
        return pltpu.make_async_copy(out_ref.at[at], out_any.at[at], out_sem.at[upper, p])

    for p in range(pieces):
        def one_row(n, carry):
            i = p * each + n
            block = vis_ref[pl.ds(pl.multiple_of(i * channels, channels), channels), :]
            block = block.T.astype(BF16)
            out_ref[i] = block[:width]
            out_ref[i + half] = block[width:]
            return carry

        lax.fori_loop(0, each, one_row, 0, unroll=8)
        put(p, 0).start()
        put(p, 1).start()
    for p in range(pieces):
        put(p, 0).wait()
        put(p, 1).wait()


def kernel_body(peers, kept, samples, filter_coefs):
    in_local, total = samples.shape
    taps, nfft = filter_coefs.shape
    width_a = nfft // WIDTH_B
    nspec = total // nfft - taps + 1
    rows = width_a * in_local
    span = 16
    pieces = 4
    pad = 8
    parts = nspec // span
    groups = width_a * span // WIDTH_B
    head = 2
    tail = 4
    chunks = 2 * parts - 2 + groups // tail
    per = 2 * (kept // peers)
    count = peers * in_local
    channels = width_a * per // 2
    x = samples.reshape(in_local, total // WIDTH_B, WIDTH_B).transpose(1, 0, 2)
    x = x.reshape(total // WIDTH_B * in_local, WIDTH_B)
    coefs = filter_coefs.reshape(taps, width_a, WIDTH_B).transpose(1, 0, 2)
    coefs = coefs.reshape(width_a * taps, WIDTH_B)
    first, twist, second = make_tables(in_local, width_a, kept)
    order = np.zeros((per, peers, in_local, peers, per, in_local), np.float32)
    for s in range(per):
        for p in range(peers):
            order[s, p, range(in_local), p, s, range(in_local)] = 1
    order = jnp.asarray(order.reshape(per * count, per * count), BF16)
    blocks = (peers, parts * groups, per * in_local, WIDTH_B)
    lines = (parts * groups, per * count, WIDTH_B)
    inputs = (x, coefs, first, twist, second, order)
    inputs = [pltpu.with_memory_space_constraint(a, pltpu.HBM) for a in inputs]
    vis = pl.pallas_call(
        functools.partial(
            correlator_kernel, (peers, in_local, nspec, taps, kept, span, head, tail, pieces, pad)
        ),
        out_shape=jax.ShapeDtypeStruct((count // 2 * channels, 2 * count), F32),
        in_specs=[pl.BlockSpec(memory_space=pl.ANY)] * len(inputs),
        out_specs=pl.BlockSpec(memory_space=pltpu.VMEM),
        scratch_shapes=[pltpu.VMEM(a.shape, a.dtype) for a in inputs] + [
            pltpu.VMEM((taps * rows, WIDTH_B), F32),
            pltpu.VMEM((span * (rows + pad), WIDTH_B), F32),
            pltpu.VMEM((span * (rows + pad), WIDTH_B), F32),
            pltpu.VMEM((2 * kept * in_local, WIDTH_B), F32),
            pltpu.VMEM(blocks, BF16),
            pltpu.VMEM(blocks, BF16),
            pltpu.VMEM(lines, BF16),
            pltpu.VMEM(lines, BF16),
            pltpu.VMEM((groups * per, per * count, WIDTH_B), F32),
            pltpu.SemaphoreType.DMA((len(inputs) - 1,)),
            pltpu.SemaphoreType.DMA((parts + 1,)),
            pltpu.SemaphoreType.DMA((chunks, peers)),
            pltpu.SemaphoreType.DMA((chunks, peers)),
            pltpu.SemaphoreType.DMA,
        ],
        compiler_params=pltpu.CompilerParams(
            collective_id=0, has_side_effects=True, vmem_limit_bytes=48 * 2**20
        ),
        name="correlator",
    )(*inputs)
    out = pl.pallas_call(
        functools.partial(turn_kernel, channels, pieces),
        out_shape=jax.ShapeDtypeStruct((count, count, channels), BF16),
        in_specs=[pl.BlockSpec(memory_space=pltpu.VMEM)],
        out_specs=pl.BlockSpec(memory_space=pl.ANY),
        scratch_shapes=[
            pltpu.VMEM((count, count, channels), BF16),
            pltpu.SemaphoreType.DMA((2, pieces)),
        ],
        compiler_params=pltpu.CompilerParams(vmem_limit_bytes=16 * 2**20),
        name="turn",
    )(vis)
    return out.transpose(2, 0, 1)


def solution(mesh):
    peers = mesh.shape["inputs"]

    def body(samples, filter_coefs):
        in_local = samples.shape[0]
        kept = WIDTH_B // 4
        nfft = filter_coefs.shape[1]
        nspec = samples.shape[1] // nfft - filter_coefs.shape[0] + 1
        fits = kept % peers == 0 and in_local <= 8 and 2 * peers * in_local == WIDTH_B
        fits = fits and nspec % 16 == 0 and nspec >= 64 and nfft % (32 * WIDTH_B) == 0
        if fits and (2 * in_local * (kept // peers)) % 16 == 0:
            return kernel_body(peers, kept, samples, filter_coefs)
        return plain_body(samples, filter_coefs)

    return jax.shard_map(
        body,
        mesh=mesh,
        in_specs=(P(("groups", "inputs"), None), P()),
        out_specs=P(("groups", "inputs"), None, None),
        check_vma=False,
    )
```

```python
import functools
import math

import jax
import jax.numpy as jnp
import numpy as np
from jax import lax
from jax.experimental import pallas as pl
from jax.experimental.pallas import tpu as pltpu
from jax.sharding import PartitionSpec as P


def phase_table(first, second, period):
    rows = lax.broadcasted_iota(jnp.int32, (first, second), 0)
    cols = lax.broadcasted_iota(jnp.int32, (first, second), 1)
    angle = 2.0 * math.pi / period * (rows * cols % period).astype(jnp.float32)
    return (jnp.cos(angle), -jnp.sin(angle))


def correlate_items(block):
    count = block.shape[0]
    nspec_local = block.shape[2] // 2
    rotated = jnp.concatenate([-block[..., nspec_local:], block[..., :nspec_local]], axis=-1)
    real_sum = jnp.einsum("ikt,jkt->kij", block, block, preferred_element_type=jnp.float32)
    imag_sum = jnp.einsum("ikt,jkt->kij", block, rotated, preferred_element_type=jnp.float32)
    rows = lax.broadcasted_iota(jnp.int32, (count, count), 0)
    cols = lax.broadcasted_iota(jnp.int32, (count, count), 1)
    return (jnp.where(rows >= cols, real_sum, imag_sum) / nspec_local).astype(jnp.bfloat16)


def correlate_turned(block):
    flat_block = block.reshape(block.shape[0], block.shape[2], block.shape[3])
    return correlate_items(flat_block)


def plain_body(samples, filter_coefs):
    in_local, total = samples.shape
    taps_count, nfft_local = filter_coefs.shape
    frame_count = total // nfft_local
    nspec_local = frame_count - taps_count + 1
    width_b = 128
    width_a = nfft_local // width_b
    kept_width = width_b // 4
    frames = samples.reshape(in_local, frame_count, nfft_local).astype(jnp.float32)
    filtered = filter_coefs[0] * frames[:, 0:nspec_local]
    for tap_index in range(1, taps_count):
        filtered = (
            filtered + filter_coefs[tap_index] * frames[:, tap_index : tap_index + nspec_local]
        )
    grid_view = filtered.astype(jnp.bfloat16).reshape(in_local, nspec_local, width_a, width_b)
    first_cos, first_sin = phase_table(width_a, width_a, width_a)
    first_table = jnp.concatenate([first_cos, first_sin], axis=1).astype(jnp.bfloat16)
    first_out = jnp.einsum(
        "itab,ak->itkb", grid_view, first_table, preferred_element_type=jnp.float32
    )
    real_one = first_out[:, :, :width_a]
    imag_one = first_out[:, :, width_a:]
    twist_cos, twist_sin = phase_table(width_a, width_b, nfft_local)
    real_two = real_one * twist_cos - imag_one * twist_sin
    imag_two = real_one * twist_sin + imag_one * twist_cos
    stacked = jnp.concatenate(
        [real_two.astype(jnp.bfloat16), imag_two.astype(jnp.bfloat16)], axis=3
    )
    second_cos, second_sin = phase_table(width_b, width_b, width_b)
    second_cos = second_cos[:, :kept_width]
    second_sin = second_sin[:, :kept_width]
    upper_rows = jnp.concatenate([second_cos, second_sin], axis=1)
    lower_rows = jnp.concatenate([-second_sin, second_cos], axis=1)
    second_table = jnp.concatenate([upper_rows, lower_rows], axis=0).astype(jnp.bfloat16)
    second_out = jnp.einsum(
        "itkn,nq->iqkt", stacked, second_table, preferred_element_type=jnp.float32
    )
    real_out = second_out[:, :kept_width]
    imag_out = second_out[:, kept_width:]
    channels = width_a * kept_width
    spectra = jnp.concatenate(
        [real_out.astype(jnp.bfloat16), imag_out.astype(jnp.bfloat16)], axis=3
    )
    spectra = spectra.reshape(in_local, channels, 2 * nspec_local)
    peers = lax.axis_size("inputs")
    per_peer = channels // peers
    owner_view = spectra.reshape(in_local, peers, per_peer, 2 * nspec_local)
    result = correlate_turned(
        lax.all_to_all(owner_view, "inputs", split_axis=1, concat_axis=0, tiled=True)
    )
    return result


WIDTH_B = 128
BF16 = jnp.bfloat16
F32 = jnp.float32
NT = (((1,), (1,)), ((), ()))


def np_phase(first, second, period):
    turns = np.outer(np.arange(first), np.arange(second)) % period
    angle = np.float32(2.0 * math.pi / period) * turns.astype(np.float32)
    return np.cos(angle), -np.sin(angle)


def make_tables(in_local, width_a, kept):
    nfft = width_a * WIDTH_B
    half = width_a // 2
    cos_a, sin_a = (t.T for t in np_phase(width_a, width_a, width_a))
    first = np.concatenate([cos_a[:half + 1], sin_a[1:half]], axis=0)
    first = np.kron(first, np.eye(in_local, dtype=np.float32))
    mirrored = [*range(half + 1), *range(width_a - 1, half, -1)]
    twist = np.concatenate(
        [np.repeat(t[mirrored], in_local, axis=0) for t in np_phase(width_a, WIDTH_B, nfft)],
        axis=0,
    )
    cos_b, sin_b = (t[:, :kept].T for t in np_phase(WIDTH_B, WIDTH_B, WIDTH_B))
    second = np.concatenate(
        [np.concatenate([cos_b, -sin_b], axis=1), np.concatenate([sin_b, cos_b], axis=1)], axis=0
    )
    return jnp.asarray(first, BF16), jnp.asarray(twist, F32), jnp.asarray(second, BF16)


def correlator_kernel(
    dims, x_any, coef_any, first_any, twist_any, second_any, order_any, vis_ref,
    x_ref, coef_in, first_ref, twist_ref, second_ref, order_ref, coef_ref,
    real_ref, imag_ref, turn_ref, send_ref, recv_ref, line_ref, quad_ref, sum_ref,
    load_sem, x_sem, send_sem, recv_sem, own_sem,
):
    peers, in_local, nspec, taps, kept, span, head, tail, pieces, pad = dims
    rows = first_ref.shape[1]
    width_a = rows // in_local
    parts = nspec // span
    shared = WIDTH_B // (2 * span)
    wide = shared * span
    groups = width_a // (2 * shared)
    slot = rows + pad
    ahead = 2
    me = lax.axis_index("inputs")

    def partner(n):
        return lax.rem(me + n + 1, peers)

    barrier = pltpu.get_barrier_semaphore()

    def greet(n, carry):
        pl.semaphore_signal(
            barrier, inc=1, device_id={"inputs": partner(n)},
            device_id_type=pl.DeviceIdType.MESH,
        )
        return carry


    def load_frames(start, count, n):
        at = pl.ds(start * rows, count * rows)
        return pltpu.make_async_copy(x_any.at[at], x_ref.at[at], x_sem.at[n])

    def load_part(h):
        return load_frames(h * span + taps - 1, span, h)

    small = [
        pltpu.make_async_copy(src, dst, load_sem.at[n])
        for n, (src, dst) in enumerate((
            (coef_any, coef_in), (first_any, first_ref), (twist_any, twist_ref),
            (second_any, second_ref), (order_any, order_ref),
        ))
    ]
    small[0].start()
    load_frames(0, taps - 1, parts).start()
    load_part(0).start()
    for copy in small[1:-1]:
        copy.start()
    lax.fori_loop(0, peers - 1, greet, 0, unroll=5)

    small[0].wait()
    for m in range(taps):
        tap = coef_in[pl.ds(m, width_a, stride=taps), :]
        for i in range(in_local):
            coef_ref[pl.ds(m * rows + i, width_a, stride=in_local), :] = tap
    for copy in small[1:-1]:
        copy.wait()
    load_frames(0, taps - 1, parts).wait()

    lane_block = 64
    low_rows = rows // 2
    edge = lax.broadcasted_iota(jnp.int32, (8, WIDTH_B), 0) < in_local

    def two_spectra(h, tp):
        late_t = tp * 2
        t = h * span + late_t
        filtered = []
        for r in range(0, rows, lane_block):
            frames = [
                x_ref[pl.ds(pl.multiple_of((t + m) * rows + r, lane_block), lane_block), :].astype(F32)
                for m in range(taps + 1)
            ]
            pair = []
            for late in range(2):
                acc = None
                for m in range(taps):
                    at = m * rows + r
                    term = coef_ref[at:at + lane_block, :] * frames[m + late]
                    acc = term if acc is None else acc + term
                pair.append(acc.astype(BF16))
            filtered.append(jnp.concatenate(pair, axis=1))
        filtered = jnp.concatenate(filtered, axis=0)
        out = jnp.dot(first_ref[...], filtered, preferred_element_type=F32)
        w_re, w_im = twist_ref[:low_rows, :], twist_ref[rows:rows + low_rows, :]
        v_re, v_im = twist_ref[low_rows:rows, :], twist_ref[rows + low_rows:, :]
        for late in range(2):
            cols = slice(late * WIDTH_B, (late + 1) * WIDTH_B)
            re, im = out[:low_rows, cols], out[low_rows:, cols]
            mirror = jnp.concatenate([jnp.where(edge, im[:8], re[:8]), re[8:]], axis=0)
            im = jnp.concatenate([jnp.where(edge, 0.0, im[:8]), im[8:]], axis=0)
            at = pl.ds(pl.multiple_of((late_t + late) * slot, 8), low_rows)
            real_ref[at, :] = re * w_re - im * w_im
            imag_ref[at, :] = re * w_im + im * w_re
            at = pl.ds(pl.multiple_of((late_t + late) * slot + low_rows, 8), low_rows)
            real_ref[at, :] = mirror * v_re + im * v_im
            imag_ref[at, :] = mirror * v_im - im * v_re

    per_dest = kept // peers * in_local

    def channel_group(h, kp):
        parts_out = []
        for kk in range(2):
            both = []
            for i in range(in_local):
                for u in range(shared):
                    k = (kp * 2 + kk) * shared + u
                    k = jnp.where(k <= width_a // 2, k, width_a // 2 * 3 - k)
                    at = pl.ds(k * in_local + i, span, stride=slot)
                    both.append(jnp.concatenate(
                        [real_ref[at, :].astype(BF16), imag_ref[at, :].astype(BF16)], axis=1
                    ))
            both = jnp.concatenate(both, axis=0)
            res = lax.dot_general(second_ref[...], both, NT, preferred_element_type=F32)
            for i in range(in_local):
                cols = slice(i * wide, (i + 1) * wide)
                turn_ref[pl.ds(kk * kept * in_local + i, kept, stride=in_local), :] = (
                    jnp.concatenate([res[:kept, cols], res[kept:, cols]], axis=1)
                )
            part = turn_ref[kk * kept * in_local:(kk + 1) * kept * in_local, :]
            parts_out.append(part.reshape(peers, per_dest, WIDTH_B))
        send_ref[:, h * groups + kp] = jnp.concatenate(parts_out, axis=1).astype(BF16)

    def remote(c, h, start, size, n):
        dest = partner(n)
        at = pl.ds(h * groups + start, size)
        return pltpu.make_async_remote_copy(
            src_ref=send_ref.at[dest, at], dst_ref=recv_ref.at[me, at],
            send_sem=send_sem.at[c, n], recv_sem=recv_sem.at[c, n],
            device_id={"inputs": dest}, device_id_type=pl.DeviceIdType.MESH,
        )

    def push(c, h, start, size):
        def one(n, u):
            remote(c, h, start, size, n).start()
            return u

        lax.fori_loop(0, peers - 1, one, 0, unroll=5)

    def arrive(c, h, start, size):
        def one(n, u):
            remote(c, h, start, size, n).wait()
            return u

        lax.fori_loop(0, peers - 1, one, 0, unroll=5)

    def forward(h, carry):
        load_part(h).wait()

        @pl.when(h < parts - 1)
        def _():
            load_part(h + 1).start()

        def spectra(tp, u):
            two_spectra(h, tp)
            return u

        lax.fori_loop(0, span // 2, spectra, 0, unroll=8)

        def two_groups(n, u):
            channel_group(h, 2 * n)
            channel_group(h, 2 * n + 1)
            return u

        is_first = h == 0
        is_last = h == parts - 1
        cut = jnp.where(is_first, head // 2, 0)
        lax.fori_loop(0, cut, two_groups, 0)

        @pl.when(is_first)
        def _():
            pl.semaphore_wait(barrier, peers - 1)
            push(0, h, 0, head)

        lax.fori_loop(cut, groups // 2, two_groups, 0)

        @pl.when(is_first)
        def _():
            push(1, h, head, groups - head)

        @pl.when(is_last)
        def _():
            def piece(q, u):
                later = q // (groups // tail)
                j = q % (groups // tail)

                def one(n, v):
                    @pl.when((partner(n) >= ahead) == (later == 1))
                    def _():
                        remote(2 * parts - 2 + j, h, j * tail, tail, n).start()

                    return v

                return lax.fori_loop(0, peers - 1, one, u)

            lax.fori_loop(0, 2 * (groups // tail), piece, 0)

        @pl.when(jnp.logical_not(is_first | is_last))
        def _():
            push(2 * h + 1, h, 0, groups)

        return carry

    lax.fori_loop(0, parts, forward, 0)
    small[-1].start()
    small[-1].wait()
    own = pltpu.make_async_copy(send_ref.at[me], recv_ref.at[me], own_sem)
    own.start()
    own.wait()

    count = peers * in_local
    per = 2 * (kept // peers)
    halves = per // 2
    channels = width_a * halves
    low = count // 2
    i_at = lax.broadcasted_iota(jnp.int32, (low, WIDTH_B), 0)
    lane = lax.broadcasted_iota(jnp.int32, (low, WIDTH_B), 1)
    first_half = lane < count
    top_real = i_at >= lane
    low_real = i_at + low >= lane - count
    lane_row = lax.broadcasted_iota(jnp.int32, (count, WIDTH_B), 1)
    masks = [
        jnp.where((lane_row % wide) // span == u, 1.0, 0.0).astype(BF16) for u in range(shared)
    ]

    signs = jnp.where(
        lax.broadcasted_iota(jnp.int32, (per * count, WIDTH_B), 1) < wide, -1.0, 1.0
    )

    def swap(v):
        return pltpu.roll(v, wide, 1)

    def line_up(g):
        both = [recv_ref[:, g + n].reshape(per * count, WIDTH_B) for n in range(2)]
        lined = jnp.dot(
            order_ref[...], jnp.concatenate(both, axis=1), preferred_element_type=F32
        )
        for n in range(2):
            one = lined[:, n * WIDTH_B:(n + 1) * WIDTH_B]
            line_ref[g + n] = one.astype(BF16)
            quad_ref[g + n] = (swap(one) * signs).astype(BF16)

    def gram(kp, s, first, last):
        at = slice(s * count, (s + 1) * count)
        tiles = [line_ref[h * groups + kp, at, :] for h in range(first, last)]
        turned = [quad_ref[h * groups + kp, at, :] for h in range(first, last)]
        right = jnp.concatenate(
            [jnp.concatenate(tiles, axis=1), jnp.concatenate(turned, axis=1)], axis=0
        )
        left = jnp.concatenate(
            [jnp.concatenate([t * m for t in tiles], axis=1) for m in masks], axis=0
        )
        return lax.dot_general(left, right, NT, preferred_element_type=F32)

    def select(res, u):
        top = res[u * count:u * count + low]
        bottom = res[u * count + low:(u + 1) * count]
        return jnp.where(
            first_half,
            jnp.where(top_real, top, swap(top)),
            jnp.where(low_real, swap(bottom), bottom),
        )

    def correlate_early(kp, carry):
        for s in range(per):
            res = gram(kp, s, 0, parts - 2)
            for u in range(shared):
                sum_ref[kp * per + s, u * low:(u + 1) * low, :] = select(res, u)
        return carry

    def correlate(kp):
        for s in range(per):
            res = gram(kp, s, parts - 2, parts)
            for u in range(shared):
                vis = select(res, u) + sum_ref[kp * per + s, u * low:(u + 1) * low, :]
                c = (s % halves) * width_a + (kp * 2 + s // halves) * shared + u
                vis_ref[pl.ds(c, low, stride=channels), :] = vis * (1.0 / nspec)

    def lines(h):
        def one(n, u):
            line_up(h * groups + 2 * n)
            return u

        lax.fori_loop(0, groups // 2, one, 0)

    def middle(h, carry):
        arrive(2 * h + 1, h, 0, groups)
        lines(h)

        @pl.when(h == parts - 3)
        def _():
            lax.fori_loop(0, groups, correlate_early, 0, unroll=2)

        return carry

    def finish(n, u):
        line_up((parts - 1) * groups + 2 * n)
        correlate(2 * n)
        correlate(2 * n + 1)
        return u

    def last_part(j, u):
        arrive(2 * parts - 2 + j, parts - 1, j * tail, tail)
        for n in range(tail // 2):
            finish(j * (tail // 2) + n, 0)
        return u

    arrive(0, 0, 0, head)
    arrive(1, 0, head, groups - head)
    lines(0)
    lax.fori_loop(1, parts - 1, middle, 0)
    lax.fori_loop(0, groups // tail, last_part, 0)


def turn_kernel(channels, pieces, vis_ref, out_any, out_ref, out_sem):
    half = out_ref.shape[0] // 2
    width = out_ref.shape[1]
    each = half // pieces

    def put(p, upper):
        at = pl.ds(p * each + upper * half, each)
        return pltpu.make_async_copy(out_ref.at[at], out_any.at[at], out_sem.at[upper, p])

    for p in range(pieces):
        def one_row(n, carry):
            i = p * each + n
            block = vis_ref[pl.ds(pl.multiple_of(i * channels, channels), channels), :]
            block = block.T.astype(BF16)
            out_ref[i] = block[:width]
            out_ref[i + half] = block[width:]
            return carry

        lax.fori_loop(0, each, one_row, 0, unroll=8)
        put(p, 0).start()
        put(p, 1).start()
    for p in range(pieces):
        put(p, 0).wait()
        put(p, 1).wait()


def kernel_body(peers, kept, samples, filter_coefs):
    in_local, total = samples.shape
    taps, nfft = filter_coefs.shape
    width_a = nfft // WIDTH_B
    nspec = total // nfft - taps + 1
    rows = width_a * in_local
    span = 16
    pieces = 4
    pad = 8
    parts = nspec // span
    groups = width_a * span // WIDTH_B
    head = 2
    tail = 4
    chunks = 2 * parts - 2 + groups // tail
    per = 2 * (kept // peers)
    count = peers * in_local
    channels = width_a * per // 2
    x = samples.reshape(in_local, total // WIDTH_B, WIDTH_B).transpose(1, 0, 2)
    x = x.reshape(total // WIDTH_B * in_local, WIDTH_B)
    coefs = filter_coefs.reshape(taps, width_a, WIDTH_B).transpose(1, 0, 2)
    coefs = coefs.reshape(width_a * taps, WIDTH_B)
    first, twist, second = make_tables(in_local, width_a, kept)
    order = np.zeros((per, peers, in_local, peers, per, in_local), np.float32)
    for s in range(per):
        for p in range(peers):
            order[s, p, range(in_local), p, s, range(in_local)] = 1
    order = jnp.asarray(order.reshape(per * count, per * count), BF16)
    blocks = (peers, parts * groups, per * in_local, WIDTH_B)
    lines = (parts * groups, per * count, WIDTH_B)
    inputs = (x, coefs, first, twist, second, order)
    inputs = [pltpu.with_memory_space_constraint(a, pltpu.HBM) for a in inputs]
    vis = pl.pallas_call(
        functools.partial(
            correlator_kernel, (peers, in_local, nspec, taps, kept, span, head, tail, pieces, pad)
        ),
        out_shape=jax.ShapeDtypeStruct((count // 2 * channels, 2 * count), F32),
        in_specs=[pl.BlockSpec(memory_space=pl.ANY)] * len(inputs),
        out_specs=pl.BlockSpec(memory_space=pltpu.VMEM),
        scratch_shapes=[pltpu.VMEM(a.shape, a.dtype) for a in inputs] + [
            pltpu.VMEM((taps * rows, WIDTH_B), F32),
            pltpu.VMEM((span * (rows + pad), WIDTH_B), F32),
            pltpu.VMEM((span * (rows + pad), WIDTH_B), F32),
            pltpu.VMEM((2 * kept * in_local, WIDTH_B), F32),
            pltpu.VMEM(blocks, BF16),
            pltpu.VMEM(blocks, BF16),
            pltpu.VMEM(lines, BF16),
            pltpu.VMEM(lines, BF16),
            pltpu.VMEM((groups * per, WIDTH_B // (2 * span) * (count // 2), WIDTH_B), F32),
            pltpu.SemaphoreType.DMA((len(inputs) - 1,)),
            pltpu.SemaphoreType.DMA((parts + 1,)),
            pltpu.SemaphoreType.DMA((chunks, peers)),
            pltpu.SemaphoreType.DMA((chunks, peers)),
            pltpu.SemaphoreType.DMA,
        ],
        compiler_params=pltpu.CompilerParams(
            collective_id=0, has_side_effects=True, vmem_limit_bytes=48 * 2**20
        ),
        name="correlator",
    )(*inputs)
    out = pl.pallas_call(
        functools.partial(turn_kernel, channels, pieces),
        out_shape=jax.ShapeDtypeStruct((count, count, channels), BF16),
        in_specs=[pl.BlockSpec(memory_space=pltpu.VMEM)],
        out_specs=pl.BlockSpec(memory_space=pl.ANY),
        scratch_shapes=[
            pltpu.VMEM((count, count, channels), BF16),
            pltpu.SemaphoreType.DMA((2, pieces)),
        ],
        compiler_params=pltpu.CompilerParams(vmem_limit_bytes=16 * 2**20),
        name="turn",
    )(vis)
    return out.transpose(2, 0, 1)


def solution(mesh):
    peers = mesh.shape["inputs"]

    def body(samples, filter_coefs):
        in_local = samples.shape[0]
        kept = WIDTH_B // 4
        nfft = filter_coefs.shape[1]
        nspec = samples.shape[1] // nfft - filter_coefs.shape[0] + 1
        fits = kept % peers == 0 and in_local <= 8 and 2 * peers * in_local == WIDTH_B
        fits = fits and nspec % 16 == 0 and nspec >= 64 and nfft % (32 * WIDTH_B) == 0
        if fits and (2 * in_local * (kept // peers)) % 16 == 0:
            return kernel_body(peers, kept, samples, filter_coefs)
        return plain_body(samples, filter_coefs)

    return jax.shard_map(
        body,
        mesh=mesh,
        in_specs=(P(("groups", "inputs"), None), P()),
        out_specs=P(("groups", "inputs"), None, None),
        check_vma=False,
    )
```

```python
import functools
import math

import jax
import jax.numpy as jnp
import numpy as np
from jax import lax
from jax.experimental import pallas as pl
from jax.experimental.pallas import tpu as pltpu
from jax.sharding import PartitionSpec as P


def phase_table(first, second, period):
    rows = lax.broadcasted_iota(jnp.int32, (first, second), 0)
    cols = lax.broadcasted_iota(jnp.int32, (first, second), 1)
    angle = 2.0 * math.pi / period * (rows * cols % period).astype(jnp.float32)
    return (jnp.cos(angle), -jnp.sin(angle))


def correlate_items(block):
    count = block.shape[0]
    nspec_local = block.shape[2] // 2
    rotated = jnp.concatenate([-block[..., nspec_local:], block[..., :nspec_local]], axis=-1)
    real_sum = jnp.einsum("ikt,jkt->kij", block, block, preferred_element_type=jnp.float32)
    imag_sum = jnp.einsum("ikt,jkt->kij", block, rotated, preferred_element_type=jnp.float32)
    rows = lax.broadcasted_iota(jnp.int32, (count, count), 0)
    cols = lax.broadcasted_iota(jnp.int32, (count, count), 1)
    return (jnp.where(rows >= cols, real_sum, imag_sum) / nspec_local).astype(jnp.bfloat16)


def correlate_turned(block):
    flat_block = block.reshape(block.shape[0], block.shape[2], block.shape[3])
    return correlate_items(flat_block)


def plain_body(samples, filter_coefs):
    in_local, total = samples.shape
    taps_count, nfft_local = filter_coefs.shape
    frame_count = total // nfft_local
    nspec_local = frame_count - taps_count + 1
    width_b = 128
    width_a = nfft_local // width_b
    kept_width = width_b // 4
    frames = samples.reshape(in_local, frame_count, nfft_local).astype(jnp.float32)
    filtered = filter_coefs[0] * frames[:, 0:nspec_local]
    for tap_index in range(1, taps_count):
        filtered = (
            filtered + filter_coefs[tap_index] * frames[:, tap_index : tap_index + nspec_local]
        )
    grid_view = filtered.astype(jnp.bfloat16).reshape(in_local, nspec_local, width_a, width_b)
    first_cos, first_sin = phase_table(width_a, width_a, width_a)
    first_table = jnp.concatenate([first_cos, first_sin], axis=1).astype(jnp.bfloat16)
    first_out = jnp.einsum(
        "itab,ak->itkb", grid_view, first_table, preferred_element_type=jnp.float32
    )
    real_one = first_out[:, :, :width_a]
    imag_one = first_out[:, :, width_a:]
    twist_cos, twist_sin = phase_table(width_a, width_b, nfft_local)
    real_two = real_one * twist_cos - imag_one * twist_sin
    imag_two = real_one * twist_sin + imag_one * twist_cos
    stacked = jnp.concatenate(
        [real_two.astype(jnp.bfloat16), imag_two.astype(jnp.bfloat16)], axis=3
    )
    second_cos, second_sin = phase_table(width_b, width_b, width_b)
    second_cos = second_cos[:, :kept_width]
    second_sin = second_sin[:, :kept_width]
    upper_rows = jnp.concatenate([second_cos, second_sin], axis=1)
    lower_rows = jnp.concatenate([-second_sin, second_cos], axis=1)
    second_table = jnp.concatenate([upper_rows, lower_rows], axis=0).astype(jnp.bfloat16)
    second_out = jnp.einsum(
        "itkn,nq->iqkt", stacked, second_table, preferred_element_type=jnp.float32
    )
    real_out = second_out[:, :kept_width]
    imag_out = second_out[:, kept_width:]
    channels = width_a * kept_width
    spectra = jnp.concatenate(
        [real_out.astype(jnp.bfloat16), imag_out.astype(jnp.bfloat16)], axis=3
    )
    spectra = spectra.reshape(in_local, channels, 2 * nspec_local)
    peers = lax.axis_size("inputs")
    per_peer = channels // peers
    owner_view = spectra.reshape(in_local, peers, per_peer, 2 * nspec_local)
    result = correlate_turned(
        lax.all_to_all(owner_view, "inputs", split_axis=1, concat_axis=0, tiled=True)
    )
    return result


WIDTH_B = 128
BF16 = jnp.bfloat16
F32 = jnp.float32
NT = (((1,), (1,)), ((), ()))


def np_phase(first, second, period):
    turns = np.outer(np.arange(first), np.arange(second)) % period
    angle = np.float32(2.0 * math.pi / period) * turns.astype(np.float32)
    return np.cos(angle), -np.sin(angle)


def make_tables(in_local, width_a, kept):
    nfft = width_a * WIDTH_B
    half = width_a // 2
    cos_a, sin_a = (t.T for t in np_phase(width_a, width_a, width_a))
    first = np.concatenate([cos_a[:half + 1], sin_a[1:half]], axis=0)
    first = np.kron(first, np.eye(in_local, dtype=np.float32))
    mirrored = [*range(half + 1), *range(width_a - 1, half, -1)]
    twist = np.concatenate(
        [np.repeat(t[mirrored], in_local, axis=0) for t in np_phase(width_a, WIDTH_B, nfft)],
        axis=0,
    )
    cos_b, sin_b = (t[:, :kept].T for t in np_phase(WIDTH_B, WIDTH_B, WIDTH_B))
    second = np.concatenate(
        [np.concatenate([cos_b, -sin_b], axis=1), np.concatenate([sin_b, cos_b], axis=1)], axis=0
    )
    return jnp.asarray(first, BF16), jnp.asarray(twist, F32), jnp.asarray(second, BF16)


def correlator_kernel(
    dims, x_any, coef_any, first_any, twist_any, second_any, order_any, vis_ref,
    x_ref, coef_in, first_ref, twist_ref, second_ref, order_ref, coef_ref,
    real_ref, imag_ref, turn_ref, send_ref, recv_ref, line_ref, quad_ref, sum_ref,
    load_sem, x_sem, send_sem, recv_sem, own_sem,
):
    peers, in_local, nspec, taps, kept, span, head, tail, pieces, pad = dims
    rows = first_ref.shape[1]
    width_a = rows // in_local
    parts = nspec // span
    shared = WIDTH_B // (2 * span)
    wide = shared * span
    groups = width_a // (2 * shared)
    slot = rows + pad
    ahead = 2
    me = lax.axis_index("inputs")

    def partner(n):
        return lax.rem(me + n + 1, peers)

    barrier = pltpu.get_barrier_semaphore()

    def greet(n, carry):
        pl.semaphore_signal(
            barrier, inc=1, device_id={"inputs": partner(n)},
            device_id_type=pl.DeviceIdType.MESH,
        )
        return carry


    def load_frames(start, count, n):
        at = pl.ds(start * rows, count * rows)
        return pltpu.make_async_copy(x_any.at[at], x_ref.at[at], x_sem.at[n])

    def load_part(h):
        return load_frames(h * span + taps - 1, span, h)

    small = [
        pltpu.make_async_copy(src, dst, load_sem.at[n])
        for n, (src, dst) in enumerate((
            (coef_any, coef_in), (first_any, first_ref), (twist_any, twist_ref),
            (second_any, second_ref), (order_any, order_ref),
        ))
    ]
    small[0].start()
    load_frames(0, taps - 1, parts).start()
    load_part(0).start()
    for copy in small[1:-1]:
        copy.start()
    lax.fori_loop(0, peers - 1, greet, 0, unroll=5)

    small[0].wait()
    for m in range(taps):
        tap = coef_in[pl.ds(m, width_a, stride=taps), :]
        for i in range(in_local):
            coef_ref[pl.ds(m * rows + i, width_a, stride=in_local), :] = tap
    for copy in small[1:-1]:
        copy.wait()
    load_frames(0, taps - 1, parts).wait()

    lane_block = 64
    low_rows = rows // 2
    edge = lax.broadcasted_iota(jnp.int32, (8, WIDTH_B), 0) < in_local

    def two_spectra(h, tp):
        late_t = tp * 2
        t = h * span + late_t
        filtered = []
        for r in range(0, rows, lane_block):
            frames = [
                x_ref[pl.ds(pl.multiple_of((t + m) * rows + r, lane_block), lane_block), :].astype(F32)
                for m in range(taps + 1)
            ]
            pair = []
            for late in range(2):
                acc = None
                for m in range(taps):
                    at = m * rows + r
                    term = coef_ref[at:at + lane_block, :] * frames[m + late]
                    acc = term if acc is None else acc + term
                pair.append(acc.astype(BF16))
            filtered.append(jnp.concatenate(pair, axis=1))
        filtered = jnp.concatenate(filtered, axis=0)
        out = jnp.dot(first_ref[...], filtered, preferred_element_type=F32)
        w_re, w_im = twist_ref[:low_rows, :], twist_ref[rows:rows + low_rows, :]
        v_re, v_im = twist_ref[low_rows:rows, :], twist_ref[rows + low_rows:, :]
        for late in range(2):
            cols = slice(late * WIDTH_B, (late + 1) * WIDTH_B)
            re, im = out[:low_rows, cols], out[low_rows:, cols]
            mirror = jnp.concatenate([jnp.where(edge, im[:8], re[:8]), re[8:]], axis=0)
            im = jnp.concatenate([jnp.where(edge, 0.0, im[:8]), im[8:]], axis=0)
            at = pl.ds(pl.multiple_of((late_t + late) * slot, 8), low_rows)
            real_ref[at, :] = re * w_re - im * w_im
            imag_ref[at, :] = re * w_im + im * w_re
            at = pl.ds(pl.multiple_of((late_t + late) * slot + low_rows, 8), low_rows)
            real_ref[at, :] = mirror * v_re + im * v_im
            imag_ref[at, :] = mirror * v_im - im * v_re

    per_dest = kept // peers * in_local

    def channel_group(h, kp):
        parts_out = []
        for kk in range(2):
            both = []
            for i in range(in_local):
                for u in range(shared):
                    k = (kp * 2 + kk) * shared + u
                    k = jnp.where(k <= width_a // 2, k, width_a // 2 * 3 - k)
                    at = pl.ds(k * in_local + i, span, stride=slot)
                    both.append(jnp.concatenate(
                        [real_ref[at, :].astype(BF16), imag_ref[at, :].astype(BF16)], axis=1
                    ))
            both = jnp.concatenate(both, axis=0)
            res = lax.dot_general(second_ref[...], both, NT, preferred_element_type=F32)
            for i in range(in_local):
                cols = slice(i * wide, (i + 1) * wide)
                turn_ref[pl.ds(kk * kept * in_local + i, kept, stride=in_local), :] = (
                    jnp.concatenate([res[:kept, cols], res[kept:, cols]], axis=1)
                )
            part = turn_ref[kk * kept * in_local:(kk + 1) * kept * in_local, :]
            parts_out.append(part.reshape(peers, per_dest, WIDTH_B))
        send_ref[:, h * groups + kp] = jnp.concatenate(parts_out, axis=1).astype(BF16)

    def remote(c, h, start, size, n):
        dest = partner(n)
        at = pl.ds(h * groups + start, size)
        return pltpu.make_async_remote_copy(
            src_ref=send_ref.at[dest, at], dst_ref=recv_ref.at[me, at],
            send_sem=send_sem.at[c, n], recv_sem=recv_sem.at[c, n],
            device_id={"inputs": dest}, device_id_type=pl.DeviceIdType.MESH,
        )

    def push(c, h, start, size):
        def one(n, u):
            remote(c, h, start, size, n).start()
            return u

        lax.fori_loop(0, peers - 1, one, 0, unroll=5)

    def arrive(c, h, start, size):
        def one(n, u):
            remote(c, h, start, size, n).wait()
            return u

        lax.fori_loop(0, peers - 1, one, 0, unroll=5)

    def forward(h, carry):
        load_part(h).wait()

        @pl.when(h < parts - 1)
        def _():
            load_part(h + 1).start()

        def spectra(tp, u):
            two_spectra(h, tp)
            return u

        lax.fori_loop(0, span // 2, spectra, 0, unroll=8)

        def two_groups(n, u):
            channel_group(h, 2 * n)
            channel_group(h, 2 * n + 1)
            return u

        is_first = h == 0
        is_last = h == parts - 1
        cut = jnp.where(is_first, head // 2, 0)
        lax.fori_loop(0, cut, two_groups, 0)

        @pl.when(is_first)
        def _():
            pl.semaphore_wait(barrier, peers - 1)
            push(0, h, 0, head)

        lax.fori_loop(cut, groups // 2, two_groups, 0)

        @pl.when(is_first)
        def _():
            push(1, h, head, groups - head)

        @pl.when(is_last)
        def _():
            def piece(q, u):
                later = q // (groups // tail)
                j = q % (groups // tail)

                def one(n, v):
                    @pl.when((partner(n) >= ahead) == (later == 1))
                    def _():
                        remote(2 * parts - 2 + j, h, j * tail, tail, n).start()

                    return v

                return lax.fori_loop(0, peers - 1, one, u)

            lax.fori_loop(0, 2 * (groups // tail), piece, 0)

        @pl.when(jnp.logical_not(is_first | is_last))
        def _():
            push(2 * h + 1, h, 0, groups)

        return carry

    lax.fori_loop(0, parts, forward, 0)
    small[-1].start()
    small[-1].wait()
    own = pltpu.make_async_copy(send_ref.at[me], recv_ref.at[me], own_sem)
    own.start()
    own.wait()

    count = peers * in_local
    per = 2 * (kept // peers)
    halves = per // 2
    channels = width_a * halves
    low = count // 2
    i_at = lax.broadcasted_iota(jnp.int32, (low, WIDTH_B), 0)
    lane = lax.broadcasted_iota(jnp.int32, (low, WIDTH_B), 1)
    first_half = lane < count
    top_real = i_at >= lane
    low_real = i_at + low >= lane - count
    lane_row = lax.broadcasted_iota(jnp.int32, (count, WIDTH_B), 1)
    masks = [
        jnp.where((lane_row % wide) // span == u, 1.0, 0.0).astype(BF16) for u in range(shared)
    ]

    signs = jnp.where(
        lax.broadcasted_iota(jnp.int32, (per * count, WIDTH_B), 1) < wide, -1.0, 1.0
    )

    def swap(v):
        return pltpu.roll(v, wide, 1)

    def line_up(g):
        both = [recv_ref[:, g + n].reshape(per * count, WIDTH_B) for n in range(2)]
        lined = jnp.dot(
            order_ref[...], jnp.concatenate(both, axis=1), preferred_element_type=F32
        )
        for n in range(2):
            one = lined[:, n * WIDTH_B:(n + 1) * WIDTH_B]
            line_ref[g + n] = one.astype(BF16)
            quad_ref[g + n] = (swap(one) * signs).astype(BF16)

    def gram(kp, s, first, last):
        at = slice(s * count, (s + 1) * count)
        tiles = [line_ref[h * groups + kp, at, :] for h in range(first, last)]
        turned = [quad_ref[h * groups + kp, at, :] for h in range(first, last)]
        right = jnp.concatenate(
            [jnp.concatenate(tiles, axis=1), jnp.concatenate(turned, axis=1)], axis=0
        )
        left = jnp.concatenate(
            [jnp.concatenate([t * m for t in tiles], axis=1) for m in masks], axis=0
        )
        return lax.dot_general(left, right, NT, preferred_element_type=F32)

    def select(res, u):
        top = res[u * count:u * count + low]
        bottom = res[u * count + low:(u + 1) * count]
        return jnp.where(
            first_half,
            jnp.where(top_real, top, swap(top)),
            jnp.where(low_real, swap(bottom), bottom),
        )

    def correlate_early(kp, carry):
        for s in range(per):
            res = gram(kp, s, 0, parts - 2)
            for u in range(shared):
                sum_ref[kp * per + s, u * low:(u + 1) * low, :] = select(res, u)
        return carry

    def gram_pair(kp, s, h):
        g = h * groups + kp
        ats = [slice(n * count, (n + 1) * count) for n in (s, s + 1)]
        tiles = [line_ref[g, at, :] for at in ats]
        sides = [jnp.concatenate([line_ref[g, at, :], quad_ref[g, at, :]], axis=0) for at in ats]
        none = jnp.zeros_like(sides[0])
        right = jnp.concatenate([
            jnp.concatenate([sides[0], none], axis=1), jnp.concatenate([none, sides[1]], axis=1)
        ], axis=0)
        left = jnp.concatenate(
            [jnp.concatenate([t * m for t in tiles], axis=1) for m in masks], axis=0
        )
        return lax.dot_general(left, right, NT, preferred_element_type=F32)

    def correlate_more(kp, carry):
        for s in range(per):
            if s % 2 == 0:
                both = gram_pair(kp, s, parts - 2)
            res = both[:, s % 2 * WIDTH_B:(s % 2 + 1) * WIDTH_B]
            for u in range(shared):
                sum_ref[kp * per + s, u * low:(u + 1) * low, :] += select(res, u)
        return carry

    def correlate(kp):
        for s in range(per):
            if s % 2 == 0:
                both = gram_pair(kp, s, parts - 1)
            res = both[:, s % 2 * WIDTH_B:(s % 2 + 1) * WIDTH_B]
            for u in range(shared):
                vis = select(res, u) + sum_ref[kp * per + s, u * low:(u + 1) * low, :]
                c = (s % halves) * width_a + (kp * 2 + s // halves) * shared + u
                vis_ref[pl.ds(c, low, stride=channels), :] = vis * (1.0 / nspec)

    def lines(h):
        def one(n, u):
            line_up(h * groups + 2 * n)
            return u

        lax.fori_loop(0, groups // 2, one, 0)

    def middle(h, carry):
        arrive(2 * h + 1, h, 0, groups)
        lines(h)

        @pl.when(h == parts - 3)
        def _():
            lax.fori_loop(0, groups, correlate_early, 0, unroll=2)

        return carry

    def finish(n, u):
        line_up((parts - 1) * groups + 2 * n)
        correlate(2 * n)
        correlate(2 * n + 1)
        return u

    def last_part(j, u):
        arrive(2 * parts - 2 + j, parts - 1, j * tail, tail)
        for n in range(tail // 2):
            finish(j * (tail // 2) + n, 0)
        return u

    arrive(0, 0, 0, head)
    arrive(1, 0, head, groups - head)
    lines(0)
    lax.fori_loop(1, parts - 1, middle, 0)
    lax.fori_loop(0, groups, correlate_more, 0, unroll=2)
    lax.fori_loop(0, groups // tail, last_part, 0)


def turn_kernel(channels, pieces, vis_ref, out_any, out_ref, out_sem):
    half = out_ref.shape[0] // 2
    width = out_ref.shape[1]
    each = half // pieces

    def put(p, upper):
        at = pl.ds(p * each + upper * half, each)
        return pltpu.make_async_copy(out_ref.at[at], out_any.at[at], out_sem.at[upper, p])

    for p in range(pieces):
        def one_row(n, carry):
            i = p * each + n
            block = vis_ref[pl.ds(pl.multiple_of(i * channels, channels), channels), :]
            block = block.T.astype(BF16)
            out_ref[i] = block[:width]
            out_ref[i + half] = block[width:]
            return carry

        lax.fori_loop(0, each, one_row, 0, unroll=8)
        put(p, 0).start()
        put(p, 1).start()
    for p in range(pieces):
        put(p, 0).wait()
        put(p, 1).wait()


def kernel_body(peers, kept, samples, filter_coefs):
    in_local, total = samples.shape
    taps, nfft = filter_coefs.shape
    width_a = nfft // WIDTH_B
    nspec = total // nfft - taps + 1
    rows = width_a * in_local
    span = 16
    pieces = 4
    pad = 8
    parts = nspec // span
    groups = width_a * span // WIDTH_B
    head = 2
    tail = 4
    chunks = 2 * parts - 2 + groups // tail
    per = 2 * (kept // peers)
    count = peers * in_local
    channels = width_a * per // 2
    x = samples.reshape(in_local, total // WIDTH_B, WIDTH_B).transpose(1, 0, 2)
    x = x.reshape(total // WIDTH_B * in_local, WIDTH_B)
    coefs = filter_coefs.reshape(taps, width_a, WIDTH_B).transpose(1, 0, 2)
    coefs = coefs.reshape(width_a * taps, WIDTH_B)
    first, twist, second = make_tables(in_local, width_a, kept)
    order = np.zeros((per, peers, in_local, peers, per, in_local), np.float32)
    for s in range(per):
        for p in range(peers):
            order[s, p, range(in_local), p, s, range(in_local)] = 1
    order = jnp.asarray(order.reshape(per * count, per * count), BF16)
    blocks = (peers, parts * groups, per * in_local, WIDTH_B)
    lines = (parts * groups, per * count, WIDTH_B)
    inputs = (x, coefs, first, twist, second, order)
    inputs = [pltpu.with_memory_space_constraint(a, pltpu.HBM) for a in inputs]
    vis = pl.pallas_call(
        functools.partial(
            correlator_kernel, (peers, in_local, nspec, taps, kept, span, head, tail, pieces, pad)
        ),
        out_shape=jax.ShapeDtypeStruct((count // 2 * channels, 2 * count), F32),
        in_specs=[pl.BlockSpec(memory_space=pl.ANY)] * len(inputs),
        out_specs=pl.BlockSpec(memory_space=pltpu.VMEM),
        scratch_shapes=[pltpu.VMEM(a.shape, a.dtype) for a in inputs] + [
            pltpu.VMEM((taps * rows, WIDTH_B), F32),
            pltpu.VMEM((span * (rows + pad), WIDTH_B), F32),
            pltpu.VMEM((span * (rows + pad), WIDTH_B), F32),
            pltpu.VMEM((2 * kept * in_local, WIDTH_B), F32),
            pltpu.VMEM(blocks, BF16),
            pltpu.VMEM(blocks, BF16),
            pltpu.VMEM(lines, BF16),
            pltpu.VMEM(lines, BF16),
            pltpu.VMEM((groups * per, WIDTH_B // (2 * span) * (count // 2), WIDTH_B), F32),
            pltpu.SemaphoreType.DMA((len(inputs) - 1,)),
            pltpu.SemaphoreType.DMA((parts + 1,)),
            pltpu.SemaphoreType.DMA((chunks, peers)),
            pltpu.SemaphoreType.DMA((chunks, peers)),
            pltpu.SemaphoreType.DMA,
        ],
        compiler_params=pltpu.CompilerParams(
            collective_id=0, has_side_effects=True, vmem_limit_bytes=48 * 2**20
        ),
        name="correlator",
    )(*inputs)
    out = pl.pallas_call(
        functools.partial(turn_kernel, channels, pieces),
        out_shape=jax.ShapeDtypeStruct((count, count, channels), BF16),
        in_specs=[pl.BlockSpec(memory_space=pltpu.VMEM)],
        out_specs=pl.BlockSpec(memory_space=pl.ANY),
        scratch_shapes=[
            pltpu.VMEM((count, count, channels), BF16),
            pltpu.SemaphoreType.DMA((2, pieces)),
        ],
        compiler_params=pltpu.CompilerParams(vmem_limit_bytes=16 * 2**20),
        name="turn",
    )(vis)
    return out.transpose(2, 0, 1)


def solution(mesh):
    peers = mesh.shape["inputs"]

    def body(samples, filter_coefs):
        in_local = samples.shape[0]
        kept = WIDTH_B // 4
        nfft = filter_coefs.shape[1]
        nspec = samples.shape[1] // nfft - filter_coefs.shape[0] + 1
        fits = kept % peers == 0 and in_local <= 8 and 2 * peers * in_local == WIDTH_B
        fits = fits and nspec % 16 == 0 and nspec >= 64 and nfft % (32 * WIDTH_B) == 0
        if fits and (2 * in_local * (kept // peers)) % 16 == 0:
            return kernel_body(peers, kept, samples, filter_coefs)
        return plain_body(samples, filter_coefs)

    return jax.shard_map(
        body,
        mesh=mesh,
        in_specs=(P(("groups", "inputs"), None), P()),
        out_specs=P(("groups", "inputs"), None, None),
        check_vma=False,
    )
```

```python
import functools
import math

import jax
import jax.numpy as jnp
import numpy as np
from jax import lax
from jax.experimental import pallas as pl
from jax.experimental.pallas import tpu as pltpu
from jax.sharding import PartitionSpec as P


def phase_table(first, second, period):
    rows = lax.broadcasted_iota(jnp.int32, (first, second), 0)
    cols = lax.broadcasted_iota(jnp.int32, (first, second), 1)
    angle = 2.0 * math.pi / period * (rows * cols % period).astype(jnp.float32)
    return (jnp.cos(angle), -jnp.sin(angle))


def correlate_items(block):
    count = block.shape[0]
    nspec_local = block.shape[2] // 2
    rotated = jnp.concatenate([-block[..., nspec_local:], block[..., :nspec_local]], axis=-1)
    real_sum = jnp.einsum("ikt,jkt->kij", block, block, preferred_element_type=jnp.float32)
    imag_sum = jnp.einsum("ikt,jkt->kij", block, rotated, preferred_element_type=jnp.float32)
    rows = lax.broadcasted_iota(jnp.int32, (count, count), 0)
    cols = lax.broadcasted_iota(jnp.int32, (count, count), 1)
    return (jnp.where(rows >= cols, real_sum, imag_sum) / nspec_local).astype(jnp.bfloat16)


def correlate_turned(block):
    flat_block = block.reshape(block.shape[0], block.shape[2], block.shape[3])
    return correlate_items(flat_block)


def plain_body(samples, filter_coefs):
    in_local, total = samples.shape
    taps_count, nfft_local = filter_coefs.shape
    frame_count = total // nfft_local
    nspec_local = frame_count - taps_count + 1
    width_b = 128
    width_a = nfft_local // width_b
    kept_width = width_b // 4
    frames = samples.reshape(in_local, frame_count, nfft_local).astype(jnp.float32)
    filtered = filter_coefs[0] * frames[:, 0:nspec_local]
    for tap_index in range(1, taps_count):
        filtered = (
            filtered + filter_coefs[tap_index] * frames[:, tap_index : tap_index + nspec_local]
        )
    grid_view = filtered.astype(jnp.bfloat16).reshape(in_local, nspec_local, width_a, width_b)
    first_cos, first_sin = phase_table(width_a, width_a, width_a)
    first_table = jnp.concatenate([first_cos, first_sin], axis=1).astype(jnp.bfloat16)
    first_out = jnp.einsum(
        "itab,ak->itkb", grid_view, first_table, preferred_element_type=jnp.float32
    )
    real_one = first_out[:, :, :width_a]
    imag_one = first_out[:, :, width_a:]
    twist_cos, twist_sin = phase_table(width_a, width_b, nfft_local)
    real_two = real_one * twist_cos - imag_one * twist_sin
    imag_two = real_one * twist_sin + imag_one * twist_cos
    stacked = jnp.concatenate(
        [real_two.astype(jnp.bfloat16), imag_two.astype(jnp.bfloat16)], axis=3
    )
    second_cos, second_sin = phase_table(width_b, width_b, width_b)
    second_cos = second_cos[:, :kept_width]
    second_sin = second_sin[:, :kept_width]
    upper_rows = jnp.concatenate([second_cos, second_sin], axis=1)
    lower_rows = jnp.concatenate([-second_sin, second_cos], axis=1)
    second_table = jnp.concatenate([upper_rows, lower_rows], axis=0).astype(jnp.bfloat16)
    second_out = jnp.einsum(
        "itkn,nq->iqkt", stacked, second_table, preferred_element_type=jnp.float32
    )
    real_out = second_out[:, :kept_width]
    imag_out = second_out[:, kept_width:]
    channels = width_a * kept_width
    spectra = jnp.concatenate(
        [real_out.astype(jnp.bfloat16), imag_out.astype(jnp.bfloat16)], axis=3
    )
    spectra = spectra.reshape(in_local, channels, 2 * nspec_local)
    peers = lax.axis_size("inputs")
    per_peer = channels // peers
    owner_view = spectra.reshape(in_local, peers, per_peer, 2 * nspec_local)
    result = correlate_turned(
        lax.all_to_all(owner_view, "inputs", split_axis=1, concat_axis=0, tiled=True)
    )
    return result


WIDTH_B = 128
BF16 = jnp.bfloat16
F32 = jnp.float32
NT = (((1,), (1,)), ((), ()))


def np_phase(first, second, period):
    turns = np.outer(np.arange(first), np.arange(second)) % period
    angle = np.float32(2.0 * math.pi / period) * turns.astype(np.float32)
    return np.cos(angle), -np.sin(angle)


def make_tables(in_local, width_a, kept):
    nfft = width_a * WIDTH_B
    half = width_a // 2
    cos_a, sin_a = (t.T for t in np_phase(width_a, width_a, width_a))
    first = np.concatenate([cos_a[:half + 1], sin_a[1:half]], axis=0)
    first = np.kron(first, np.eye(in_local, dtype=np.float32))
    mirrored = [*range(half + 1), *range(width_a - 1, half, -1)]
    twist = np.concatenate(
        [np.repeat(t[mirrored], in_local, axis=0) for t in np_phase(width_a, WIDTH_B, nfft)],
        axis=0,
    )
    cos_b, sin_b = (t[:, :kept].T for t in np_phase(WIDTH_B, WIDTH_B, WIDTH_B))
    second = np.concatenate(
        [np.concatenate([cos_b, -sin_b], axis=1), np.concatenate([sin_b, cos_b], axis=1)], axis=0
    )
    return jnp.asarray(first, BF16), jnp.asarray(twist, F32), jnp.asarray(second, BF16)


def correlator_kernel(
    dims, x_any, coef_any, first_any, twist_any, second_any, order_any, vis_ref,
    x_ref, coef_in, first_ref, twist_ref, second_ref, order_ref, coef_ref,
    real_ref, imag_ref, turn_ref, send_ref, recv_ref, line_ref, quad_ref, sum_ref,
    load_sem, x_sem, send_sem, recv_sem, own_sem,
):
    peers, in_local, nspec, taps, kept, span, head, tail, pieces, pad = dims
    rows = first_ref.shape[1]
    width_a = rows // in_local
    parts = nspec // span
    shared = WIDTH_B // (2 * span)
    wide = shared * span
    groups = width_a // (2 * shared)
    slot = rows + pad
    ahead = 2
    me = lax.axis_index("inputs")

    def partner(n):
        return lax.rem(me + n + 1, peers)

    barrier = pltpu.get_barrier_semaphore()

    def greet(n, carry):
        pl.semaphore_signal(
            barrier, inc=1, device_id={"inputs": partner(n)},
            device_id_type=pl.DeviceIdType.MESH,
        )
        return carry


    def load_frames(start, count, n):
        at = pl.ds(start * rows, count * rows)
        return pltpu.make_async_copy(x_any.at[at], x_ref.at[at], x_sem.at[n])

    each = span // 2

    def load_part(g):
        return load_frames(g * each + taps - 1, each, g)

    small = [
        pltpu.make_async_copy(src, dst, load_sem.at[n])
        for n, (src, dst) in enumerate((
            (coef_any, coef_in), (first_any, first_ref), (twist_any, twist_ref),
            (second_any, second_ref), (order_any, order_ref),
        ))
    ]
    small[0].start()
    load_frames(0, taps - 1, 2 * parts).start()
    load_part(0).start()
    load_part(1).start()
    for copy in small[1:-1]:
        copy.start()
    lax.fori_loop(0, peers - 1, greet, 0, unroll=5)

    small[0].wait()
    for m in range(taps):
        tap = coef_in[pl.ds(m, width_a, stride=taps), :]
        for i in range(in_local):
            coef_ref[pl.ds(m * rows + i, width_a, stride=in_local), :] = tap
    for copy in small[1:-1]:
        copy.wait()
    load_frames(0, taps - 1, 2 * parts).wait()

    lane_block = 64
    low_rows = rows // 2
    edge = lax.broadcasted_iota(jnp.int32, (8, WIDTH_B), 0) < in_local

    def two_spectra(h, tp):
        late_t = tp * 2
        t = h * span + late_t
        filtered = []
        for r in range(0, rows, lane_block):
            frames = [
                x_ref[pl.ds(pl.multiple_of((t + m) * rows + r, lane_block), lane_block), :].astype(F32)
                for m in range(taps + 1)
            ]
            pair = []
            for late in range(2):
                acc = None
                for m in range(taps):
                    at = m * rows + r
                    term = coef_ref[at:at + lane_block, :] * frames[m + late]
                    acc = term if acc is None else acc + term
                pair.append(acc.astype(BF16))
            filtered.append(jnp.concatenate(pair, axis=1))
        filtered = jnp.concatenate(filtered, axis=0)
        out = jnp.dot(first_ref[...], filtered, preferred_element_type=F32)
        w_re, w_im = twist_ref[:low_rows, :], twist_ref[rows:rows + low_rows, :]
        v_re, v_im = twist_ref[low_rows:rows, :], twist_ref[rows + low_rows:, :]
        for late in range(2):
            cols = slice(late * WIDTH_B, (late + 1) * WIDTH_B)
            re, im = out[:low_rows, cols], out[low_rows:, cols]
            mirror = jnp.concatenate([jnp.where(edge, im[:8], re[:8]), re[8:]], axis=0)
            im = jnp.concatenate([jnp.where(edge, 0.0, im[:8]), im[8:]], axis=0)
            at = pl.ds(pl.multiple_of((late_t + late) * slot, 8), low_rows)
            real_ref[at, :] = re * w_re - im * w_im
            imag_ref[at, :] = re * w_im + im * w_re
            at = pl.ds(pl.multiple_of((late_t + late) * slot + low_rows, 8), low_rows)
            real_ref[at, :] = mirror * v_re + im * v_im
            imag_ref[at, :] = mirror * v_im - im * v_re

    per_dest = kept // peers * in_local

    def channel_group(h, kp):
        parts_out = []
        for kk in range(2):
            both = []
            for i in range(in_local):
                for u in range(shared):
                    k = (kp * 2 + kk) * shared + u
                    k = jnp.where(k <= width_a // 2, k, width_a // 2 * 3 - k)
                    at = pl.ds(k * in_local + i, span, stride=slot)
                    both.append(jnp.concatenate(
                        [real_ref[at, :].astype(BF16), imag_ref[at, :].astype(BF16)], axis=1
                    ))
            both = jnp.concatenate(both, axis=0)
            res = lax.dot_general(second_ref[...], both, NT, preferred_element_type=F32)
            for i in range(in_local):
                cols = slice(i * wide, (i + 1) * wide)
                turn_ref[pl.ds(kk * kept * in_local + i, kept, stride=in_local), :] = (
                    jnp.concatenate([res[:kept, cols], res[kept:, cols]], axis=1)
                )
            part = turn_ref[kk * kept * in_local:(kk + 1) * kept * in_local, :]
            parts_out.append(part.reshape(peers, per_dest, WIDTH_B))
        send_ref[:, h * groups + kp] = jnp.concatenate(parts_out, axis=1).astype(BF16)

    def remote(c, h, start, size, n):
        dest = partner(n)
        at = pl.ds(h * groups + start, size)
        return pltpu.make_async_remote_copy(
            src_ref=send_ref.at[dest, at], dst_ref=recv_ref.at[me, at],
            send_sem=send_sem.at[c, n], recv_sem=recv_sem.at[c, n],
            device_id={"inputs": dest}, device_id_type=pl.DeviceIdType.MESH,
        )

    def push(c, h, start, size):
        def one(n, u):
            remote(c, h, start, size, n).start()
            return u

        lax.fori_loop(0, peers - 1, one, 0, unroll=5)

    def arrive(c, h, start, size):
        def one(n, u):
            remote(c, h, start, size, n).wait()
            return u

        lax.fori_loop(0, peers - 1, one, 0, unroll=5)

    def forward(h, carry):
        def spectra(tp, u):
            two_spectra(h, tp)
            return u

        def stretch(n, u):
            load_part(2 * h + n).wait()

            @pl.when(h < parts - 1)
            def _():
                load_part(2 * h + 2 + n).start()

            return lax.fori_loop(0, each // 2, lambda tp, v: spectra(n * (each // 2) + tp, v), u, unroll=4)

        lax.fori_loop(0, 2, stretch, 0)

        def two_groups(n, u):
            channel_group(h, 2 * n)
            channel_group(h, 2 * n + 1)
            return u

        is_first = h == 0
        is_last = h == parts - 1
        cut = jnp.where(is_first, head // 2, 0)
        lax.fori_loop(0, cut, two_groups, 0)

        @pl.when(is_first)
        def _():
            pl.semaphore_wait(barrier, peers - 1)
            push(0, h, 0, head)

        lax.fori_loop(cut, groups // 2, two_groups, 0)

        @pl.when(is_first)
        def _():
            push(1, h, head, groups - head)

        @pl.when(is_last)
        def _():
            def piece(q, u):
                later = q // (groups // tail)
                j = q % (groups // tail)

                def one(n, v):
                    @pl.when((partner(n) >= ahead) == (later == 1))
                    def _():
                        remote(2 * parts - 2 + j, h, j * tail, tail, n).start()

                    return v

                return lax.fori_loop(0, peers - 1, one, u)

            lax.fori_loop(0, 2 * (groups // tail), piece, 0)

        @pl.when(jnp.logical_not(is_first | is_last))
        def _():
            push(2 * h + 1, h, 0, groups)

        return carry

    lax.fori_loop(0, parts, forward, 0)
    small[-1].start()
    small[-1].wait()
    own = pltpu.make_async_copy(send_ref.at[me], recv_ref.at[me], own_sem)
    own.start()
    own.wait()

    count = peers * in_local
    per = 2 * (kept // peers)
    halves = per // 2
    channels = width_a * halves
    low = count // 2
    i_at = lax.broadcasted_iota(jnp.int32, (low, WIDTH_B), 0)
    lane = lax.broadcasted_iota(jnp.int32, (low, WIDTH_B), 1)
    first_half = lane < count
    top_real = i_at >= lane
    low_real = i_at + low >= lane - count
    lane_row = lax.broadcasted_iota(jnp.int32, (count, WIDTH_B), 1)
    masks = [
        jnp.where((lane_row % wide) // span == u, 1.0, 0.0).astype(BF16) for u in range(shared)
    ]

    signs = jnp.where(
        lax.broadcasted_iota(jnp.int32, (per * count, WIDTH_B), 1) < wide, -1.0, 1.0
    )

    def swap(v):
        return pltpu.roll(v, wide, 1)

    def line_up(g):
        both = [recv_ref[:, g + n].reshape(per * count, WIDTH_B) for n in range(2)]
        lined = jnp.dot(
            order_ref[...], jnp.concatenate(both, axis=1), preferred_element_type=F32
        )
        for n in range(2):
            one = lined[:, n * WIDTH_B:(n + 1) * WIDTH_B]
            line_ref[g + n] = one.astype(BF16)
            quad_ref[g + n] = (swap(one) * signs).astype(BF16)

    def gram(kp, s, first, last):
        at = slice(s * count, (s + 1) * count)
        tiles = [line_ref[h * groups + kp, at, :] for h in range(first, last)]
        turned = [quad_ref[h * groups + kp, at, :] for h in range(first, last)]
        right = jnp.concatenate(
            [jnp.concatenate(tiles, axis=1), jnp.concatenate(turned, axis=1)], axis=0
        )
        left = jnp.concatenate(
            [jnp.concatenate([t * m for t in tiles], axis=1) for m in masks], axis=0
        )
        return lax.dot_general(left, right, NT, preferred_element_type=F32)

    def select(res, u):
        top = res[u * count:u * count + low]
        bottom = res[u * count + low:(u + 1) * count]
        return jnp.where(
            first_half,
            jnp.where(top_real, top, swap(top)),
            jnp.where(low_real, swap(bottom), bottom),
        )

    def correlate_early(kp, carry):
        for s in range(per):
            res = gram(kp, s, 0, parts - 2)
            for u in range(shared):
                sum_ref[kp * per + s, u * low:(u + 1) * low, :] = select(res, u)
        return carry

    def correlate(kp):
        for s in range(per):
            res = gram(kp, s, parts - 2, parts)
            for u in range(shared):
                vis = select(res, u) + sum_ref[kp * per + s, u * low:(u + 1) * low, :]
                c = (s % halves) * width_a + (kp * 2 + s // halves) * shared + u
                vis_ref[pl.ds(c, low, stride=channels), :] = vis * (1.0 / nspec)

    def lines(h):
        def one(n, u):
            line_up(h * groups + 2 * n)
            return u

        lax.fori_loop(0, groups // 2, one, 0)

    def middle(h, carry):
        arrive(2 * h + 1, h, 0, groups)
        lines(h)

        @pl.when(h == parts - 3)
        def _():
            lax.fori_loop(0, groups, correlate_early, 0, unroll=2)

        return carry

    def finish(n, u):
        line_up((parts - 1) * groups + 2 * n)
        correlate(2 * n)
        correlate(2 * n + 1)
        return u

    def last_part(j, u):
        arrive(2 * parts - 2 + j, parts - 1, j * tail, tail)
        for n in range(tail // 2):
            finish(j * (tail // 2) + n, 0)
        return u

    arrive(0, 0, 0, head)
    arrive(1, 0, head, groups - head)
    lines(0)
    lax.fori_loop(1, parts - 1, middle, 0)
    lax.fori_loop(0, groups // tail, last_part, 0)


def turn_kernel(channels, pieces, vis_ref, out_any, out_ref, out_sem):
    half = out_ref.shape[0] // 2
    width = out_ref.shape[1]
    each = half // pieces

    def put(p, upper):
        at = pl.ds(p * each + upper * half, each)
        return pltpu.make_async_copy(out_ref.at[at], out_any.at[at], out_sem.at[upper, p])

    for p in range(pieces):
        def one_row(n, carry):
            i = p * each + n
            block = vis_ref[pl.ds(pl.multiple_of(i * channels, channels), channels), :]
            block = block.T.astype(BF16)
            out_ref[i] = block[:width]
            out_ref[i + half] = block[width:]
            return carry

        lax.fori_loop(0, each, one_row, 0, unroll=8)
        put(p, 0).start()
        put(p, 1).start()
    for p in range(pieces):
        put(p, 0).wait()
        put(p, 1).wait()


def kernel_body(peers, kept, samples, filter_coefs):
    in_local, total = samples.shape
    taps, nfft = filter_coefs.shape
    width_a = nfft // WIDTH_B
    nspec = total // nfft - taps + 1
    rows = width_a * in_local
    span = 16
    pieces = 4
    pad = 8
    parts = nspec // span
    groups = width_a * span // WIDTH_B
    head = 2
    tail = 4
    chunks = 2 * parts - 2 + groups // tail
    per = 2 * (kept // peers)
    count = peers * in_local
    channels = width_a * per // 2
    x = samples.reshape(in_local, total // WIDTH_B, WIDTH_B).transpose(1, 0, 2)
    x = x.reshape(total // WIDTH_B * in_local, WIDTH_B)
    coefs = filter_coefs.reshape(taps, width_a, WIDTH_B).transpose(1, 0, 2)
    coefs = coefs.reshape(width_a * taps, WIDTH_B)
    first, twist, second = make_tables(in_local, width_a, kept)
    order = np.zeros((per, peers, in_local, peers, per, in_local), np.float32)
    for s in range(per):
        for p in range(peers):
            order[s, p, range(in_local), p, s, range(in_local)] = 1
    order = jnp.asarray(order.reshape(per * count, per * count), BF16)
    blocks = (peers, parts * groups, per * in_local, WIDTH_B)
    lines = (parts * groups, per * count, WIDTH_B)
    inputs = (x, coefs, first, twist, second, order)
    inputs = [pltpu.with_memory_space_constraint(a, pltpu.HBM) for a in inputs]
    vis = pl.pallas_call(
        functools.partial(
            correlator_kernel, (peers, in_local, nspec, taps, kept, span, head, tail, pieces, pad)
        ),
        out_shape=jax.ShapeDtypeStruct((count // 2 * channels, 2 * count), F32),
        in_specs=[pl.BlockSpec(memory_space=pl.ANY)] * len(inputs),
        out_specs=pl.BlockSpec(memory_space=pltpu.VMEM),
        scratch_shapes=[pltpu.VMEM(a.shape, a.dtype) for a in inputs] + [
            pltpu.VMEM((taps * rows, WIDTH_B), F32),
            pltpu.VMEM((span * (rows + pad), WIDTH_B), F32),
            pltpu.VMEM((span * (rows + pad), WIDTH_B), F32),
            pltpu.VMEM((2 * kept * in_local, WIDTH_B), F32),
            pltpu.VMEM(blocks, BF16),
            pltpu.VMEM(blocks, BF16),
            pltpu.VMEM(lines, BF16),
            pltpu.VMEM(lines, BF16),
            pltpu.VMEM((groups * per, WIDTH_B // (2 * span) * (count // 2), WIDTH_B), F32),
            pltpu.SemaphoreType.DMA((len(inputs) - 1,)),
            pltpu.SemaphoreType.DMA((2 * parts + 1,)),
            pltpu.SemaphoreType.DMA((chunks, peers)),
            pltpu.SemaphoreType.DMA((chunks, peers)),
            pltpu.SemaphoreType.DMA,
        ],
        compiler_params=pltpu.CompilerParams(
            collective_id=0, has_side_effects=True, vmem_limit_bytes=48 * 2**20
        ),
        name="correlator",
    )(*inputs)
    out = pl.pallas_call(
        functools.partial(turn_kernel, channels, pieces),
        out_shape=jax.ShapeDtypeStruct((count, count, channels), BF16),
        in_specs=[pl.BlockSpec(memory_space=pltpu.VMEM)],
        out_specs=pl.BlockSpec(memory_space=pl.ANY),
        scratch_shapes=[
            pltpu.VMEM((count, count, channels), BF16),
            pltpu.SemaphoreType.DMA((2, pieces)),
        ],
        compiler_params=pltpu.CompilerParams(vmem_limit_bytes=16 * 2**20),
        name="turn",
    )(vis)
    return out.transpose(2, 0, 1)


def solution(mesh):
    peers = mesh.shape["inputs"]

    def body(samples, filter_coefs):
        in_local = samples.shape[0]
        kept = WIDTH_B // 4
        nfft = filter_coefs.shape[1]
        nspec = samples.shape[1] // nfft - filter_coefs.shape[0] + 1
        fits = kept % peers == 0 and in_local <= 8 and 2 * peers * in_local == WIDTH_B
        fits = fits and nspec % 16 == 0 and nspec >= 64 and nfft % (32 * WIDTH_B) == 0
        if fits and (2 * in_local * (kept // peers)) % 16 == 0:
            return kernel_body(peers, kept, samples, filter_coefs)
        return plain_body(samples, filter_coefs)

    return jax.shard_map(
        body,
        mesh=mesh,
        in_specs=(P(("groups", "inputs"), None), P()),
        out_specs=P(("groups", "inputs"), None, None),
        check_vma=False,
    )
```
